128 devices in a mesh: tm: 16 (over z, y_hi, core), space: 8 (over x, y_lo).
Axes of the slice: x: 4, y: 4 (y_hi: 2, y_lo: 2; y = y_hi * 2 + y_lo), z: 4, core: 2. Of those that a mesh axis runs over, the one named last changes fastest.
Arguments:
- rhs: float32 [32, 384, 2048], P('tm', None, 'space'), may hold values from -6 to 6
- material: float32 [2048], P('space'), may hold values from 1 to 4
- modal_rates: float32 [384], replicated, may hold values from 0.25 to 8
- modes_in: float32 [384, 384], replicated, may hold values from -0.3125 to 0.3125
- modes_out: float32 [384, 384], replicated, may hold values from -0.3125 to 0.3125
- face_lift: float32 [6, 384, 96], replicated, may hold values from -0.109375 to 0.109375
- neighbours: int32 [6, 2048], P(None, 'space'), may hold values from 0 to 383, as said below
- halo_send: int32 [2, 1024], P(None, 'space'), may hold values from 0 to 255, as said below
Outputs:
- solution: float32 [32, 384, 2048], P('tm', None, 'space')
The draws below stay inside these ranges and needn't reach their ends.
Inputs may be any that keep to these rules, and one draw needn't show every extreme that they name: neighbours[f, e] names the element across face f of element e (faces at -x, +x, -y, +y, -z, +z) by its position in e's block of 256; each block is a slab of 2 x 8 x 16 elements, periodic in y and z, numbered in an order of its own. A value 256 + t occurs in rows 0 and 1 only and names the t-th element sent from the block below (row 0) or above (row 1). `halo_send`: in each block of 128 entries, row 0 lists the positions of the slab's elements on its -x side and row 1 those on its +x side, in the order in which the neighbouring slabs' neighbours refer to them; together they name every element of the slab once.
All inputs are finite; a program needn't handle non-finite values.
Results may differ from the reference program's by a relative error of at most 0.00026.
Values sent between devices are 32-bit elements; how exact they have to be, the bound alone decides.
No kernel may reach another device: no remote copies, remote signals or barrier semaphores. Data moves between devices by JAX's collectives and lax.ppermute only.
A program may use at most 64 MiB of HBM per device.

```python
import math
import jax
import jax.numpy as jnp
from jax import lax

FIELDS = 6
NP = 4
NB = 384
NFT = 96
EX = 2
EY = 8
EZ = 16
SWEEPS = 2
HALO = 128
ELEM_DEV = 256
ELEMS = 2048
STEPS = 32
N_SPACE = 8


def slab_orders(key):
    device_keys = jax.random.split(key, N_SPACE)
    permuted = jax.vmap(lambda sub_key: jax.random.permutation(sub_key, ELEM_DEV))(device_keys)
    return permuted.astype(jnp.int32)


def draw_neighbours(key, part):
    orders = slab_orders(key)
    grid_cells = jnp.argsort(orders, axis=1).astype(jnp.int32)
    layer_size = EY * EZ
    coord_x = grid_cells // layer_size
    in_layer = grid_cells % layer_size
    coord_y = in_layer // EZ
    coord_z = in_layer % EZ

    def located(target):
        return jnp.take_along_axis(orders, target.astype(jnp.int32), axis=1)
    lower_side = jnp.where(coord_x == 0, ELEM_DEV + in_layer, located(jnp.maximum(grid_cells - layer_size, 0)))
    upper_side = jnp.where(coord_x == EX - 1, ELEM_DEV + in_layer, located(jnp.minimum(grid_cells + layer_size, ELEM_DEV - 1)))
    column_base = coord_x * layer_size + coord_z
    south_side = located(column_base + (coord_y + EY - 1) % EY * EZ)
    north_side = located(column_base + (coord_y + 1) % EY * EZ)
    row_base = coord_x * layer_size + coord_y * EZ
    below_side = located(row_base + (coord_z + EZ - 1) % EZ)
    above_side = located(row_base + (coord_z + 1) % EZ)
    neighbour_table = jnp.stack([lower_side, upper_side, south_side, north_side, below_side, above_side])
    return neighbour_table.reshape(6, N_SPACE * ELEM_DEV).astype(jnp.int32)


def draw_halo_send(key, part):
    orders = slab_orders(key)
    layer_size = EY * EZ
    first_side = orders[:, :layer_size]
    last_side = orders[:, (EX - 1) * layer_size:EX * layer_size]
    return jnp.stack([first_side.reshape(-1), last_side.reshape(-1)]).astype(jnp.int32)


def steps_of(rng, shape, cuts, smallest, high):
    gain = 1.0
    for axis_at, blocks in cuts:
        draws = jax.random.uniform(jax.random.fold_in(jax.random.fold_in(rng, 6), axis_at), (blocks,), jnp.float32, smallest / len(cuts), high / len(cuts))
        gain = gain * jnp.repeat(jnp.exp(draws), shape[axis_at] // blocks).reshape((-1,) + (1,) * (len(shape) - 1 - axis_at))
    return gain


def bell_draw(rng, shape, spread, bound, cuts=(), kind=jnp.bfloat16):
    values = jax.random.normal(rng, shape, jnp.float32) * spread
    if len(cuts) > 0:
        values = steps_of(rng, shape, cuts, -0.22, 0.18) * values
    return jnp.clip(values, min=-bound, max=bound).astype(kind)


def setup_inputs(seed: int = 0) -> dict:
    splits = jax.random.split(jax.random.key(seed), 9)
    return {
        "rhs": bell_draw(splits[0], (STEPS, NB, ELEMS), 1.0, 6.0, ((0, 16), (2, 8)), jnp.float32),
        "material": jnp.clip(jnp.exp(math.log(4.0) - 1.3862944 * jax.random.uniform(splits[1], (ELEMS,), jnp.float32) ** steps_of(splits[1], (ELEMS,), ((0, 8),), -0.2, 0.2)), 1.0, 4.0),
        "modal_rates": jnp.clip(jnp.exp(jax.random.uniform(splits[2], (NB,), jnp.float32, math.log(0.25), math.log(8.0))), 0.25, 8.0),
        "modes_in": bell_draw(splits[3], (NB, NB), NB ** -0.5, 0.3125, (), jnp.float32),
        "modes_out": bell_draw(splits[4], (NB, NB), NB ** -0.5, 0.3125, (), jnp.float32),
        "face_lift": bell_draw(splits[5], (6, NB, NFT), (36 * NFT) ** -0.5, 0.109375, (), jnp.float32),
        "neighbours": draw_neighbours(jax.random.fold_in(splits[8], 71), 0),
        "halo_send": draw_halo_send(jax.random.fold_in(splits[8], 71), 0),
    }


OPPOSITE = (1, 0, 3, 2, 5, 4)


def face_trace(unknowns, which_face):
    leading = unknowns.shape[:-2]
    shaped = unknowns.reshape(leading + (FIELDS, NP, NP, NP, unknowns.shape[-1]))
    node_axis = len(leading) + 1 + which_face // 2
    node_place = 0 if which_face % 2 == 0 else NP - 1
    face_piece = lax.index_in_dim(shaped, node_place, node_axis, keepdims=False)
    return face_piece.reshape(leading + (FIELDS * NP * NP, unknowns.shape[-1]))


def global_sources(neighbours, halo_send):
    elements = neighbours.shape[1]
    block_index = jnp.arange(elements, dtype=jnp.int32) // ELEM_DEV
    source_rows = []
    for which_face in range(6):
        entry_index = neighbours[which_face].astype(jnp.int32)
        inside = block_index * ELEM_DEV + jnp.minimum(entry_index, ELEM_DEV - 1)
        if which_face < 2:
            other_block = block_index - 1 if which_face == 0 else block_index + 1
            sent_row = 1 if which_face == 0 else 0
            has_block = (other_block >= 0) & (other_block < N_SPACE)
            safe_block = jnp.clip(other_block, 0, N_SPACE - 1)
            halo_slot = jnp.maximum(entry_index - ELEM_DEV, 0)
            sent_index = halo_send[sent_row, safe_block * HALO + halo_slot].astype(jnp.int32)
            remote = jnp.where(has_block, safe_block * ELEM_DEV + sent_index, elements)
            inside = jnp.where(entry_index < ELEM_DEV, inside, remote)
        source_rows.append(inside.astype(jnp.int32))
    return jnp.stack(source_rows)


def element_solve(given_rhs, shift_real, shift_imag, material, modal_rates, modes_in, modes_out):
    projected = jnp.einsum("mn,cne->cme", modes_in, given_rhs, precision=lax.Precision.HIGHEST)
    denom_real = shift_real * material[None, :] + modal_rates[:, None]
    denom_imag = shift_imag * material[None, :] + jnp.zeros_like(modal_rates)[:, None]
    magnitude = denom_real * denom_real + denom_imag * denom_imag
    upper_real = (projected[0] * denom_real + projected[1] * denom_imag) / magnitude
    upper_imag = (projected[1] * denom_real - projected[0] * denom_imag) / magnitude
    divided = jnp.stack([upper_real, upper_imag])
    return jnp.einsum("mn,cne->cme", modes_out, divided, precision=lax.Precision.HIGHEST)


def face_coupling(unknowns, sources, face_lift):
    zero_column = jnp.zeros(unknowns.shape[:-2] + (FIELDS * NP * NP, 1), unknowns.dtype)
    gathered = []
    for which_face in range(6):
        padded = jnp.concatenate([face_trace(unknowns, OPPOSITE[which_face]), zero_column], axis=-1)
        gathered.append(jnp.take(padded, sources[which_face], axis=-1))
    return jnp.einsum("fmt,fcte->cme", face_lift, jnp.stack(gathered), precision=lax.Precision.HIGHEST)


def reference(rhs, material, modal_rates, modes_in, modes_out, face_lift, neighbours, halo_send):
    total_steps = rhs.shape[0]
    decay_ratio = 0.1 ** (1.0 / total_steps)
    step_count = jnp.arange(total_steps).astype(jnp.float32)
    weights = decay_ratio ** step_count
    spectrum = jnp.fft.fft(rhs * weights[:, None, None], axis=0)
    angles = (2.0 * jnp.pi / total_steps) * step_count
    lam_real = 1.0 - decay_ratio * jnp.cos(angles)
    lam_imag = decay_ratio * jnp.sin(angles)
    sources = global_sources(neighbours, halo_send)

    def solve_frequency(inputs):
        spec_real, spec_imag, shift_real, shift_imag = inputs
        given_rhs = jnp.stack([spec_real, spec_imag])
        current = element_solve(given_rhs, shift_real, shift_imag, material, modal_rates, modes_in, modes_out)
        for sweep_number in range(SWEEPS):
            corrected = given_rhs - face_coupling(current, sources, face_lift)
            current = element_solve(corrected, shift_real, shift_imag, material, modal_rates, modes_in, modes_out)
        return current

    spec_parts = (jnp.real(spectrum).astype(jnp.float32), jnp.imag(spectrum).astype(jnp.float32), lam_real, lam_imag)
    solved = lax.map(solve_frequency, spec_parts)
    signal = jnp.real(jnp.fft.ifft(solved[:, 0] + 1j * solved[:, 1], axis=0))
    return (signal / weights[:, None, None]).astype(jnp.float32)
```

```python
import math

import jax
import jax.numpy as jnp
import ml_dtypes
import numpy as np
from jax import lax
from jax.experimental import pallas as pl
from jax.experimental.pallas import tpu as pltpu
from jax.sharding import PartitionSpec as P

NB = 384
NFT = 96
LANES = 128
STEPS = 32
SLAB = 256
SHEET = 16
ROWS = STEPS * SHEET
HALF = ROWS // 2
SLABS = 8
DECAY = 0.1 ** (1.0 / STEPS)

RING = (0, 1, 4, 5, 8, 9, 12, 13, 14, 15, 10, 11, 6, 7, 2, 3)
SHEET_OF = tuple(RING.index(device) for device in range(16))
SAME_CHIP = [(i, i ^ 1) for i in range(16)]
NEXT_CHIP = [(RING[2 * i + 1], RING[(2 * i + 2) % 16]) for i in range(8)]
NEXT_CHIP = NEXT_CHIP + [(b, a) for a, b in NEXT_CHIP]
EVEN_SIDES = [(i, i ^ 1) for i in range(8)]
ODD_SIDES = [(1, 2), (2, 1), (3, 4), (4, 3), (5, 6), (6, 5)]

F32 = jnp.float32
BF16 = jnp.bfloat16
NN = (((1,), (0,)), ((), ()))
NT = (((1,), (1,)), ((), ()))
TN = (((0,), (0,)), ((), ()))


def halves(table):
    high = table.astype(np.float32).astype(ml_dtypes.bfloat16)
    low = (table - high.astype(np.float64)).astype(np.float32).astype(ml_dtypes.bfloat16)
    return high, low


def transform_tables():
    steps = np.arange(STEPS, dtype=np.float64)
    freqs = np.arange(STEPS // 2, dtype=np.float64)
    angles = 2.0 * np.pi / STEPS * np.outer(freqs, steps)
    real, imag = np.cos(angles), -np.sin(angles)
    imag[0] = np.cos(np.pi * steps)
    forward = np.concatenate([real, imag]) * DECAY**steps
    real_back, imag_back = 2.0 * np.cos(angles), -2.0 * np.sin(angles)
    real_back[0] = 1.0
    imag_back[0] = np.cos(np.pi * steps)
    inverse = np.concatenate([real_back, imag_back]).T / STEPS * (DECAY**-steps)[:, None]
    eye = np.eye(SHEET)
    return halves(np.kron(forward, eye)), halves(np.kron(inverse, eye))


def trace_rows():
    pick = np.zeros((6 * LANES, NB), np.float32)
    for face in range(6):
        for lane in range(NFT):
            field, first, second = lane // 16, lane // 4 % 4, lane % 4
            place = [first, second]
            place.insert(face // 2, 0 if face % 2 == 0 else 3)
            pick[face * LANES + lane, field * 64 + place[0] * 16 + place[1] * 4 + place[2]] = 1.0
    return pick.astype(ml_dtypes.bfloat16)


def split(values):
    high = values.astype(BF16)
    low = (values - high.astype(F32)).astype(BF16)
    return high, low


def dot(a, b, dims):
    return lax.dot_general(a, b, dims, preferred_element_type=F32)


def dot3(a, b, dims):
    return dot(a[0], b[0], dims) + (dot(a[0], b[1], dims) + dot(a[1], b[0], dims))


def arrange_kernel(place, chain, nbr, material, rhs, sent, order, sheet_material):
    mine = place[1]

    def upper(slab, element):
        return chain[slab * 8 + lax.shift_right_logical(element, 7), element & 127] & 511

    element = chain[2, 0] & 255
    origin = element
    for slab in range(SLABS - 1):
        label = upper(slab, upper(slab, element) & 255) & 127
        element = chain[(slab + 1) * 8 + 2, label] & 255
        origin = jnp.where(mine == slab + 1, element, origin)

    def across(face, at):
        return nbr[face, at] & 255

    column = [origin]
    for _ in range(15):
        column.append(across(5, column[-1]))
    rows = [column]
    for _ in range(7):
        rows.append([across(3, at) for at in rows[-1]])
    layers = [rows, [[across(1, at) for at in row] for row in rows]]

    sub = lax.broadcasted_iota(jnp.int32, (8, LANES), 0)
    lane = lax.broadcasted_iota(jnp.int32, (8, LANES), 1)
    for device in range(16):
        sheet = SHEET_OF[device]
        low, high = [], []
        for layer in range(2):
            at = jnp.zeros((8, LANES), jnp.int32)
            for row in range(8):
                at = jnp.where(sub == row, layers[layer][row][sheet], at)
            low.append(jnp.where(lane == at, 1.0, 0.0).astype(F32))
            high.append(jnp.where(lane + LANES == at, 1.0, 0.0).astype(F32))
        order[device * 16 : device * 16 + 16, :LANES] = jnp.concatenate(low).astype(BF16)
        order[device * 16 : device * 16 + 16, LANES:] = jnp.concatenate(high).astype(BF16)

    own = order[pl.ds(pl.multiple_of(place[0] * 16, 16), 16), :].astype(F32)
    column_sum = jnp.sum(own * material[...], axis=1, keepdims=True)
    sheet_material[...] = jnp.broadcast_to(column_sum, (16, LANES))
    picks = order[...]
    for step in range(2):
        high, low = split(rhs[step])
        placed = dot(picks, high, NT) + dot(picks, low, NT)
        sent[:, step * 16 : step * 16 + 16, :] = placed.reshape(16, 16, NB)


def prepare_kernel(
    modes_in, modes_out, face_lift, rates, sheet_material, pick,
    in_h, in_l, out_h, out_l, trace_h, trace_l, lift_h, lift_l, same_r, same_i, cross, lift,
):
    in_parts = split(modes_in[...])
    in_h[...], in_l[...] = in_parts
    out_parts = split(modes_out[...])
    out_h[...], out_l[...] = out_parts
    trace_h[...] = dot(pick[...], out_parts[0], NN).astype(BF16)
    trace_l[...] = dot(pick[...], out_parts[1], NN).astype(BF16)
    lift[...] = jnp.zeros_like(lift)
    for face in range(6):
        lift[:, face * LANES : face * LANES + NFT] = face_lift[face]
    lifted = split(dot3(in_parts, split(lift[...]), NN))
    lift_h[...], lift_l[...] = lifted
    for freq in range(16):
        angle = 2.0 * math.pi / STEPS * freq
        rows = slice(freq * 16, freq * 16 + 16)
        own = sheet_material[:, :1]
        real = (1.0 - DECAY * math.cos(angle)) * own + rates[...]
        imag = jnp.broadcast_to((DECAY * math.sin(angle) if freq else 0.0) * own, (16, NB))
        size = real * real + imag * imag
        same = real / size
        same_r[rows, :] = same
        same_i[rows, :] = same if freq else 1.0 / ((1.0 + DECAY) * own + rates[...])
        cross[rows, :] = imag / size


def divided(modal, same_r, same_i, cross):
    real, imag = modal[:HALF], modal[HALF:]
    mixed = cross[...]
    return jnp.concatenate(
        [real * same_r[...] + imag * mixed, imag * same_i[...] - real * mixed]
    )


def send_traces(place, traces, inner, to_chip, to_next, to_even, to_odd):
    core_low = place[0] & 1 == 0
    slab_even = place[1] & 1 == 0
    inner[...] = traces[:, : 4 * LANES]
    below, above = traces[:, 4 * LANES : 5 * LANES], traces[:, 5 * LANES :]
    to_chip[...] = jnp.where(core_low, above, below)
    to_next[...] = jnp.where(core_low, below, above)
    sides = traces[:, : 2 * LANES].reshape(STEPS, 2, 8, 2 * LANES)
    lower = sides[:, 0, :, :LANES].reshape(HALF, LANES)
    upper = sides[:, 1, :, LANES:].reshape(HALF, LANES)
    to_even[...] = jnp.where(slab_even, upper, lower)
    to_odd[...] = jnp.where(slab_even, lower, upper)


def first_kernel(
    place, steps, forward_h, forward_l, in_h, in_l, trace_h, trace_l, same_r, same_i, cross,
    modal, inner, to_chip, to_next, to_even, to_odd,
):
    spectrum = dot3((forward_h[...], forward_l[...]), split(steps[...]), NN)
    start = dot3(split(spectrum), (in_h[...], in_l[...]), NT)
    modal[...] = start
    solved = split(divided(start, same_r, same_i, cross))
    traces = dot3(solved, (trace_h[...], trace_l[...]), NT)
    send_traces(place, traces, inner, to_chip, to_next, to_even, to_odd)


def gathered(place, inner, from_chip, from_next, from_even, from_odd):
    core_low = place[0] & 1 == 0
    slab_even = place[1] & 1 == 0

    def face(which):
        return inner[:, which * LANES : which * LANES + LANES]

    below = jnp.where(slab_even, from_odd[...], from_even[...]).reshape(STEPS, 1, 8, LANES)
    above = jnp.where(slab_even, from_even[...], from_odd[...]).reshape(STEPS, 1, 8, LANES)
    first = face(0).reshape(STEPS, 2, 8, LANES)
    second = face(1).reshape(STEPS, 2, 8, LANES)
    minus_x = jnp.concatenate([below, second[:, :1]], axis=1).reshape(ROWS, LANES)
    plus_x = jnp.concatenate([first[:, 1:], above], axis=1).reshape(ROWS, LANES)
    minus_y = pltpu.roll(face(3).reshape(ROWS // 8, 8, LANES), 1, 1).reshape(ROWS, LANES)
    plus_y = pltpu.roll(face(2).reshape(ROWS // 8, 8, LANES), 7, 1).reshape(ROWS, LANES)
    minus_z = jnp.where(core_low, from_next[...], from_chip[...])
    plus_z = jnp.where(core_low, from_chip[...], from_next[...])
    return jnp.concatenate([minus_x, plus_x, minus_y, plus_y, minus_z, plus_z], axis=1)


def sweep_kernel(
    place, modal, inner, from_chip, from_next, from_even, from_odd,
    lift_h, lift_l, trace_h, trace_l, same_r, same_i, cross,
    inner_out, to_chip, to_next, to_even, to_odd,
):
    faces = split(gathered(place, inner, from_chip, from_next, from_even, from_odd))
    corrected = modal[...] - dot3(faces, (lift_h[...], lift_l[...]), NT)
    solved = split(divided(corrected, same_r, same_i, cross))
    traces = dot3(solved, (trace_h[...], trace_l[...]), NT)
    send_traces(place, traces, inner_out, to_chip, to_next, to_even, to_odd)


def last_kernel(
    place, modal, inner, from_chip, from_next, from_even, from_odd,
    lift_h, lift_l, out_h, out_l, same_r, same_i, cross, inverse_h, inverse_l,
    steps,
):
    faces = split(gathered(place, inner, from_chip, from_next, from_even, from_odd))
    corrected = modal[...] - dot3(faces, (lift_h[...], lift_l[...]), NT)
    solved = split(divided(corrected, same_r, same_i, cross))
    nodal = split(dot3(solved, (out_h[...], out_l[...]), NT))
    steps[...] = dot3((inverse_h[...], inverse_l[...]), nodal, NN)


def restore_kernel(arrived, order, out):
    for step in range(2):
        values = arrived[:, step * 16 : step * 16 + 16, :].reshape(SLAB, NB)
        high, low = split(values)
        picks = order[...]
        out[step] = dot(high, picks, TN) + dot(low, picks, TN)


SMEM = pl.BlockSpec(memory_space=pltpu.SMEM)
VMEM = pl.BlockSpec(memory_space=pltpu.VMEM)


def call(body, outs, scalars, arrays, flops, scratch=()):
    shapes = [jax.ShapeDtypeStruct(shape, kind) for shape, kind in outs]
    moved = sum(math.prod(s) * jnp.dtype(k).itemsize for s, k in outs)
    moved += sum(a.size * a.dtype.itemsize for a in arrays)
    return pl.pallas_call(
        body,
        out_shape=shapes,
        in_specs=[SMEM] * len(scalars) + [VMEM] * len(arrays),
        out_specs=[VMEM] * len(shapes),
        scratch_shapes=list(scratch),
        compiler_params=pltpu.CompilerParams(vmem_limit_bytes=40 * 2**20),
        cost_estimate=pl.CostEstimate(flops=flops, bytes_accessed=moved, transcendentals=0),
    )(*scalars, *arrays)


def shards(rhs, material, modal_rates, modes_in, modes_out, face_lift, neighbours, halo_send):
    (forward_h, forward_l), (inverse_h, inverse_l) = transform_tables()
    pick = trace_rows()
    place = jnp.stack([lax.axis_index("tm"), lax.axis_index("space")]).astype(jnp.int32)

    table = jnp.concatenate(
        [neighbours[1].reshape(2, LANES), halo_send, jnp.zeros((4, LANES), jnp.int32)]
    )
    chain = lax.all_to_all(
        jnp.broadcast_to(table, (SLABS, 8, LANES)), "space", 0, 0, tiled=True
    ).reshape(SLABS * 8, LANES)

    sent, order, sheet_material = call(
        arrange_kernel,
        [((16, 32, NB), F32), ((SLAB, SLAB), BF16), ((16, LANES), F32)],
        [place, chain, neighbours],
        [material.reshape(1, SLAB), rhs],
        2 * 4 * 256 * 256 * 384,
    )
    arrived = lax.all_to_all(sent, "tm", 0, 0, tiled=True).reshape(ROWS, NB)
    square = [((NB, NB), BF16)] * 4
    in_h, in_l, out_h, out_l, trace_h, trace_l, lift_h, lift_l, same_r, same_i, cross = call(
        prepare_kernel,
        square + [((6 * LANES, NB), BF16)] * 2 + [((NB, 6 * LANES), BF16)] * 2 + [((HALF, NB), F32)] * 3,
        [],
        [modes_in, modes_out, face_lift, modal_rates.reshape(1, NB), sheet_material, jnp.asarray(pick)],
        2 * 5 * 384 * 384 * 768,
        [pltpu.VMEM((NB, 6 * LANES), F32)],
    )

    halo = [((ROWS, 4 * LANES), F32)] + [((ROWS, LANES), F32)] * 2 + [((HALF, LANES), F32)] * 2

    def exchange(to_chip, to_next, to_even, to_odd):
        return [
            lax.ppermute(to_chip, "tm", SAME_CHIP),
            lax.ppermute(to_next, "tm", NEXT_CHIP),
            lax.ppermute(to_even, "space", EVEN_SIDES),
            lax.ppermute(to_odd, "space", ODD_SIDES),
        ]

    coefficients = [same_r, same_i, cross]
    modal, inner, *outgoing = call(
        first_kernel,
        [((ROWS, NB), F32)] + halo,
        [place],
        [arrived, jnp.asarray(forward_h), jnp.asarray(forward_l), in_h, in_l, trace_h, trace_l] + coefficients,
        2 * 3 * 512 * 384 * (512 + 384 + 768),
    )
    incoming = exchange(*outgoing)
    inner, *outgoing = call(
        sweep_kernel,
        halo,
        [place],
        [modal, inner, *incoming, lift_h, lift_l, trace_h, trace_l] + coefficients,
        2 * 3 * 512 * 384 * (768 + 768),
    )
    incoming = exchange(*outgoing)
    (steps,) = call(
        last_kernel,
        [((ROWS, NB), F32)],
        [place],
        [modal, inner, *incoming, lift_h, lift_l, out_h, out_l]
        + coefficients
        + [jnp.asarray(inverse_h), jnp.asarray(inverse_l)],
        2 * 3 * 512 * 384 * (768 + 512 + 384),
    )
    back = lax.all_to_all(steps.reshape(16, 32, NB), "tm", 0, 0, tiled=True)
    (out,) = call(
        restore_kernel, [((2, NB, SLAB), F32)], [], [back, order], 2 * 4 * 256 * 256 * 384
    )
    return out


def solution(mesh):
    return jax.shard_map(
        shards,
        mesh=mesh,
        in_specs=(
            P("tm", None, "space"),
            P("space"),
            P(),
            P(),
            P(),
            P(),
            P(None, "space"),
            P(None, "space"),
        ),
        out_specs=P("tm", None, "space"),
        check_vma=False,
    )
```

```python
import math

import jax
import jax.numpy as jnp
import ml_dtypes
import numpy as np
from jax import lax
from jax.experimental import pallas as pl
from jax.experimental.pallas import tpu as pltpu
from jax.sharding import PartitionSpec as P

NB = 384
NFT = 96
LANES = 128
STEPS = 32
SLAB = 256
SHEET = 16
ROWS = STEPS * SHEET
HALF = ROWS // 2
SLABS = 8
DECAY = 0.1 ** (1.0 / STEPS)

RING = (0, 1, 4, 5, 8, 9, 12, 13, 14, 15, 10, 11, 6, 7, 2, 3)
SHEET_OF = tuple(RING.index(device) for device in range(16))
SAME_CHIP = [(i, i ^ 1) for i in range(16)]
NEXT_CHIP = [(RING[2 * i + 1], RING[(2 * i + 2) % 16]) for i in range(8)]
NEXT_CHIP = NEXT_CHIP + [(b, a) for a, b in NEXT_CHIP]
EVEN_SIDES = [(i, i ^ 1) for i in range(8)]
ODD_SIDES = [(1, 2), (2, 1), (3, 4), (4, 3), (5, 6), (6, 5)]

F32 = jnp.float32
BF16 = jnp.bfloat16
NN = (((1,), (0,)), ((), ()))
NT = (((1,), (1,)), ((), ()))
TN = (((0,), (0,)), ((), ()))


def real_fft(steps):
    count = len(steps)
    if count == 2:
        return [(steps[0] + steps[1], None), (steps[0] - steps[1], None)]
    even, odd = real_fft(steps[0::2]), real_fft(steps[1::2])
    out = [None] * (count // 2 + 1)
    out[0] = (even[0][0] + odd[0][0], None)
    out[count // 2] = (even[0][0] - odd[0][0], None)
    out[count // 4] = (even[count // 4][0], -odd[count // 4][0])
    for freq in range(1, count // 4):
        cos, sin = math.cos(2.0 * math.pi * freq / count), math.sin(2.0 * math.pi * freq / count)
        real, imag = odd[freq]
        turned_real, turned_imag = real * cos + imag * sin, imag * cos - real * sin
        real, imag = even[freq]
        out[freq] = (real + turned_real, imag + turned_imag)
        out[count // 2 - freq] = (real - turned_real, turned_imag - imag)
    return out


def real_ifft(freqs):
    count = 2 * (len(freqs) - 1)
    first, last = freqs[0][0], freqs[-1][0]
    if count == 2:
        return [first + last, first - last]
    even, odd = [None] * (count // 4 + 1), [None] * (count // 4 + 1)
    even[0], odd[0] = (first + last, None), (first - last, None)
    middle = freqs[count // 4]
    even[-1], odd[-1] = (2.0 * middle[0], None), (-2.0 * middle[1], None)
    for freq in range(1, count // 4):
        cos, sin = math.cos(2.0 * math.pi * freq / count), math.sin(2.0 * math.pi * freq / count)
        (real, imag), (other_real, other_imag) = freqs[freq], freqs[count // 2 - freq]
        even[freq] = (real + other_real, imag - other_imag)
        real, imag = real - other_real, imag + other_imag
        odd[freq] = (real * cos - imag * sin, imag * cos + real * sin)
    out = [None] * count
    out[0::2], out[1::2] = real_ifft(even), real_ifft(odd)
    return out


def tiles():
    for block in range(SHEET // 8):
        for lane in range(0, NB, LANES):
            yield lambda row: (slice(row * SHEET + block * 8, row * SHEET + block * 8 + 8), slice(lane, lane + LANES))


def to_frequencies(steps, spectrum):
    for at in tiles():
        freqs = real_fft([steps[at(n)] * DECAY**n for n in range(STEPS)])
        for freq in range(16):
            spectrum[at(freq)] = freqs[freq][0]
            spectrum[at(16 + freq)] = freqs[freq][1] if freq else freqs[16][0]


def to_steps(spectrum, steps):
    for at in tiles():
        pairs = [(spectrum[at(freq)], spectrum[at(16 + freq)]) for freq in range(16)]
        freqs = [(pairs[0][0], None)] + pairs[1:] + [(pairs[0][1], None)]
        for n, value in enumerate(real_ifft(freqs)):
            steps[at(n)] = value * (DECAY**-n / STEPS)


def trace_rows():
    pick = np.zeros((6 * LANES, NB), np.float32)
    for face in range(6):
        for lane in range(NFT):
            field, first, second = lane // 16, lane // 4 % 4, lane % 4
            place = [first, second]
            place.insert(face // 2, 0 if face % 2 == 0 else 3)
            pick[face * LANES + lane, field * 64 + place[0] * 16 + place[1] * 4 + place[2]] = 1.0
    return pick.astype(ml_dtypes.bfloat16)


def split(values):
    high = values.astype(BF16)
    low = (values - high.astype(F32)).astype(BF16)
    return high, low


def dot(a, b, dims):
    return lax.dot_general(a, b, dims, preferred_element_type=F32)


def dot3(a, b, dims):
    return dot(a[0], b[0], dims) + (dot(a[0], b[1], dims) + dot(a[1], b[0], dims))


def table_kernel(place, nbr, halo, table):
    upper = place[1] >= SLABS // 2
    steps = jnp.where(upper, nbr[1:2, :], nbr[0:1, :])
    labels = jnp.where(upper, halo[0:1, :], halo[1:2, :])
    rows = [steps[:, :LANES], steps[:, LANES:], labels, labels, nbr[1:2, :LANES], nbr[1:2, LANES:], labels, labels]
    packed = jnp.concatenate(rows)
    for member in range(SLABS // 2):
        table[member] = packed


def order_kernel(nbr, halo, rhs, placed, order, spot):
    def across(face, at):
        return nbr[face, at] & 255

    column = [halo[0, 0] & 255]
    for _ in range(15):
        column.append(across(5, column[-1]))
    rows = [column]
    for _ in range(7):
        rows.append([across(3, at) for at in rows[-1]])
    layers = [rows, [[across(1, at) for at in row] for row in rows]]
    for row in range(8):
        for sheet in range(16):
            spot[rows[row][sheet]] = row * 16 + sheet

    sub = lax.broadcasted_iota(jnp.int32, (8, LANES), 0)
    lane = lax.broadcasted_iota(jnp.int32, (8, LANES), 1)
    for sheet in range(16):
        for layer in range(2):
            at = jnp.zeros((8, LANES), jnp.int32)
            for row in range(8):
                at = jnp.where(sub == row, layers[layer][row][sheet], at)
            order[sheet * 2 + layer, :, :LANES] = jnp.where(lane == at, 1.0, 0.0).astype(F32)
            order[sheet * 2 + layer, :, LANES:] = jnp.where(lane + LANES == at, 1.0, 0.0).astype(F32)

    picks = order[...].reshape(SLAB, SLAB).astype(BF16)
    for step in range(2):
        high, low = split(rhs[step])
        values = dot(picks, high, NT) + dot(picks, low, NT)
        placed[step] = values.reshape(32, 8, NB)


def align_kernel(place, chain, spot, tables, placed, sent, shift):
    group = lax.shift_right_logical(place[1], 2)
    member = place[1] & 3

    def step(slab, at):
        return chain[slab * 8 + lax.shift_right_logical(at, 7), at & 127]

    upper_rows = tables[28:30, :]
    index = lax.broadcasted_iota(jnp.int32, (2, LANES), 0) * LANES + lax.broadcasted_iota(jnp.int32, (2, LANES), 1)
    facing = jnp.sum(jnp.where(upper_rows == SLAB, index, 0)) & 255
    near = jnp.where(group == 0, facing, chain[2, 0] & 255)
    origin = near
    for hop in range(4):
        slab = jnp.where(group == 0, 3 - hop, hop)
        far = step(slab, near) & 255
        origin = jnp.where(slab == member, jnp.where(group == 0, far, near), origin)
        if hop < 3:
            label = step(slab, far) & 127
            ahead = jnp.where(group == 0, 2 - hop, hop + 1)
            near = chain[ahead * 8 + 2, label] & 255
    found = spot[origin] & 127
    first_row, first_sheet = lax.shift_right_logical(found, 4), found & 15
    shift[0] = (8 - first_row) & 7
    shift[1] = first_sheet
    for device in range(16):
        sheet = (SHEET_OF[device] + first_sheet) & 15
        for at in range(2):
            values = placed[at, pl.ds(sheet * 2, 2)]
            values = pltpu.roll(values, (8 - first_row) & 7, 1)
            sent[device, at * 16 : at * 16 + 16, :] = values.reshape(16, NB)


def prepare_kernel(
    place, shift, placed_order, material, modes_in, modes_out, face_lift, rates, pick,
    order, in_h, in_l, out_h, out_l, trace_h, trace_l, lift_h, lift_l, same_r, same_i, cross, lift,
):
    for device in range(16):
        sheet = (SHEET_OF[device] + shift[1]) & 15
        picks = pltpu.roll(placed_order[pl.ds(sheet * 2, 2)], shift[0], 1)
        order[device * 16 : device * 16 + 16, :] = picks.reshape(16, SLAB).astype(BF16)
    own_picks = order[pl.ds(pl.multiple_of(place[0] * 16, 16), 16), :].astype(F32)
    own = jnp.sum(own_picks * material[...], axis=1, keepdims=True)
    in_parts = split(modes_in[...])
    in_h[...], in_l[...] = in_parts
    out_parts = split(modes_out[...])
    out_h[...], out_l[...] = out_parts
    trace_h[...] = dot(pick[...], out_parts[0], NN).astype(BF16)
    trace_l[...] = dot(pick[...], out_parts[1], NN).astype(BF16)
    lift[...] = jnp.zeros_like(lift)
    for face in range(6):
        lift[:, face * LANES : face * LANES + NFT] = face_lift[face]
    lifted = split(dot3(in_parts, split(lift[...]), NN))
    lift_h[...], lift_l[...] = lifted
    for freq in range(16):
        angle = 2.0 * math.pi / STEPS * freq
        rows = slice(freq * 16, freq * 16 + 16)
        real = (1.0 - DECAY * math.cos(angle)) * own + rates[...]
        imag = jnp.broadcast_to((DECAY * math.sin(angle) if freq else 0.0) * own, (16, NB))
        size = real * real + imag * imag
        same = real / size
        same_r[rows, :] = same
        same_i[rows, :] = same if freq else 1.0 / ((1.0 + DECAY) * own + rates[...])
        cross[rows, :] = imag / size


def divided(modal, same_r, same_i, cross):
    real, imag = modal[:HALF], modal[HALF:]
    mixed = cross[...]
    return jnp.concatenate(
        [real * same_r[...] + imag * mixed, imag * same_i[...] - real * mixed]
    )


def pack(values):
    quarter = values.shape[0] // 4
    lane = lax.broadcasted_iota(jnp.int32, (quarter, LANES), 1)
    tail = values[3 * quarter :]
    parts = []
    for part in range(3):
        moved = pltpu.roll(tail, NFT - 32 * part, 1)
        parts.append(jnp.where(lane < NFT, values[part * quarter : (part + 1) * quarter], moved))
    return jnp.concatenate(parts)


def unpack(packed):
    quarter = packed.shape[0] // 3
    lane = lax.broadcasted_iota(jnp.int32, (quarter, LANES), 1)
    moved = [pltpu.roll(packed[part * quarter : (part + 1) * quarter], 32 + 32 * part, 1) for part in range(3)]
    tail = jnp.where(lane < 32, moved[0], jnp.where(lane < 64, moved[1], moved[2]))
    return jnp.concatenate([packed, tail])


def send_traces(place, traces, inner, to_chip, to_next, to_even, to_odd):
    core_low = place[0] & 1 == 0
    slab_even = place[1] & 1 == 0
    inner[...] = traces[:, : 4 * LANES]
    below, above = traces[:, 4 * LANES : 5 * LANES], traces[:, 5 * LANES :]
    to_chip[...] = pack(jnp.where(core_low, above, below))
    to_next[...] = pack(jnp.where(core_low, below, above))
    sides = traces[:, : 2 * LANES].reshape(STEPS, 2, 8, 2 * LANES)
    lower = sides[:, 0, :, :LANES].reshape(HALF, LANES)
    upper = sides[:, 1, :, LANES:].reshape(HALF, LANES)
    to_even[...] = pack(jnp.where(slab_even, upper, lower))
    to_odd[...] = pack(jnp.where(slab_even, lower, upper))


def first_kernel(
    place, steps, in_h, in_l, trace_h, trace_l, same_r, same_i, cross,
    modal, inner, to_chip, to_next, to_even, to_odd, spectrum,
):
    to_frequencies(steps, spectrum)
    start = dot3(split(spectrum[...]), (in_h[...], in_l[...]), NT)
    modal[...] = start
    solved = split(divided(start, same_r, same_i, cross))
    traces = dot3(solved, (trace_h[...], trace_l[...]), NT)
    send_traces(place, traces, inner, to_chip, to_next, to_even, to_odd)


def gathered(place, inner, from_chip, from_next, from_even, from_odd):
    core_low = place[0] & 1 == 0
    slab_even = place[1] & 1 == 0

    def face(which):
        return inner[:, which * LANES : which * LANES + LANES]

    below = unpack(jnp.where(slab_even, from_odd[...], from_even[...])).reshape(STEPS, 1, 8, LANES)
    above = unpack(jnp.where(slab_even, from_even[...], from_odd[...])).reshape(STEPS, 1, 8, LANES)
    first = face(0).reshape(STEPS, 2, 8, LANES)
    second = face(1).reshape(STEPS, 2, 8, LANES)
    minus_x = jnp.concatenate([below, second[:, :1]], axis=1).reshape(ROWS, LANES)
    plus_x = jnp.concatenate([first[:, 1:], above], axis=1).reshape(ROWS, LANES)
    minus_y = pltpu.roll(face(3).reshape(ROWS // 8, 8, LANES), 1, 1).reshape(ROWS, LANES)
    plus_y = pltpu.roll(face(2).reshape(ROWS // 8, 8, LANES), 7, 1).reshape(ROWS, LANES)
    minus_z = unpack(jnp.where(core_low, from_next[...], from_chip[...]))
    plus_z = unpack(jnp.where(core_low, from_chip[...], from_next[...]))
    return jnp.concatenate([minus_x, plus_x, minus_y, plus_y, minus_z, plus_z], axis=1)


def sweep_kernel(
    place, modal, inner, from_chip, from_next, from_even, from_odd,
    lift_h, lift_l, trace_h, trace_l, same_r, same_i, cross,
    inner_out, to_chip, to_next, to_even, to_odd,
):
    faces = split(gathered(place, inner, from_chip, from_next, from_even, from_odd))
    corrected = modal[...] - dot3(faces, (lift_h[...], lift_l[...]), NT)
    solved = split(divided(corrected, same_r, same_i, cross))
    traces = dot3(solved, (trace_h[...], trace_l[...]), NT)
    send_traces(place, traces, inner_out, to_chip, to_next, to_even, to_odd)


def last_kernel(
    place, modal, inner, from_chip, from_next, from_even, from_odd,
    lift_h, lift_l, out_h, out_l, same_r, same_i, cross,
    steps, spectrum,
):
    faces = split(gathered(place, inner, from_chip, from_next, from_even, from_odd))
    corrected = modal[...] - dot3(faces, (lift_h[...], lift_l[...]), NT)
    solved = split(divided(corrected, same_r, same_i, cross))
    spectrum[...] = dot3(solved, (out_h[...], out_l[...]), NT)
    to_steps(spectrum, steps)


def restore_kernel(arrived, order, out):
    for step in range(2):
        values = arrived[:, step * 16 : step * 16 + 16, :].reshape(SLAB, NB)
        high, low = split(values)
        picks = order[...]
        out[step] = dot(high, picks, TN) + dot(low, picks, TN)


SMEM = pl.BlockSpec(memory_space=pltpu.SMEM)
VMEM = pl.BlockSpec(memory_space=pltpu.VMEM)


def call(body, outs, scalars, arrays, flops, scratch=(), scalar_outs=(), megabytes=16):
    outs = [jax.ShapeDtypeStruct(shape, kind) for shape, kind in outs]
    scalar_outs = [jax.ShapeDtypeStruct(shape, jnp.int32) for shape in scalar_outs]
    moved = sum(a.size * a.dtype.itemsize for a in [*outs, *arrays])
    return pl.pallas_call(
        body,
        out_shape=outs + scalar_outs,
        in_specs=[SMEM] * len(scalars) + [VMEM] * len(arrays),
        out_specs=[VMEM] * len(outs) + [SMEM] * len(scalar_outs),
        scratch_shapes=list(scratch),
        compiler_params=pltpu.CompilerParams(vmem_limit_bytes=megabytes * 2**20),
        cost_estimate=pl.CostEstimate(flops=flops, bytes_accessed=moved, transcendentals=0),
    )(*scalars, *arrays)


def shards(rhs, material, modal_rates, modes_in, modes_out, face_lift, neighbours, halo_send):
    place = jnp.stack([lax.axis_index("tm"), lax.axis_index("space")]).astype(jnp.int32)
    (table,) = call(table_kernel, [((4, 8, LANES), jnp.int32)], [place], [neighbours, halo_send], 10**4)
    chain = lax.all_to_all(
        table, "space", 0, 0, tiled=True, axis_index_groups=[[0, 1, 2, 3], [4, 5, 6, 7]]
    ).reshape(32, LANES)
    placed, placed_order, spot = call(
        order_kernel,
        [((2, 32, 8, NB), F32), ((32, 8, SLAB), F32)],
        [neighbours, halo_send],
        [rhs],
        2 * 4 * 256 * 256 * 384,
        scalar_outs=[(SLAB,)],
    )
    sent, shift = call(
        align_kernel, [((16, 32, NB), F32)], [place, chain, spot], [chain, placed], 10**6, scalar_outs=[(2,)]
    )
    arrived = lax.all_to_all(sent, "tm", 0, 0, tiled=True).reshape(ROWS, NB)
    order, in_h, in_l, out_h, out_l, trace_h, trace_l, lift_h, lift_l, same_r, same_i, cross = call(
        prepare_kernel,
        [((SLAB, SLAB), BF16)]
        + [((NB, NB), BF16)] * 4
        + [((6 * LANES, NB), BF16)] * 2
        + [((NB, 6 * LANES), BF16)] * 2
        + [((HALF, NB), F32)] * 3,
        [place, shift],
        [placed_order, material.reshape(1, SLAB), modes_in, modes_out, face_lift, modal_rates.reshape(1, NB)]
        + [jnp.asarray(trace_rows())],
        2 * 5 * 384 * 384 * 768,
        [pltpu.VMEM((NB, 6 * LANES), F32)],
    )

    faces = [((ROWS, 4 * LANES), F32)] + [((ROWS * 3 // 4, LANES), F32)] * 2 + [((HALF * 3 // 4, LANES), F32)] * 2

    def exchange(to_chip, to_next, to_even, to_odd):
        from_odd = lax.ppermute(to_odd, "space", ODD_SIDES)
        from_even = lax.ppermute(to_even, "space", EVEN_SIDES)
        from_next = lax.ppermute(to_next, "tm", NEXT_CHIP)
        from_chip = lax.ppermute(to_chip, "tm", SAME_CHIP)
        return from_chip, from_next, from_even, from_odd

    coefficients = [same_r, same_i, cross]
    modal, inner, *outgoing = call(
        first_kernel,
        [((ROWS, NB), F32)] + faces,
        [place],
        [arrived, in_h, in_l, trace_h, trace_l] + coefficients,
        2 * 3 * 512 * 384 * (384 + 768),
        [pltpu.VMEM((ROWS, NB), F32)],
    )
    incoming = exchange(*outgoing)
    inner, *outgoing = call(
        sweep_kernel,
        faces,
        [place],
        [modal, inner, *incoming, lift_h, lift_l, trace_h, trace_l] + coefficients,
        2 * 3 * 512 * 384 * (768 + 768),
    )
    incoming = exchange(*outgoing)
    (steps,) = call(
        last_kernel,
        [((ROWS, NB), F32)],
        [place],
        [modal, inner, *incoming, lift_h, lift_l, out_h, out_l] + coefficients,
        2 * 3 * 512 * 384 * (768 + 384),
        [pltpu.VMEM((ROWS, NB), F32)],
    )
    back = lax.all_to_all(steps.reshape(16, 32, NB), "tm", 0, 0, tiled=True)
    (out,) = call(
        restore_kernel, [((2, NB, SLAB), F32)], [], [back, order], 2 * 4 * 256 * 256 * 384
    )
    return out


def solution(mesh):
    return jax.shard_map(
        shards,
        mesh=mesh,
        in_specs=(
            P("tm", None, "space"),
            P("space"),
            P(),
            P(),
            P(),
            P(),
            P(None, "space"),
            P(None, "space"),
        ),
        out_specs=P("tm", None, "space"),
        check_vma=False,
    )
```

```python
import math

import jax
import jax.numpy as jnp
import ml_dtypes
import numpy as np
from jax import lax
from jax.experimental import pallas as pl
from jax.experimental.pallas import tpu as pltpu
from jax.sharding import PartitionSpec as P

NB = 384
NFT = 96
LANES = 128
STEPS = 32
SLAB = 256
SHEET = 16
ROWS = STEPS * SHEET
HALF = ROWS // 2
SLABS = 8
DECAY = 0.1 ** (1.0 / STEPS)

RING = (0, 1, 4, 5, 8, 9, 12, 13, 14, 15, 10, 11, 6, 7, 2, 3)
SHEET_OF = tuple(RING.index(device) for device in range(16))
SAME_CHIP = [(i, i ^ 1) for i in range(16)]
NEXT_CHIP = [(RING[2 * i + 1], RING[(2 * i + 2) % 16]) for i in range(8)]
NEXT_CHIP = NEXT_CHIP + [(b, a) for a, b in NEXT_CHIP]
EVEN_SIDES = [(i, i ^ 1) for i in range(8)]
ODD_SIDES = [(1, 2), (2, 1), (3, 4), (4, 3), (5, 6), (6, 5)]

F32 = jnp.float32
BF16 = jnp.bfloat16
NN = (((1,), (0,)), ((), ()))
NT = (((1,), (1,)), ((), ()))
TN = (((0,), (0,)), ((), ()))


def real_fft(steps):
    count = len(steps)
    if count == 2:
        return [(steps[0] + steps[1], None), (steps[0] - steps[1], None)]
    even, odd = real_fft(steps[0::2]), real_fft(steps[1::2])
    out = [None] * (count // 2 + 1)
    out[0] = (even[0][0] + odd[0][0], None)
    out[count // 2] = (even[0][0] - odd[0][0], None)
    out[count // 4] = (even[count // 4][0], -odd[count // 4][0])
    for freq in range(1, count // 4):
        cos, sin = math.cos(2.0 * math.pi * freq / count), math.sin(2.0 * math.pi * freq / count)
        real, imag = odd[freq]
        turned_real, turned_imag = real * cos + imag * sin, imag * cos - real * sin
        real, imag = even[freq]
        out[freq] = (real + turned_real, imag + turned_imag)
        out[count // 2 - freq] = (real - turned_real, turned_imag - imag)
    return out


def real_ifft(freqs):
    count = 2 * (len(freqs) - 1)
    first, last = freqs[0][0], freqs[-1][0]
    if count == 2:
        return [first + last, first - last]
    even, odd = [None] * (count // 4 + 1), [None] * (count // 4 + 1)
    even[0], odd[0] = (first + last, None), (first - last, None)
    middle = freqs[count // 4]
    even[-1], odd[-1] = (2.0 * middle[0], None), (-2.0 * middle[1], None)
    for freq in range(1, count // 4):
        cos, sin = math.cos(2.0 * math.pi * freq / count), math.sin(2.0 * math.pi * freq / count)
        (real, imag), (other_real, other_imag) = freqs[freq], freqs[count // 2 - freq]
        even[freq] = (real + other_real, imag - other_imag)
        real, imag = real - other_real, imag + other_imag
        odd[freq] = (real * cos - imag * sin, imag * cos + real * sin)
    out = [None] * count
    out[0::2], out[1::2] = real_ifft(even), real_ifft(odd)
    return out


def tiles():
    for block in range(SHEET // 8):
        for lane in range(0, NB, LANES):
            yield lambda row: (slice(row * SHEET + block * 8, row * SHEET + block * 8 + 8), slice(lane, lane + LANES))


def to_frequencies(steps, spectrum):
    for at in tiles():
        freqs = real_fft([steps[at(n)] * DECAY**n for n in range(STEPS)])
        for freq in range(16):
            spectrum[at(freq)] = freqs[freq][0]
            spectrum[at(16 + freq)] = freqs[freq][1] if freq else freqs[16][0]


def to_steps(spectrum, steps):
    for at in tiles():
        pairs = [(spectrum[at(freq)], spectrum[at(16 + freq)]) for freq in range(16)]
        freqs = [(pairs[0][0], None)] + pairs[1:] + [(pairs[0][1], None)]
        for n, value in enumerate(real_ifft(freqs)):
            steps[at(n)] = value * (DECAY**-n / STEPS)


def trace_rows():
    pick = np.zeros((6 * LANES, NB), np.float32)
    for face in range(6):
        for lane in range(NFT):
            field, first, second = lane // 16, lane // 4 % 4, lane % 4
            place = [first, second]
            place.insert(face // 2, 0 if face % 2 == 0 else 3)
            pick[face * LANES + lane, field * 64 + place[0] * 16 + place[1] * 4 + place[2]] = 1.0
    return pick.astype(ml_dtypes.bfloat16)


def split(values):
    high = values.astype(BF16)
    low = (values - high.astype(F32)).astype(BF16)
    return high, low


def dot(a, b, dims):
    return lax.dot_general(a, b, dims, preferred_element_type=F32)


def dot3(a, b, dims):
    return dot(a[0], b[0], dims) + (dot(a[0], b[1], dims) + dot(a[1], b[0], dims))


def table_kernel(place, nbr_far, halo_far, table, nbr, halo, done):
    copies = [
        pltpu.make_async_copy(far, near, done.at[at])
        for at, (far, near) in enumerate([(nbr_far, nbr), (halo_far, halo)])
    ]
    for copy in copies:
        copy.start()
    for copy in copies:
        copy.wait()
    upper = place[1] >= SLABS // 2
    steps = jnp.where(upper, nbr[1:2, :], nbr[0:1, :])
    labels = jnp.where(upper, halo[0:1, :], halo[1:2, :])
    rows = [steps[:, :LANES], steps[:, LANES:], labels, labels, nbr[1:2, :LANES], nbr[1:2, LANES:], labels, labels]
    packed = jnp.concatenate(rows)
    for member in range(SLABS // 2):
        table[member] = packed


def order_kernel(nbr_far, halo_far, rhs_far, placed, order, spot, nbr, halo, rhs, done):
    copies = [
        pltpu.make_async_copy(far, near, done.at[at])
        for at, (far, near) in enumerate([(nbr_far, nbr), (halo_far, halo), (rhs_far, rhs)])
    ]
    for copy in copies:
        copy.start()
    copies[0].wait()
    copies[1].wait()

    def across(face, at):
        return nbr[face, at] & 255

    column = [halo[0, 0] & 255]
    for _ in range(15):
        column.append(across(5, column[-1]))
    rows = [column]
    for _ in range(7):
        rows.append([across(3, at) for at in rows[-1]])
    layers = [rows, [[across(1, at) for at in row] for row in rows]]
    for row in range(8):
        for sheet in range(16):
            spot[rows[row][sheet]] = row * 16 + sheet

    sub = lax.broadcasted_iota(jnp.int32, (8, LANES), 0)
    lane = lax.broadcasted_iota(jnp.int32, (8, LANES), 1)
    for sheet in range(16):
        for layer in range(2):
            at = jnp.zeros((8, LANES), jnp.int32)
            for row in range(8):
                at = jnp.where(sub == row, layers[layer][row][sheet], at)
            order[sheet * 2 + layer, :, :LANES] = jnp.where(lane == at, 1.0, 0.0).astype(F32)
            order[sheet * 2 + layer, :, LANES:] = jnp.where(lane + LANES == at, 1.0, 0.0).astype(F32)

    picks = order[...].reshape(SLAB, SLAB).astype(BF16)
    copies[2].wait()
    for step in range(2):
        high, low = split(rhs[step])
        values = dot(picks, high, NT) + dot(picks, low, NT)
        placed[step] = values.reshape(32, 8, NB)


def align_kernel(place, spot, placed, far, sent, shift, chain, tables, done):
    copies = [pltpu.make_async_copy(far, near, done.at[at]) for at, near in enumerate([chain, tables])]
    for copy in copies:
        copy.start()
    for copy in copies:
        copy.wait()
    group = lax.shift_right_logical(place[1], 2)
    member = place[1] & 3

    def step(slab, at):
        return chain[slab * 8 + lax.shift_right_logical(at, 7), at & 127]

    upper_rows = tables[28:30, :]
    index = lax.broadcasted_iota(jnp.int32, (2, LANES), 0) * LANES + lax.broadcasted_iota(jnp.int32, (2, LANES), 1)
    facing = jnp.sum(jnp.where(upper_rows == SLAB, index, 0)) & 255
    near = jnp.where(group == 0, facing, chain[2, 0] & 255)
    origin = near
    for hop in range(4):
        slab = jnp.where(group == 0, 3 - hop, hop)
        far_side = step(slab, near) & 255
        origin = jnp.where(slab == member, jnp.where(group == 0, far_side, near), origin)
        if hop < 3:
            label = step(slab, far_side) & 127
            ahead = jnp.where(group == 0, 2 - hop, hop + 1)
            near = chain[ahead * 8 + 2, label] & 255
    found = spot[origin] & 127
    first_row, first_sheet = lax.shift_right_logical(found, 4), found & 15
    shift[0] = (8 - first_row) & 7
    shift[1] = first_sheet
    for device in range(16):
        sheet = (SHEET_OF[device] + first_sheet) & 15
        for at in range(2):
            values = placed[at, pl.ds(sheet * 2, 2)]
            values = pltpu.roll(values, (8 - first_row) & 7, 1)
            sent[device, at * 16 : at * 16 + 16, :] = values.reshape(16, NB)


def first_weights(ref):
    return [ref.at[a:b] for a, b in [(0, 384), (384, 768), (768, 1536), (1536, 2304)]]


def second_weights(ref):
    return [ref.at[a:b] for a, b in [(0, 768), (768, 1536), (1536, 1920), (1920, 2304)]]


def prepare_kernel(place, shift, placed_order, material, modes_in, modes_out, face_lift, rates, pick, *refs):
    order, first_set, factors, second_far, second_set, lift, done = refs
    in_h, in_l, trace_h, trace_l = first_weights(first_set)
    lift_h, lift_l, out_h, out_l = second_weights(second_set)
    same_r, same_i, cross = factors.at[0], factors.at[1], factors.at[2]
    in_parts = split(modes_in[...])
    in_h[...], in_l[...] = in_parts
    out_parts = split(modes_out[...])
    out_h[...], out_l[...] = out_parts
    trace_h[...] = dot(pick[...], out_parts[0], NN).astype(BF16)
    trace_l[...] = dot(pick[...], out_parts[1], NN).astype(BF16)
    for device in range(16):
        sheet = (SHEET_OF[device] + shift[1]) & 15
        picks = pltpu.roll(placed_order[pl.ds(sheet * 2, 2)], shift[0], 1)
        order[device * 16 : device * 16 + 16, :] = picks.reshape(16, SLAB).astype(BF16)
    own_picks = order[pl.ds(pl.multiple_of(place[0] * 16, 16), 16), :].astype(F32)
    own = jnp.sum(own_picks * material[...], axis=1, keepdims=True)
    for freq in range(16):
        angle = 2.0 * math.pi / STEPS * freq
        rows = slice(freq * 16, freq * 16 + 16)
        real = (1.0 - DECAY * math.cos(angle)) * own + rates[...]
        imag = jnp.broadcast_to((DECAY * math.sin(angle) if freq else 0.0) * own, (16, NB))
        size = real * real + imag * imag
        same = real / size
        same_r[rows, :] = same
        same_i[rows, :] = same if freq else 1.0 / ((1.0 + DECAY) * own + rates[...])
        cross[rows, :] = imag / size
    lift[...] = jnp.zeros_like(lift)
    for face in range(6):
        lift[face * LANES : face * LANES + NFT, :] = face_lift[face]
    lift_h[...], lift_l[...] = split(dot3(split(lift[...]), in_parts, NT))
    copy = pltpu.make_async_copy(second_set, second_far, done)
    copy.start()
    copy.wait()


def divided(modal, factors):
    real, imag = modal[:HALF], modal[HALF:]
    mixed = factors[2]
    return jnp.concatenate(
        [real * factors[0] + imag * mixed, imag * factors[1] - real * mixed]
    )


def pack(values):
    quarter = values.shape[0] // 4
    lane = lax.broadcasted_iota(jnp.int32, (quarter, LANES), 1)
    tail = values[3 * quarter :]
    parts = []
    for part in range(3):
        moved = pltpu.roll(tail, NFT - 32 * part, 1)
        parts.append(jnp.where(lane < NFT, values[part * quarter : (part + 1) * quarter], moved))
    return jnp.concatenate(parts)


def unpack(packed):
    quarter = packed.shape[0] // 3
    lane = lax.broadcasted_iota(jnp.int32, (quarter, LANES), 1)
    moved = [pltpu.roll(packed[part * quarter : (part + 1) * quarter], 32 + 32 * part, 1) for part in range(3)]
    tail = jnp.where(lane < 32, moved[0], jnp.where(lane < 64, moved[1], moved[2]))
    return jnp.concatenate([packed, tail])


def send_traces(place, traces, inner, to_chip, to_next, to_even, to_odd):
    core_low = place[0] & 1 == 0
    slab_even = place[1] & 1 == 0
    inner[...] = traces[:, : 4 * LANES]
    below, above = traces[:, 4 * LANES : 5 * LANES], traces[:, 5 * LANES :]
    to_chip[...] = pack(jnp.where(core_low, above, below))
    to_next[...] = pack(jnp.where(core_low, below, above))
    sides = traces[:, : 2 * LANES].reshape(STEPS, 2, 8, 2 * LANES)
    lower = sides[:, 0, :, :LANES].reshape(HALF, LANES)
    upper = sides[:, 1, :, LANES:].reshape(HALF, LANES)
    to_even[...] = pack(jnp.where(slab_even, upper, lower))
    to_odd[...] = pack(jnp.where(slab_even, lower, upper))


def first_kernel(
    place, steps, first_set, factors,
    modal, inner, to_chip, to_next, to_even, to_odd, spectrum,
):
    in_h, in_l, trace_h, trace_l = first_weights(first_set)
    to_frequencies(steps, spectrum)
    start = dot3(split(spectrum[...]), (in_h[...], in_l[...]), NT)
    modal[...] = start
    solved = split(divided(start, factors))
    traces = dot3(solved, (trace_h[...], trace_l[...]), NT)
    send_traces(place, traces, inner, to_chip, to_next, to_even, to_odd)


def gathered(place, inner, from_chip, from_next, from_even, from_odd):
    core_low = place[0] & 1 == 0
    slab_even = place[1] & 1 == 0

    def face(which):
        return inner[:, which * LANES : which * LANES + LANES]

    below = unpack(jnp.where(slab_even, from_odd[...], from_even[...])).reshape(STEPS, 1, 8, LANES)
    above = unpack(jnp.where(slab_even, from_even[...], from_odd[...])).reshape(STEPS, 1, 8, LANES)
    first = face(0).reshape(STEPS, 2, 8, LANES)
    second = face(1).reshape(STEPS, 2, 8, LANES)
    minus_x = jnp.concatenate([below, second[:, :1]], axis=1).reshape(ROWS, LANES)
    plus_x = jnp.concatenate([first[:, 1:], above], axis=1).reshape(ROWS, LANES)
    minus_y = pltpu.roll(face(3).reshape(ROWS // 8, 8, LANES), 1, 1).reshape(ROWS, LANES)
    plus_y = pltpu.roll(face(2).reshape(ROWS // 8, 8, LANES), 7, 1).reshape(ROWS, LANES)
    minus_z = unpack(jnp.where(core_low, from_next[...], from_chip[...]))
    plus_z = unpack(jnp.where(core_low, from_chip[...], from_next[...]))
    return jnp.concatenate([minus_x, plus_x, minus_y, plus_y, minus_z, plus_z], axis=1)


def sweep_kernel(
    place, from_chip, from_next, from_even, from_odd, modal, inner,
    first_set, second_set, factors,
    inner_out, to_chip, to_next, to_even, to_odd,
):
    _, _, trace_h, trace_l = first_weights(first_set)
    lift_h, lift_l, _, _ = second_weights(second_set)
    faces = split(gathered(place, inner, from_chip, from_next, from_even, from_odd))
    corrected = modal[...] - dot3(faces, (lift_h[...], lift_l[...]), NN)
    solved = split(divided(corrected, factors))
    traces = dot3(solved, (trace_h[...], trace_l[...]), NT)
    send_traces(place, traces, inner_out, to_chip, to_next, to_even, to_odd)


def last_kernel(
    place, from_chip, from_next, from_even, from_odd, modal, inner,
    second_set, factors,
    steps, spectrum,
):
    lift_h, lift_l, out_h, out_l = second_weights(second_set)
    faces = split(gathered(place, inner, from_chip, from_next, from_even, from_odd))
    corrected = modal[...] - dot3(faces, (lift_h[...], lift_l[...]), NN)
    solved = split(divided(corrected, factors))
    spectrum[...] = dot3(solved, (out_h[...], out_l[...]), NT)
    to_steps(spectrum, steps)


def restore_kernel(arrived, order, out):
    for step in range(2):
        values = arrived[:, step * 16 : step * 16 + 16, :].reshape(SLAB, NB)
        high, low = split(values)
        picks = order[...]
        out[step] = dot(high, picks, TN) + dot(low, picks, TN)


SMEM = pl.BlockSpec(memory_space=pltpu.SMEM)
VMEM = pl.BlockSpec(memory_space=pltpu.VMEM)
HBM = pl.BlockSpec(memory_space=pltpu.HBM)
KEPT = pl.BlockSpec(memory_space=pltpu.VMEM)
DMA = pltpu.SemaphoreType.DMA
HELD = ((HBM, pltpu.HBM), (KEPT, pltpu.VMEM))


def call(body, ins, outs, flops, scratch=(), megabytes=8):
    shapes = [jax.ShapeDtypeStruct(shape, kind) for shape, kind, _ in outs]
    moved = sum(a.size * a.dtype.itemsize for a in shapes + [a for a, _ in ins])
    for held, space in HELD:
        ins = [(pltpu.with_memory_space_constraint(a, space) if spec is held else a, spec) for a, spec in ins]
        shapes = [space(shape, kind) if spec is held else old for old, (shape, kind, spec) in zip(shapes, outs)]
    return pl.pallas_call(
        body,
        out_shape=shapes,
        in_specs=[spec for _, spec in ins],
        out_specs=[spec for _, _, spec in outs],
        scratch_shapes=list(scratch),
        compiler_params=pltpu.CompilerParams(vmem_limit_bytes=megabytes * 2**20),
        cost_estimate=pl.CostEstimate(flops=flops, bytes_accessed=moved, transcendentals=0),
    )(*[a for a, _ in ins])


def shards(rhs, material, modal_rates, modes_in, modes_out, face_lift, neighbours, halo_send):
    place = (jnp.stack([lax.axis_index("tm"), lax.axis_index("space")]).astype(jnp.int32), SMEM)
    (table,) = call(
        table_kernel,
        [place, (neighbours, HBM), (halo_send, HBM)],
        [((4, 8, LANES), jnp.int32, KEPT)],
        10**4,
        [pltpu.VMEM(neighbours.shape, jnp.int32), pltpu.VMEM(halo_send.shape, jnp.int32), DMA((2,))],
    )
    chain = lax.all_to_all(
        table, "space", 0, 0, tiled=True, axis_index_groups=[[0, 1, 2, 3], [4, 5, 6, 7]]
    ).reshape(32, LANES)
    placed, placed_order, spot = call(
        order_kernel,
        [(neighbours, HBM), (halo_send, HBM), (rhs, HBM)],
        [((2, 32, 8, NB), F32, KEPT), ((32, 8, SLAB), F32, KEPT), ((SLAB,), jnp.int32, SMEM)],
        2 * 4 * 256 * 256 * 384,
        [
            pltpu.SMEM(neighbours.shape, jnp.int32),
            pltpu.SMEM(halo_send.shape, jnp.int32),
            pltpu.VMEM(rhs.shape, F32),
            DMA((3,)),
        ],
    )
    sent, shift = call(
        align_kernel,
        [place, (spot, SMEM), (placed, KEPT), (chain, VMEM)],
        [((16, 32, NB), F32, KEPT), ((2,), jnp.int32, SMEM)],
        10**6,
        [pltpu.SMEM((32, LANES), jnp.int32), pltpu.VMEM((32, LANES), jnp.int32), DMA((2,))],
    )
    arrived = lax.all_to_all(sent, "tm", 0, 0, tiled=True).reshape(ROWS, NB)
    weights = [modes_in, modes_out, jnp.swapaxes(face_lift, 1, 2), modal_rates.reshape(1, NB), trace_rows()]
    prepared = [((SLAB, SLAB), BF16, KEPT), ((2304, NB), BF16, KEPT), ((3, HALF, NB), F32, KEPT), ((2304, NB), BF16, HBM)]
    order, first_set, factors, second_set = call(
        prepare_kernel,
        [place, (shift, SMEM), (placed_order, KEPT), (material.reshape(1, SLAB), VMEM)]
        + [(jnp.asarray(weight), VMEM) for weight in weights],
        prepared,
        2 * 5 * 384 * 384 * 768,
        [pltpu.VMEM((2304, NB), BF16), pltpu.VMEM((6 * LANES, NB), F32), DMA],
    )

    faces = (
        [((ROWS, 4 * LANES), F32, KEPT)]
        + [((ROWS * 3 // 4, LANES), F32, VMEM)] * 2
        + [((HALF * 3 // 4, LANES), F32, VMEM)] * 2
    )

    def exchange(to_chip, to_next, to_even, to_odd):
        from_odd = lax.ppermute(to_odd, "space", ODD_SIDES)
        from_even = lax.ppermute(to_even, "space", EVEN_SIDES)
        from_next = lax.ppermute(to_next, "tm", NEXT_CHIP)
        from_chip = lax.ppermute(to_chip, "tm", SAME_CHIP)
        return from_chip, from_next, from_even, from_odd

    modal, inner, *outgoing = call(
        first_kernel,
        [place, (arrived, VMEM), (first_set, KEPT), (factors, KEPT)],
        [((ROWS, NB), F32, KEPT)] + faces,
        2 * 3 * 512 * 384 * (384 + 768),
        [pltpu.VMEM((ROWS, NB), F32)],
    )
    incoming = exchange(*outgoing)
    inner, *outgoing = call(
        sweep_kernel,
        [place]
        + [(a, VMEM) for a in incoming] + [(a, KEPT) for a in [modal, inner, first_set]] + [(second_set, VMEM), (factors, KEPT)],
        faces,
        2 * 3 * 512 * 384 * (768 + 768),
    )
    incoming = exchange(*outgoing)
    (steps,) = call(
        last_kernel,
        [place]
        + [(a, VMEM) for a in incoming] + [(a, KEPT) for a in [modal, inner]] + [(second_set, VMEM), (factors, KEPT)],
        [((ROWS, NB), F32, VMEM)],
        2 * 3 * 512 * 384 * (768 + 384),
        [pltpu.VMEM((ROWS, NB), F32)],
    )
    back = lax.all_to_all(steps.reshape(16, 32, NB), "tm", 0, 0, tiled=True)
    (out,) = call(
        restore_kernel,
        [(back, VMEM), (order, KEPT)],
        [((2, NB, SLAB), F32, VMEM)],
        2 * 4 * 256 * 256 * 384,
    )
    return out


def solution(mesh):
    return jax.shard_map(
        shards,
        mesh=mesh,
        in_specs=(
            P("tm", None, "space"),
            P("space"),
            P(),
            P(),
            P(),
            P(),
            P(None, "space"),
            P(None, "space"),
        ),
        out_specs=P("tm", None, "space"),
        check_vma=False,
    )
```

```python
import math

import jax
import jax.numpy as jnp
import ml_dtypes
import numpy as np
from jax import lax
from jax.experimental import pallas as pl
from jax.experimental.pallas import tpu as pltpu
from jax.sharding import PartitionSpec as P

NB = 384
NFT = 96
LANES = 128
STEPS = 32
SLAB = 256
SHEET = 16
ROWS = STEPS * SHEET
HALF = ROWS // 2
SLABS = 8
DECAY = 0.1 ** (1.0 / STEPS)

RING = (0, 1, 4, 5, 8, 9, 12, 13, 14, 15, 10, 11, 6, 7, 2, 3)
SHEET_OF = tuple(RING.index(device) for device in range(16))
SAME_CHIP = [(i, i ^ 1) for i in range(16)]
NEXT_CHIP = [(RING[2 * i + 1], RING[(2 * i + 2) % 16]) for i in range(8)]
NEXT_CHIP = NEXT_CHIP + [(b, a) for a, b in NEXT_CHIP]
EVEN_SIDES = [(i, i ^ 1) for i in range(8)]
ODD_SIDES = [(1, 2), (2, 1), (3, 4), (4, 3), (5, 6), (6, 5)]

F32 = jnp.float32
BF16 = jnp.bfloat16
NN = (((1,), (0,)), ((), ()))
NT = (((1,), (1,)), ((), ()))
TN = (((0,), (0,)), ((), ()))


def real_fft(steps):
    count = len(steps)
    if count == 2:
        return [(steps[0] + steps[1], None), (steps[0] - steps[1], None)]
    even, odd = real_fft(steps[0::2]), real_fft(steps[1::2])
    out = [None] * (count // 2 + 1)
    out[0] = (even[0][0] + odd[0][0], None)
    out[count // 2] = (even[0][0] - odd[0][0], None)
    out[count // 4] = (even[count // 4][0], -odd[count // 4][0])
    for freq in range(1, count // 4):
        cos, sin = math.cos(2.0 * math.pi * freq / count), math.sin(2.0 * math.pi * freq / count)
        real, imag = odd[freq]
        turned_real, turned_imag = real * cos + imag * sin, imag * cos - real * sin
        real, imag = even[freq]
        out[freq] = (real + turned_real, imag + turned_imag)
        out[count // 2 - freq] = (real - turned_real, turned_imag - imag)
    return out


def real_ifft(freqs):
    count = 2 * (len(freqs) - 1)
    first, last = freqs[0][0], freqs[-1][0]
    if count == 2:
        return [first + last, first - last]
    even, odd = [None] * (count // 4 + 1), [None] * (count // 4 + 1)
    even[0], odd[0] = (first + last, None), (first - last, None)
    middle = freqs[count // 4]
    even[-1], odd[-1] = (2.0 * middle[0], None), (-2.0 * middle[1], None)
    for freq in range(1, count // 4):
        cos, sin = math.cos(2.0 * math.pi * freq / count), math.sin(2.0 * math.pi * freq / count)
        (real, imag), (other_real, other_imag) = freqs[freq], freqs[count // 2 - freq]
        even[freq] = (real + other_real, imag - other_imag)
        real, imag = real - other_real, imag + other_imag
        odd[freq] = (real * cos - imag * sin, imag * cos + real * sin)
    out = [None] * count
    out[0::2], out[1::2] = real_ifft(even), real_ifft(odd)
    return out


def tiles():
    for lane in range(0, NB, LANES):
        for block in range(SHEET // 8):
            yield lambda row: (slice(row * SHEET + block * 8, row * SHEET + block * 8 + 8), slice(lane, lane + LANES))


def to_frequencies(steps, spectrum, copies):
    for place, at in enumerate(tiles()):
        if place % 2 == 0:
            copies[place // 2].wait()
        freqs = real_fft([steps[at(n)] * DECAY**n for n in range(STEPS)])
        for freq in range(16):
            spectrum[at(freq)] = freqs[freq][0]
            spectrum[at(16 + freq)] = freqs[freq][1] if freq else freqs[16][0]


def to_steps(spectrum, steps):
    for at in tiles():
        pairs = [(spectrum[at(freq)], spectrum[at(16 + freq)]) for freq in range(16)]
        freqs = [(pairs[0][0], None)] + pairs[1:] + [(pairs[0][1], None)]
        for n, value in enumerate(real_ifft(freqs)):
            steps[at(n)] = value * (DECAY**-n / STEPS)


def trace_rows():
    pick = np.zeros((6 * LANES, NB), np.float32)
    for face in range(6):
        for lane in range(NFT):
            field, first, second = lane // 16, lane // 4 % 4, lane % 4
            place = [first, second]
            place.insert(face // 2, 0 if face % 2 == 0 else 3)
            pick[face * LANES + lane, field * 64 + place[0] * 16 + place[1] * 4 + place[2]] = 1.0
    return pick.astype(ml_dtypes.bfloat16)


def split(values):
    high = values.astype(BF16)
    low = (values - high.astype(F32)).astype(BF16)
    return high, low


def dot(a, b, dims):
    return lax.dot_general(a, b, dims, preferred_element_type=F32)


def dot_rows(a, b):
    return dot(jnp.concatenate([a[0], a[1], a[0]], 1), jnp.concatenate([b[0], b[0], b[1]], 1), NT)


def dot_columns(a, b):
    width = b[0].shape[1]
    both = dot(a[0], jnp.concatenate([b[0], b[1]], 1), NN)
    return both[:, :width] + (both[:, width:] + dot(a[1], b[0], NN))


def table_kernel(place, nbr_far, halo_far, table, nbr, halo, done):
    copies = [
        pltpu.make_async_copy(far, near, done.at[at])
        for at, (far, near) in enumerate([(nbr_far, nbr), (halo_far, halo)])
    ]
    for copy in copies:
        copy.start()
    for copy in copies:
        copy.wait()
    upper = place[1] >= SLABS // 2
    steps = jnp.where(upper, nbr[1:2, :], nbr[0:1, :])
    labels = jnp.where(upper, halo[0:1, :], halo[1:2, :])
    rows = [steps[:, :LANES], steps[:, LANES:], labels, labels, nbr[1:2, :LANES], nbr[1:2, LANES:], labels, labels]
    packed = jnp.concatenate(rows)
    for member in range(SLABS // 2):
        table[member] = packed


def order_kernel(nbr_far, halo_far, rhs_far, placed, order, spot, nbr, halo, rhs, done):
    copies = [
        pltpu.make_async_copy(far, near, done.at[at])
        for at, (far, near) in enumerate([(nbr_far, nbr), (halo_far, halo), (rhs_far, rhs)])
    ]
    for copy in copies:
        copy.start()
    copies[0].wait()
    copies[1].wait()

    def across(face, at):
        return nbr[face, at] & 255

    column = [halo[0, 0] & 255]
    for _ in range(15):
        column.append(across(5, column[-1]))
    rows = [column]
    for _ in range(7):
        rows.append([across(3, at) for at in rows[-1]])
    layers = [rows, [[across(1, at) for at in row] for row in rows]]
    for row in range(8):
        for sheet in range(16):
            spot[rows[row][sheet]] = row * 16 + sheet

    sub = lax.broadcasted_iota(jnp.int32, (8, LANES), 0)
    lane = lax.broadcasted_iota(jnp.int32, (8, LANES), 1)
    for sheet in range(16):
        for layer in range(2):
            at = jnp.zeros((8, LANES), jnp.int32)
            for row in range(8):
                at = jnp.where(sub == row, layers[layer][row][sheet], at)
            order[sheet * 2 + layer, :, :LANES] = jnp.where(lane == at, 1.0, 0.0).astype(F32)
            order[sheet * 2 + layer, :, LANES:] = jnp.where(lane + LANES == at, 1.0, 0.0).astype(F32)

    picks = order[...].reshape(SLAB, SLAB).astype(BF16)
    copies[2].wait()
    for step in range(2):
        high, low = split(rhs[step])
        values = dot(picks, high, NT) + dot(picks, low, NT)
        placed[step] = values.reshape(32, 8, NB)


def align_kernel(place, spot, placed, far, sent, shift, chain, tables, done):
    copies = [pltpu.make_async_copy(far, near, done.at[at]) for at, near in enumerate([chain, tables])]
    for copy in copies:
        copy.start()
    for copy in copies:
        copy.wait()
    group = lax.shift_right_logical(place[1], 2)
    member = place[1] & 3

    def step(slab, at):
        return chain[slab * 8 + lax.shift_right_logical(at, 7), at & 127]

    upper_rows = tables[28:30, :]
    index = lax.broadcasted_iota(jnp.int32, (2, LANES), 0) * LANES + lax.broadcasted_iota(jnp.int32, (2, LANES), 1)
    facing = jnp.sum(jnp.where(upper_rows == SLAB, index, 0)) & 255
    near = jnp.where(group == 0, facing, chain[2, 0] & 255)
    origin = near
    for hop in range(4):
        slab = jnp.where(group == 0, 3 - hop, hop)
        far_side = step(slab, near) & 255
        origin = jnp.where(slab == member, jnp.where(group == 0, far_side, near), origin)
        if hop < 3:
            label = step(slab, far_side) & 127
            ahead = jnp.where(group == 0, 2 - hop, hop + 1)
            near = chain[ahead * 8 + 2, label] & 255
    found = spot[origin] & 127
    first_row, first_sheet = lax.shift_right_logical(found, 4), found & 15
    shift[0] = (8 - first_row) & 7
    shift[1] = first_sheet
    for device in range(16):
        sheet = (SHEET_OF[device] + first_sheet) & 15
        for at in range(2):
            values = placed[at, pl.ds(sheet * 2, 2)]
            values = pltpu.roll(values, (8 - first_row) & 7, 1)
            sent[device, at * 16 : at * 16 + 16, :] = values.reshape(16, NB)


def first_weights(ref):
    return [ref.at[a:b] for a, b in [(0, 384), (384, 768), (768, 1536), (1536, 2304)]]


def second_weights(ref):
    return [ref.at[a:b] for a, b in [(0, 768), (768, 1536), (1536, 1920), (1920, 2304)]]


def face_order(place):
    core, slab = place[0] & 1, place[1] & 1
    return [1 - slab, slab, 4 + core, 5 - core, 2, 3]


def prepare_kernel(place, shift, placed_order, material, modes_in, modes_out, face_lift, rates, pick, *refs):
    order, first_set, factors, second_far, second_set, lift, sorted_pick, done = refs
    in_h, in_l, trace_h, trace_l = first_weights(first_set)
    lift_h, lift_l, out_h, out_l = second_weights(second_set)
    same_r, same_i, cross = factors.at[0], factors.at[1], factors.at[2]
    in_parts = split(modes_in[...])
    in_h[...], in_l[...] = in_parts
    out_parts = split(modes_out[...])
    out_h[...], out_l[...] = out_parts
    for at, face in enumerate(face_order(place)):
        sorted_pick[at * LANES : (at + 1) * LANES, :] = pick[pl.ds(pl.multiple_of(face * LANES, LANES), LANES), :]
    trace_h[...] = dot(sorted_pick[...], out_parts[0], NN).astype(BF16)
    trace_l[...] = dot(sorted_pick[...], out_parts[1], NN).astype(BF16)
    for device in range(16):
        sheet = (SHEET_OF[device] + shift[1]) & 15
        picks = pltpu.roll(placed_order[pl.ds(sheet * 2, 2)], shift[0], 1)
        order[device * 16 : device * 16 + 16, :] = picks.reshape(16, SLAB).astype(BF16)
    own_picks = order[pl.ds(pl.multiple_of(place[0] * 16, 16), 16), :].astype(F32)
    own = jnp.sum(own_picks * material[...], axis=1, keepdims=True)
    for freq in range(16):
        angle = 2.0 * math.pi / STEPS * freq
        rows = slice(freq * 16, freq * 16 + 16)
        real = (1.0 - DECAY * math.cos(angle)) * own + rates[...]
        imag = jnp.broadcast_to((DECAY * math.sin(angle) if freq else 0.0) * own, (16, NB))
        size = real * real + imag * imag
        same = real / size
        same_r[rows, :] = same
        same_i[rows, :] = same if freq else 1.0 / ((1.0 + DECAY) * own + rates[...])
        cross[rows, :] = imag / size
    lift[...] = jnp.zeros_like(lift)
    for at, face in enumerate(face_order(place)):
        lift[at * LANES : at * LANES + NFT, :] = face_lift[face]
    lift_h[...], lift_l[...] = split(dot_rows(split(lift[...]), in_parts))
    copy = pltpu.make_async_copy(second_set, second_far, done)
    copy.start()
    copy.wait()


def divided(modal, factors):
    real, imag = modal[:HALF], modal[HALF:]
    mixed = factors[2]
    return jnp.concatenate(
        [real * factors[0] + imag * mixed, imag * factors[1] - real * mixed]
    )


def pack(values):
    quarter = values.shape[0] // 4
    lane = lax.broadcasted_iota(jnp.int32, (quarter, LANES), 1)
    tail = values[3 * quarter :]
    parts = []
    for part in range(3):
        moved = pltpu.roll(tail, NFT - 32 * part, 1)
        parts.append(jnp.where(lane < NFT, values[part * quarter : (part + 1) * quarter], moved))
    return jnp.concatenate(parts)


def unpack(packed):
    quarter = packed.shape[0] // 3
    lane = lax.broadcasted_iota(jnp.int32, (quarter, LANES), 1)
    moved = [pltpu.roll(packed[part * quarter : (part + 1) * quarter], 32 + 32 * part, 1) for part in range(3)]
    tail = jnp.where(lane < 32, moved[0], jnp.where(lane < 64, moved[1], moved[2]))
    return jnp.concatenate([packed, tail])


def send_traces(place, solved, trace_h, trace_l, traces, solved_h, solved_l, inner, to_chip, to_next, to_even, to_odd):
    near = 1 - (place[1] & 1)
    solved_h[...], solved_l[...] = solved
    wide = 4 * LANES
    traces[...] = dot_rows(solved, (trace_h[:wide], trace_l[:wide])).reshape(STEPS, 2, 8, wide)
    to_chip[...] = pack(traces[:, :, :, 3 * LANES :].reshape(ROWS, LANES))
    to_next[...] = pack(traces[:, :, :, 2 * LANES : 3 * LANES].reshape(ROWS, LANES))
    to_even[...] = pack(traces[:, near, :, :LANES].reshape(HALF, LANES))
    to_odd[...] = pack(traces[:, 1 - near, :, LANES : 2 * LANES].reshape(HALF, LANES))
    inner[0] = traces[:, near, :, LANES : 2 * LANES].reshape(HALF, LANES)
    inner[1] = traces[:, 1 - near, :, :LANES].reshape(HALF, LANES)


def first_kernel(
    place, far, first_set, factors,
    modal, solved_h, solved_l, inner, to_chip, to_next, to_even, to_odd, steps, spectrum, traces, done,
):
    lanes = [slice(lane, lane + LANES) for lane in range(0, NB, LANES)]
    copies = [
        pltpu.make_async_copy(far.at[:, lane], steps.at[:, lane], done.at[at]) for at, lane in enumerate(lanes)
    ]
    for copy in copies:
        copy.start()
    in_h, in_l, trace_h, trace_l = first_weights(first_set)
    to_frequencies(steps, spectrum, copies)
    start = dot_rows(split(spectrum[...]), (in_h[...], in_l[...]))
    modal[...] = start
    solved = split(divided(start, factors))
    send_traces(
        place, solved, trace_h, trace_l, traces, solved_h, solved_l, inner, to_chip, to_next, to_even, to_odd
    )


def inside_kernel(modal, solved_h, solved_l, first_set, second_set, base):
    _, _, trace_h, trace_l = first_weights(first_set)
    lift_h, lift_l, _, _ = second_weights(second_set)
    wide = 4 * LANES
    traces = dot_rows((solved_h[...], solved_l[...]), (trace_h[wide:], trace_l[wide:]))
    traces = traces.reshape(ROWS // 8, 8, 2 * LANES)
    minus_y = pltpu.roll(traces[:, :, LANES:], 1, 1).reshape(ROWS, LANES)
    plus_y = pltpu.roll(traces[:, :, :LANES], 7, 1).reshape(ROWS, LANES)
    faces = split(jnp.concatenate([minus_y, plus_y], axis=1))
    base[...] = modal[...] - dot_columns(faces, (lift_h[wide:], lift_l[wide:]))


def meet_kernel(place, from_chip, from_next, from_even, base, inner, second_set, out, faces):
    near = 1 - (place[1] & 1)
    wide = 4 * LANES
    lift_h, lift_l, _, _ = second_weights(second_set)
    faces[:, near, :, :LANES] = unpack(from_even[...]).reshape(STEPS, 8, LANES)
    faces[:, 1 - near, :, :LANES] = inner[0].reshape(STEPS, 8, LANES)
    faces[:, near, :, LANES : 2 * LANES] = inner[1].reshape(STEPS, 8, LANES)
    faces[:, 1 - near, :, LANES : 2 * LANES] = jnp.zeros((STEPS, 8, LANES), F32)
    faces[:, :, :, 2 * LANES : 3 * LANES] = unpack(from_next[...]).reshape(STEPS, 2, 8, LANES)
    faces[:, :, :, 3 * LANES :] = unpack(from_chip[...]).reshape(STEPS, 2, 8, LANES)
    coupled = dot_columns(split(faces[...].reshape(ROWS, wide)), (lift_h[:wide], lift_l[:wide]))
    out[...] = (base[...] - coupled).reshape(STEPS, 2, 8, NB)


def corrected(place, from_odd, base, lift_h, lift_l, modes):
    near = 1 - (place[1] & 1)
    rows = slice(LANES, 2 * LANES)
    coupled = dot_columns(split(unpack(from_odd[...])), (lift_h[rows], lift_l[rows]))
    modes[:, near] = base[:, near]
    modes[:, 1 - near] = base[:, 1 - near] - coupled.reshape(STEPS, 8, NB)
    return modes[...].reshape(ROWS, NB)


def sweep_kernel(
    place, from_odd, base, first_set, second_set, factors,
    solved_h, solved_l, inner_out, to_chip, to_next, to_even, to_odd, modes, traces,
):
    _, _, trace_h, trace_l = first_weights(first_set)
    lift_h, lift_l, _, _ = second_weights(second_set)
    solved = split(divided(corrected(place, from_odd, base, lift_h, lift_l, modes), factors))
    send_traces(
        place, solved, trace_h, trace_l, traces, solved_h, solved_l, inner_out, to_chip, to_next, to_even, to_odd
    )


def last_kernel(place, from_odd, base, second_set, factors, steps, modes, spectrum):
    lift_h, lift_l, out_h, out_l = second_weights(second_set)
    solved = split(divided(corrected(place, from_odd, base, lift_h, lift_l, modes), factors))
    spectrum[...] = dot_rows(solved, (out_h[...], out_l[...]))
    to_steps(spectrum, steps)


def restore_kernel(arrived, order, far, out, done):
    copies = [pltpu.make_async_copy(out.at[step], far.at[step], done.at[step]) for step in range(2)]
    for step in range(2):
        values = arrived[:, step * 16 : step * 16 + 16, :].reshape(SLAB, NB)
        high, low = split(values)
        picks = order[...]
        out[step] = dot(high, picks, TN) + dot(low, picks, TN)
        copies[step].start()
    for copy in copies:
        copy.wait()


SMEM = pl.BlockSpec(memory_space=pltpu.SMEM)
VMEM = pl.BlockSpec(memory_space=pltpu.VMEM)
HBM = pl.BlockSpec(memory_space=pltpu.HBM)
KEPT = pl.BlockSpec(memory_space=pltpu.VMEM)
DMA = pltpu.SemaphoreType.DMA
HELD = ((HBM, pltpu.HBM), (KEPT, pltpu.VMEM))


def call(body, ins, outs, flops, scratch=(), megabytes=8):
    shapes = [jax.ShapeDtypeStruct(shape, kind) for shape, kind, _ in outs]
    moved = sum(a.size * a.dtype.itemsize for a in shapes + [a for a, _ in ins])
    for held, space in HELD:
        ins = [(pltpu.with_memory_space_constraint(a, space) if spec is held else a, spec) for a, spec in ins]
        shapes = [space(shape, kind) if spec is held else old for old, (shape, kind, spec) in zip(shapes, outs)]
    return pl.pallas_call(
        body,
        out_shape=shapes,
        in_specs=[spec for _, spec in ins],
        out_specs=[spec for _, _, spec in outs],
        scratch_shapes=list(scratch),
        compiler_params=pltpu.CompilerParams(vmem_limit_bytes=megabytes * 2**20),
        cost_estimate=pl.CostEstimate(flops=flops, bytes_accessed=moved, transcendentals=0),
    )(*[a for a, _ in ins])


def shards(rhs, material, modal_rates, modes_in, modes_out, face_lift, neighbours, halo_send):
    place = (jnp.stack([lax.axis_index("tm"), lax.axis_index("space")]).astype(jnp.int32), SMEM)
    (table,) = call(
        table_kernel,
        [place, (neighbours, HBM), (halo_send, HBM)],
        [((4, 8, LANES), jnp.int32, KEPT)],
        10**4,
        [pltpu.VMEM(neighbours.shape, jnp.int32), pltpu.VMEM(halo_send.shape, jnp.int32), DMA((2,))],
    )
    chain = lax.all_to_all(
        table, "space", 0, 0, tiled=True, axis_index_groups=[[0, 1, 2, 3], [4, 5, 6, 7]]
    ).reshape(32, LANES)
    placed, placed_order, spot = call(
        order_kernel,
        [(neighbours, HBM), (halo_send, HBM), (rhs, HBM)],
        [((2, 32, 8, NB), F32, KEPT), ((32, 8, SLAB), F32, KEPT), ((SLAB,), jnp.int32, SMEM)],
        2 * 4 * 256 * 256 * 384,
        [
            pltpu.SMEM(neighbours.shape, jnp.int32),
            pltpu.SMEM(halo_send.shape, jnp.int32),
            pltpu.VMEM(rhs.shape, F32),
            DMA((3,)),
        ],
    )
    sent, shift = call(
        align_kernel,
        [place, (spot, SMEM), (placed, KEPT), (chain, VMEM)],
        [((16, 32, NB), F32, KEPT), ((2,), jnp.int32, SMEM)],
        10**6,
        [pltpu.SMEM((32, LANES), jnp.int32), pltpu.VMEM((32, LANES), jnp.int32), DMA((2,))],
    )
    arrived = lax.all_to_all(sent, "tm", 0, 0, tiled=True).reshape(ROWS, NB)
    weights = [modes_in, modes_out, jnp.swapaxes(face_lift, 1, 2), modal_rates.reshape(1, NB), trace_rows()]
    prepared = [((SLAB, SLAB), BF16, KEPT), ((2304, NB), BF16, KEPT), ((3, HALF, NB), F32, KEPT), ((2304, NB), BF16, HBM)]
    order, first_set, factors, second_set = call(
        prepare_kernel,
        [place, (shift, SMEM), (placed_order, KEPT), (material.reshape(1, SLAB), VMEM)]
        + [(jnp.asarray(weight), VMEM) for weight in weights],
        prepared,
        2 * 5 * 384 * 384 * 768,
        [pltpu.VMEM((2304, NB), BF16), pltpu.VMEM((6 * LANES, NB), F32), pltpu.VMEM((6 * LANES, NB), BF16), DMA],
    )

    faces = (
        [((ROWS, NB), BF16, KEPT)] * 2
        + [((2, HALF, LANES), F32, KEPT)]
        + [((ROWS * 3 // 4, LANES), F32, VMEM)] * 2
        + [((HALF * 3 // 4, LANES), F32, VMEM)] * 2
    )
    face_scratch = pltpu.VMEM((STEPS, 2, 8, 4 * LANES), F32)

    def exchange(to_chip, to_next, to_even, to_odd):
        from_odd = lax.ppermute(to_odd, "space", ODD_SIDES)
        from_even = lax.ppermute(to_even, "space", EVEN_SIDES)
        from_next = lax.ppermute(to_next, "tm", NEXT_CHIP)
        from_chip = lax.ppermute(to_chip, "tm", SAME_CHIP)
        return from_chip, from_next, from_even, from_odd

    def inside(solved_h, solved_l, inner, from_chip, from_next, from_even):
        (base,) = call(
            inside_kernel,
            [(a, KEPT) for a in (modal, solved_h, solved_l, first_set)] + [(second_set, VMEM)],
            [((ROWS, NB), F32, KEPT)],
            2 * 3 * 512 * 384 * 512,
        )
        (base,) = call(
            meet_kernel,
            [place]
            + [(a, VMEM) for a in (from_chip, from_next, from_even)]
            + [(base, KEPT), (inner, KEPT), (second_set, VMEM)],
            [((STEPS, 2, 8, NB), F32, KEPT)],
            2 * 3 * 512 * 384 * 512,
            [face_scratch],
        )
        return (base, KEPT)

    modal, solved_h, solved_l, inner, *outgoing = call(
        first_kernel,
        [place, (arrived, HBM), (first_set, KEPT), (factors, KEPT)],
        [((ROWS, NB), F32, KEPT)] + faces,
        2 * 3 * 512 * 384 * (384 + 512),
        [pltpu.VMEM((ROWS, NB), F32)] * 2 + [face_scratch, DMA((3,))],
    )
    *incoming, from_odd = exchange(*outgoing)
    base = inside(solved_h, solved_l, inner, *incoming)
    solved_h, solved_l, inner, *outgoing = call(
        sweep_kernel,
        [place, (from_odd, VMEM), base, (first_set, KEPT), (second_set, VMEM), (factors, KEPT)],
        faces,
        2 * 3 * 512 * 384 * 512,
        [pltpu.VMEM((STEPS, 2, 8, NB), F32), face_scratch],
    )
    *incoming, from_odd = exchange(*outgoing)
    base = inside(solved_h, solved_l, inner, *incoming)
    (steps,) = call(
        last_kernel,
        [place, (from_odd, VMEM), base, (second_set, VMEM), (factors, KEPT)],
        [((ROWS, NB), F32, VMEM)],
        2 * 3 * 512 * 384 * 384,
        [pltpu.VMEM((STEPS, 2, 8, NB), F32), pltpu.VMEM((ROWS, NB), F32)],
    )
    back = lax.all_to_all(steps.reshape(16, 32, NB), "tm", 0, 0, tiled=True)
    (out,) = call(
        restore_kernel,
        [(back, VMEM), (order, KEPT)],
        [((2, NB, SLAB), F32, HBM)],
        2 * 4 * 256 * 256 * 384,
        [pltpu.VMEM((2, NB, SLAB), F32), DMA((2,))],
    )
    return out


def solution(mesh):
    return jax.shard_map(
        shards,
        mesh=mesh,
        in_specs=(
            P("tm", None, "space"),
            P("space"),
            P(),
            P(),
            P(),
            P(),
            P(None, "space"),
            P(None, "space"),
        ),
        out_specs=P("tm", None, "space"),
        check_vma=False,
    )
```

```python
import math

import jax
import jax.numpy as jnp
import ml_dtypes
import numpy as np
from jax import lax
from jax.experimental import pallas as pl
from jax.experimental.pallas import tpu as pltpu
from jax.sharding import PartitionSpec as P

NB = 384
NFT = 96
LANES = 128
STEPS = 32
SLAB = 256
SHEET = 16
ROWS = STEPS * SHEET
HALF = ROWS // 2
SLABS = 8
DECAY = 0.1 ** (1.0 / STEPS)

RING = (0, 1, 4, 5, 8, 9, 12, 13, 14, 15, 10, 11, 6, 7, 2, 3)
SHEET_OF = tuple(RING.index(device) for device in range(16))
SAME_CHIP = [(i, i ^ 1) for i in range(16)]
NEXT_CHIP = [(RING[2 * i + 1], RING[(2 * i + 2) % 16]) for i in range(8)]
NEXT_CHIP = NEXT_CHIP + [(b, a) for a, b in NEXT_CHIP]
EVEN_SIDES = [(i, i ^ 1) for i in range(8)]
ODD_SIDES = [(1, 2), (2, 1), (3, 4), (4, 3), (5, 6), (6, 5)]

F32 = jnp.float32
BF16 = jnp.bfloat16
NN = (((1,), (0,)), ((), ()))
NT = (((1,), (1,)), ((), ()))
TN = (((0,), (0,)), ((), ()))


def real_fft(steps):
    count = len(steps)
    if count == 2:
        return [(steps[0] + steps[1], None), (steps[0] - steps[1], None)]
    even, odd = real_fft(steps[0::2]), real_fft(steps[1::2])
    out = [None] * (count // 2 + 1)
    out[0] = (even[0][0] + odd[0][0], None)
    out[count // 2] = (even[0][0] - odd[0][0], None)
    out[count // 4] = (even[count // 4][0], -odd[count // 4][0])
    for freq in range(1, count // 4):
        cos, sin = math.cos(2.0 * math.pi * freq / count), math.sin(2.0 * math.pi * freq / count)
        real, imag = odd[freq]
        turned_real, turned_imag = real * cos + imag * sin, imag * cos - real * sin
        real, imag = even[freq]
        out[freq] = (real + turned_real, imag + turned_imag)
        out[count // 2 - freq] = (real - turned_real, turned_imag - imag)
    return out


def real_ifft(freqs):
    count = 2 * (len(freqs) - 1)
    first, last = freqs[0][0], freqs[-1][0]
    if count == 2:
        return [first + last, first - last]
    even, odd = [None] * (count // 4 + 1), [None] * (count // 4 + 1)
    even[0], odd[0] = (first + last, None), (first - last, None)
    middle = freqs[count // 4]
    even[-1], odd[-1] = (2.0 * middle[0], None), (-2.0 * middle[1], None)
    for freq in range(1, count // 4):
        cos, sin = math.cos(2.0 * math.pi * freq / count), math.sin(2.0 * math.pi * freq / count)
        (real, imag), (other_real, other_imag) = freqs[freq], freqs[count // 2 - freq]
        even[freq] = (real + other_real, imag - other_imag)
        real, imag = real - other_real, imag + other_imag
        odd[freq] = (real * cos - imag * sin, imag * cos + real * sin)
    out = [None] * count
    out[0::2], out[1::2] = real_ifft(even), real_ifft(odd)
    return out


def tiles():
    for lane in range(0, NB, LANES):
        for block in range(SHEET // 8):
            yield lambda row: (slice(row * SHEET + block * 8, row * SHEET + block * 8 + 8), slice(lane, lane + LANES))


def to_frequencies(steps, spectrum):
    for at in tiles():
        freqs = real_fft([steps[at(n)] * DECAY**n for n in range(STEPS)])
        for freq in range(16):
            spectrum[at(freq)] = freqs[freq][0]
            spectrum[at(16 + freq)] = freqs[freq][1] if freq else freqs[16][0]


def to_steps(spectrum, steps):
    for at in tiles():
        pairs = [(spectrum[at(freq)], spectrum[at(16 + freq)]) for freq in range(16)]
        freqs = [(pairs[0][0], None)] + pairs[1:] + [(pairs[0][1], None)]
        for n, value in enumerate(real_ifft(freqs)):
            steps[at(n)] = value * (DECAY**-n / STEPS)


def trace_rows():
    pick = np.zeros((6 * LANES, NB), np.float32)
    for face in range(6):
        for lane in range(NFT):
            field, first, second = lane // 16, lane // 4 % 4, lane % 4
            place = [first, second]
            place.insert(face // 2, 0 if face % 2 == 0 else 3)
            pick[face * LANES + lane, field * 64 + place[0] * 16 + place[1] * 4 + place[2]] = 1.0
    return pick.astype(ml_dtypes.bfloat16)


def split(values):
    high = values.astype(BF16)
    low = (values - high.astype(F32)).astype(BF16)
    return high, low


def dot(a, b, dims):
    return lax.dot_general(a, b, dims, preferred_element_type=F32)


def dot_rows(a, b):
    return dot(jnp.concatenate([a[0], a[1], a[0]], 1), jnp.concatenate([b[0], b[0], b[1]], 1), NT)


def dot_columns(a, b):
    width = b[0].shape[1]
    both = dot(a[0], jnp.concatenate([b[0], b[1]], 1), NN)
    return both[:, :width] + (both[:, width:] + dot(a[1], b[0], NN))


def table_kernel(place, nbr_far, halo_far, table, nbr, halo, done):
    copies = [
        pltpu.make_async_copy(far, near, done.at[at])
        for at, (far, near) in enumerate([(nbr_far, nbr), (halo_far, halo)])
    ]
    for copy in copies:
        copy.start()
    for copy in copies:
        copy.wait()
    upper = place[1] >= SLABS // 2
    steps = jnp.where(upper, nbr[1:2, :], nbr[0:1, :])
    labels = jnp.where(upper, halo[0:1, :], halo[1:2, :])
    rows = [steps[:, :LANES], steps[:, LANES:], labels, labels, nbr[1:2, :LANES], nbr[1:2, LANES:], labels, labels]
    packed = jnp.concatenate(rows)
    for member in range(SLABS // 2):
        table[member] = packed


def order_kernel(nbr_far, halo_far, rhs_far, placed, order, spot, nbr, halo, rhs, done):
    copies = [
        pltpu.make_async_copy(far, near, done.at[at])
        for at, (far, near) in enumerate([(nbr_far, nbr), (halo_far, halo), (rhs_far, rhs)])
    ]
    for copy in copies:
        copy.start()
    copies[0].wait()
    copies[1].wait()

    def across(face, at):
        return nbr[face, at] & 255

    column = [halo[0, 0] & 255]
    for _ in range(15):
        column.append(across(5, column[-1]))
    rows = [column]
    for _ in range(7):
        rows.append([across(3, at) for at in rows[-1]])
    layers = [rows, [[across(1, at) for at in row] for row in rows]]
    for row in range(8):
        for sheet in range(16):
            spot[rows[row][sheet]] = row * 16 + sheet

    sub = lax.broadcasted_iota(jnp.int32, (8, LANES), 0)
    lane = lax.broadcasted_iota(jnp.int32, (8, LANES), 1)
    for sheet in range(16):
        for layer in range(2):
            at = jnp.zeros((8, LANES), jnp.int32)
            for row in range(8):
                at = jnp.where(sub == row, layers[layer][row][sheet], at)
            order[sheet * 2 + layer, :, :LANES] = jnp.where(lane == at, 1.0, 0.0).astype(F32)
            order[sheet * 2 + layer, :, LANES:] = jnp.where(lane + LANES == at, 1.0, 0.0).astype(F32)

    picks = order[...].reshape(SLAB, SLAB).astype(BF16)
    copies[2].wait()
    for step in range(2):
        high, low = split(rhs[step])
        values = dot(picks, high, NT) + dot(picks, low, NT)
        placed[step] = values.reshape(32, 8, NB)


def align_kernel(place, spot, placed, far, sent, shift, chain, tables, done):
    copies = [pltpu.make_async_copy(far, near, done.at[at]) for at, near in enumerate([chain, tables])]
    for copy in copies:
        copy.start()
    for copy in copies:
        copy.wait()
    group = lax.shift_right_logical(place[1], 2)
    member = place[1] & 3

    def step(slab, at):
        return chain[slab * 8 + lax.shift_right_logical(at, 7), at & 127]

    upper_rows = tables[28:30, :]
    index = lax.broadcasted_iota(jnp.int32, (2, LANES), 0) * LANES + lax.broadcasted_iota(jnp.int32, (2, LANES), 1)
    facing = jnp.sum(jnp.where(upper_rows == SLAB, index, 0)) & 255
    near = jnp.where(group == 0, facing, chain[2, 0] & 255)
    origin = near
    for hop in range(4):
        slab = jnp.where(group == 0, 3 - hop, hop)
        far_side = step(slab, near) & 255
        origin = jnp.where(slab == member, jnp.where(group == 0, far_side, near), origin)
        if hop < 3:
            label = step(slab, far_side) & 127
            ahead = jnp.where(group == 0, 2 - hop, hop + 1)
            near = chain[ahead * 8 + 2, label] & 255
    found = spot[origin] & 127
    first_row, first_sheet = lax.shift_right_logical(found, 4), found & 15
    shift[0] = (8 - first_row) & 7
    shift[1] = first_sheet
    for device in range(16):
        sheet = (SHEET_OF[device] + first_sheet) & 15
        for at in range(2):
            values = placed[at, pl.ds(sheet * 2, 2)]
            values = pltpu.roll(values, (8 - first_row) & 7, 1)
            sent[device, at * 16 : at * 16 + 16, :] = values.reshape(16, NB)


def first_weights(ref):
    return [ref.at[a:b] for a, b in [(0, 384), (384, 768), (768, 1536), (1536, 2304)]]


def second_weights(ref):
    return [ref.at[a:b] for a, b in [(0, 768), (768, 1536), (1536, 1920), (1920, 2304)]]


def face_order(place):
    core, slab = place[0] & 1, place[1] & 1
    return [1 - slab, slab, 4 + core, 5 - core, 2, 3]


def prepare_kernel(place, shift, placed_order, material, modes_in, modes_out, face_lift, rates, pick, *refs):
    order, first_set, factors_far, second_far, second_set, factors, lift, sorted_pick, done = refs
    in_h, in_l, trace_h, trace_l = first_weights(first_set)
    lift_h, lift_l, out_h, out_l = second_weights(second_set)
    same_r, same_i, cross = factors.at[0], factors.at[1], factors.at[2]
    in_parts = split(modes_in[...])
    in_h[...], in_l[...] = in_parts
    out_parts = split(modes_out[...])
    out_h[...], out_l[...] = out_parts
    for at, face in enumerate(face_order(place)):
        sorted_pick[at * LANES : (at + 1) * LANES, :] = pick[pl.ds(pl.multiple_of(face * LANES, LANES), LANES), :]
    trace_h[...] = dot(sorted_pick[...], out_parts[0], NN).astype(BF16)
    trace_l[...] = dot(sorted_pick[...], out_parts[1], NN).astype(BF16)
    for device in range(16):
        sheet = (SHEET_OF[device] + shift[1]) & 15
        picks = pltpu.roll(placed_order[pl.ds(sheet * 2, 2)], shift[0], 1)
        order[device * 16 : device * 16 + 16, :] = picks.reshape(16, SLAB).astype(BF16)
    own_picks = order[pl.ds(pl.multiple_of(place[0] * 16, 16), 16), :].astype(F32)
    own = jnp.sum(own_picks * material[...], axis=1, keepdims=True)
    for freq in range(16):
        angle = 2.0 * math.pi / STEPS * freq
        rows = slice(freq * 16, freq * 16 + 16)
        real = (1.0 - DECAY * math.cos(angle)) * own + rates[...]
        imag = jnp.broadcast_to((DECAY * math.sin(angle) if freq else 0.0) * own, (16, NB))
        size = real * real + imag * imag
        same = real / size
        same_r[rows, :] = same
        same_i[rows, :] = same if freq else 1.0 / ((1.0 + DECAY) * own + rates[...])
        cross[rows, :] = imag / size
    factors_copy = pltpu.make_async_copy(factors, factors_far, done.at[0])
    factors_copy.start()
    lift[...] = jnp.zeros_like(lift)
    for at, face in enumerate(face_order(place)):
        lift[at * LANES : at * LANES + NFT, :] = face_lift[face]
    lift_h[...], lift_l[...] = split(dot_rows(split(lift[...]), in_parts))
    copy = pltpu.make_async_copy(second_set, second_far, done.at[1])
    copy.start()
    copy.wait()
    factors_copy.wait()


def divided(modal, factors):
    real, imag = modal[:HALF], modal[HALF:]
    mixed = factors[2]
    return jnp.concatenate(
        [real * factors[0] + imag * mixed, imag * factors[1] - real * mixed]
    )


def pack(values):
    quarter = values.shape[0] // 4
    lane = lax.broadcasted_iota(jnp.int32, (quarter, LANES), 1)
    tail = values[3 * quarter :]
    parts = []
    for part in range(3):
        moved = pltpu.roll(tail, NFT - 32 * part, 1)
        parts.append(jnp.where(lane < NFT, values[part * quarter : (part + 1) * quarter], moved))
    return jnp.concatenate(parts)


def unpack(packed):
    quarter = packed.shape[0] // 3
    lane = lax.broadcasted_iota(jnp.int32, (quarter, LANES), 1)
    moved = [pltpu.roll(packed[part * quarter : (part + 1) * quarter], 32 + 32 * part, 1) for part in range(3)]
    tail = jnp.where(lane < 32, moved[0], jnp.where(lane < 64, moved[1], moved[2]))
    return jnp.concatenate([packed, tail])


def send_traces(place, solved, trace_h, trace_l, traces, solved_h, solved_l, inner, to_chip, to_next, to_even, to_odd):
    near = 1 - (place[1] & 1)
    solved_h[...], solved_l[...] = solved
    wide = 4 * LANES
    traces[...] = dot_rows(solved, (trace_h[:wide], trace_l[:wide])).reshape(STEPS, 2, 8, wide)
    to_chip[...] = pack(traces[:, :, :, 3 * LANES :].reshape(ROWS, LANES))
    to_next[...] = pack(traces[:, :, :, 2 * LANES : 3 * LANES].reshape(ROWS, LANES))
    to_even[...] = pack(traces[:, near, :, :LANES].reshape(HALF, LANES))
    to_odd[...] = pack(traces[:, 1 - near, :, LANES : 2 * LANES].reshape(HALF, LANES))
    inner[0] = traces[:, near, :, LANES : 2 * LANES].reshape(HALF, LANES)
    inner[1] = traces[:, 1 - near, :, :LANES].reshape(HALF, LANES)


def first_kernel(
    place, steps, first_set, factors_far,
    modal, solved_h, solved_l, inner, to_chip, to_next, to_even, to_odd, spectrum, traces, factors, done,
):
    factors_copy = pltpu.make_async_copy(factors_far, factors, done)
    factors_copy.start()
    in_h, in_l, trace_h, trace_l = first_weights(first_set)
    to_frequencies(steps, spectrum)
    start = dot_rows(split(spectrum[...]), (in_h[...], in_l[...]))
    modal[...] = start
    factors_copy.wait()
    solved = split(divided(start, factors))
    send_traces(
        place, solved, trace_h, trace_l, traces, solved_h, solved_l, inner, to_chip, to_next, to_even, to_odd
    )


def inside_kernel(modal, solved_h, solved_l, first_set, second_set, base):
    _, _, trace_h, trace_l = first_weights(first_set)
    lift_h, lift_l, _, _ = second_weights(second_set)
    wide = 4 * LANES
    traces = dot_rows((solved_h[...], solved_l[...]), (trace_h[wide:], trace_l[wide:]))
    traces = traces.reshape(ROWS // 8, 8, 2 * LANES)
    minus_y = pltpu.roll(traces[:, :, LANES:], 1, 1).reshape(ROWS, LANES)
    plus_y = pltpu.roll(traces[:, :, :LANES], 7, 1).reshape(ROWS, LANES)
    faces = split(jnp.concatenate([minus_y, plus_y], axis=1))
    base[...] = modal[...] - dot_columns(faces, (lift_h[wide:], lift_l[wide:]))


def meet_kernel(place, from_chip, from_next, from_even, base, inner, second_set, out, faces):
    near = 1 - (place[1] & 1)
    wide = 4 * LANES
    lift_h, lift_l, _, _ = second_weights(second_set)
    faces[:, near, :, :LANES] = unpack(from_even[...]).reshape(STEPS, 8, LANES)
    faces[:, 1 - near, :, :LANES] = inner[0].reshape(STEPS, 8, LANES)
    faces[:, near, :, LANES : 2 * LANES] = inner[1].reshape(STEPS, 8, LANES)
    faces[:, 1 - near, :, LANES : 2 * LANES] = jnp.zeros((STEPS, 8, LANES), F32)
    faces[:, :, :, 2 * LANES : 3 * LANES] = unpack(from_next[...]).reshape(STEPS, 2, 8, LANES)
    faces[:, :, :, 3 * LANES :] = unpack(from_chip[...]).reshape(STEPS, 2, 8, LANES)
    coupled = dot_columns(split(faces[...].reshape(ROWS, wide)), (lift_h[:wide], lift_l[:wide]))
    out[...] = (base[...] - coupled).reshape(STEPS, 2, 8, NB)


def corrected(place, from_odd, base, lift_h, lift_l, modes):
    near = 1 - (place[1] & 1)
    rows = slice(LANES, 2 * LANES)
    coupled = dot_columns(split(unpack(from_odd[...])), (lift_h[rows], lift_l[rows]))
    modes[:, near] = base[:, near]
    modes[:, 1 - near] = base[:, 1 - near] - coupled.reshape(STEPS, 8, NB)
    return modes[...].reshape(ROWS, NB)


def sweep_kernel(
    place, from_odd, base, first_set, second_set, factors,
    solved_h, solved_l, inner_out, to_chip, to_next, to_even, to_odd, modes, traces,
):
    _, _, trace_h, trace_l = first_weights(first_set)
    lift_h, lift_l, _, _ = second_weights(second_set)
    solved = split(divided(corrected(place, from_odd, base, lift_h, lift_l, modes), factors))
    send_traces(
        place, solved, trace_h, trace_l, traces, solved_h, solved_l, inner_out, to_chip, to_next, to_even, to_odd
    )


def last_kernel(place, from_odd, base, second_set, factors, steps, modes, spectrum):
    lift_h, lift_l, out_h, out_l = second_weights(second_set)
    solved = split(divided(corrected(place, from_odd, base, lift_h, lift_l, modes), factors))
    spectrum[...] = dot_rows(solved, (out_h[...], out_l[...]))
    to_steps(spectrum, steps)


def restore_kernel(arrived, order, far, out, done):
    copies = [pltpu.make_async_copy(out.at[step], far.at[step], done.at[step]) for step in range(2)]
    for step in range(2):
        values = arrived[:, step * 16 : step * 16 + 16, :].reshape(SLAB, NB)
        high, low = split(values)
        picks = order[...]
        out[step] = dot(high, picks, TN) + dot(low, picks, TN)
        copies[step].start()
    for copy in copies:
        copy.wait()


SMEM = pl.BlockSpec(memory_space=pltpu.SMEM)
VMEM = pl.BlockSpec(memory_space=pltpu.VMEM)
HBM = pl.BlockSpec(memory_space=pltpu.HBM)
KEPT = pl.BlockSpec(memory_space=pltpu.VMEM)
DMA = pltpu.SemaphoreType.DMA
HELD = ((HBM, pltpu.HBM), (KEPT, pltpu.VMEM))


def call(body, ins, outs, flops, scratch=(), megabytes=8):
    shapes = [jax.ShapeDtypeStruct(shape, kind) for shape, kind, _ in outs]
    moved = sum(a.size * a.dtype.itemsize for a in shapes + [a for a, _ in ins])
    for held, space in HELD:
        ins = [(pltpu.with_memory_space_constraint(a, space) if spec is held else a, spec) for a, spec in ins]
        shapes = [space(shape, kind) if spec is held else old for old, (shape, kind, spec) in zip(shapes, outs)]
    return pl.pallas_call(
        body,
        out_shape=shapes,
        in_specs=[spec for _, spec in ins],
        out_specs=[spec for _, _, spec in outs],
        scratch_shapes=list(scratch),
        compiler_params=pltpu.CompilerParams(vmem_limit_bytes=megabytes * 2**20),
        cost_estimate=pl.CostEstimate(flops=flops, bytes_accessed=moved, transcendentals=0),
    )(*[a for a, _ in ins])


def shards(rhs, material, modal_rates, modes_in, modes_out, face_lift, neighbours, halo_send):
    place = (jnp.stack([lax.axis_index("tm"), lax.axis_index("space")]).astype(jnp.int32), SMEM)
    (table,) = call(
        table_kernel,
        [place, (neighbours, HBM), (halo_send, HBM)],
        [((4, 8, LANES), jnp.int32, KEPT)],
        10**4,
        [pltpu.VMEM(neighbours.shape, jnp.int32), pltpu.VMEM(halo_send.shape, jnp.int32), DMA((2,))],
    )
    chain = lax.all_to_all(
        table, "space", 0, 0, tiled=True, axis_index_groups=[[0, 1, 2, 3], [4, 5, 6, 7]]
    ).reshape(32, LANES)
    placed, placed_order, spot = call(
        order_kernel,
        [(neighbours, HBM), (halo_send, HBM), (rhs, HBM)],
        [((2, 32, 8, NB), F32, KEPT), ((32, 8, SLAB), F32, KEPT), ((SLAB,), jnp.int32, SMEM)],
        2 * 4 * 256 * 256 * 384,
        [
            pltpu.SMEM(neighbours.shape, jnp.int32),
            pltpu.SMEM(halo_send.shape, jnp.int32),
            pltpu.VMEM(rhs.shape, F32),
            DMA((3,)),
        ],
    )
    sent, shift = call(
        align_kernel,
        [place, (spot, SMEM), (placed, KEPT), (chain, VMEM)],
        [((16, 32, NB), F32, KEPT), ((2,), jnp.int32, SMEM)],
        10**6,
        [pltpu.SMEM((32, LANES), jnp.int32), pltpu.VMEM((32, LANES), jnp.int32), DMA((2,))],
    )
    arrived = lax.all_to_all(sent, "tm", 0, 0, tiled=True).reshape(ROWS, NB)
    weights = [modes_in, modes_out, jnp.swapaxes(face_lift, 1, 2), modal_rates.reshape(1, NB), trace_rows()]
    prepared = [((SLAB, SLAB), BF16, KEPT), ((2304, NB), BF16, KEPT), ((3, HALF, NB), F32, HBM), ((2304, NB), BF16, HBM)]
    order, first_set, factors, second_set = call(
        prepare_kernel,
        [place, (shift, SMEM), (placed_order, KEPT), (material.reshape(1, SLAB), VMEM)]
        + [(jnp.asarray(weight), VMEM) for weight in weights],
        prepared,
        2 * 5 * 384 * 384 * 768,
        [pltpu.VMEM((2304, NB), BF16), pltpu.VMEM((3, HALF, NB), F32), pltpu.VMEM((6 * LANES, NB), F32), pltpu.VMEM((6 * LANES, NB), BF16), DMA((2,))],
    )

    faces = (
        [((ROWS, NB), BF16, KEPT)] * 2
        + [((2, HALF, LANES), F32, KEPT)]
        + [((ROWS * 3 // 4, LANES), F32, VMEM)] * 2
        + [((HALF * 3 // 4, LANES), F32, VMEM)] * 2
    )
    face_scratch = pltpu.VMEM((STEPS, 2, 8, 4 * LANES), F32)

    def exchange(to_chip, to_next, to_even, to_odd):
        from_odd = lax.ppermute(to_odd, "space", ODD_SIDES)
        from_even = lax.ppermute(to_even, "space", EVEN_SIDES)
        from_next = lax.ppermute(to_next, "tm", NEXT_CHIP)
        from_chip = lax.ppermute(to_chip, "tm", SAME_CHIP)
        return from_chip, from_next, from_even, from_odd

    def inside(solved_h, solved_l, inner, from_chip, from_next, from_even):
        (base,) = call(
            inside_kernel,
            [(a, KEPT) for a in (modal, solved_h, solved_l, first_set)] + [(second_set, VMEM)],
            [((ROWS, NB), F32, KEPT)],
            2 * 3 * 512 * 384 * 512,
        )
        (base,) = call(
            meet_kernel,
            [place]
            + [(a, VMEM) for a in (from_chip, from_next, from_even)]
            + [(base, KEPT), (inner, KEPT), (second_set, VMEM)],
            [((STEPS, 2, 8, NB), F32, KEPT)],
            2 * 3 * 512 * 384 * 512,
            [face_scratch],
        )
        return (base, KEPT)

    modal, solved_h, solved_l, inner, *outgoing = call(
        first_kernel,
        [place, (arrived, VMEM), (first_set, KEPT), (factors, HBM)],
        [((ROWS, NB), F32, KEPT)] + faces,
        2 * 3 * 512 * 384 * (384 + 512),
        [pltpu.VMEM((ROWS, NB), F32), face_scratch, pltpu.VMEM((3, HALF, NB), F32), DMA],
    )
    *incoming, from_odd = exchange(*outgoing)
    base = inside(solved_h, solved_l, inner, *incoming)
    solved_h, solved_l, inner, *outgoing = call(
        sweep_kernel,
        [place, (from_odd, VMEM), base, (first_set, KEPT), (second_set, VMEM), (factors, VMEM)],
        faces,
        2 * 3 * 512 * 384 * 512,
        [pltpu.VMEM((STEPS, 2, 8, NB), F32), face_scratch],
    )
    *incoming, from_odd = exchange(*outgoing)
    base = inside(solved_h, solved_l, inner, *incoming)
    (steps,) = call(
        last_kernel,
        [place, (from_odd, VMEM), base, (second_set, VMEM), (factors, VMEM)],
        [((ROWS, NB), F32, VMEM)],
        2 * 3 * 512 * 384 * 384,
        [pltpu.VMEM((STEPS, 2, 8, NB), F32), pltpu.VMEM((ROWS, NB), F32)],
    )
    back = lax.all_to_all(steps.reshape(16, 32, NB), "tm", 0, 0, tiled=True)
    (out,) = call(
        restore_kernel,
        [(back, VMEM), (order, KEPT)],
        [((2, NB, SLAB), F32, HBM)],
        2 * 4 * 256 * 256 * 384,
        [pltpu.VMEM((2, NB, SLAB), F32), DMA((2,))],
    )
    return out


def solution(mesh):
    return jax.shard_map(
        shards,
        mesh=mesh,
        in_specs=(
            P("tm", None, "space"),
            P("space"),
            P(),
            P(),
            P(),
            P(),
            P(None, "space"),
            P(None, "space"),
        ),
        out_specs=P("tm", None, "space"),
        check_vma=False,
    )
```

```python
import math

import jax
import jax.numpy as jnp
import ml_dtypes
import numpy as np
from jax import lax
from jax.experimental import pallas as pl
from jax.experimental.pallas import tpu as pltpu
from jax.sharding import PartitionSpec as P

NB = 384
NFT = 96
LANES = 128
STEPS = 32
SLAB = 256
SHEET = 16
ROWS = STEPS * SHEET
HALF = ROWS // 2
SLABS = 8
DECAY = 0.1 ** (1.0 / STEPS)

RING = (0, 1, 4, 5, 8, 9, 12, 13, 14, 15, 10, 11, 6, 7, 2, 3)
SHEET_OF = tuple(RING.index(device) for device in range(16))
SAME_CHIP = [(i, i ^ 1) for i in range(16)]
NEXT_CHIP = [(RING[2 * i + 1], RING[(2 * i + 2) % 16]) for i in range(8)]
NEXT_CHIP = NEXT_CHIP + [(b, a) for a, b in NEXT_CHIP]
EVEN_SIDES = [(i, i ^ 1) for i in range(8)]
ODD_SIDES = [(1, 2), (2, 1), (3, 4), (4, 3), (5, 6), (6, 5)]

F32 = jnp.float32
BF16 = jnp.bfloat16
NN = (((1,), (0,)), ((), ()))
NT = (((1,), (1,)), ((), ()))
TN = (((0,), (0,)), ((), ()))


def real_fft(steps):
    count = len(steps)
    if count == 2:
        return [(steps[0] + steps[1], None), (steps[0] - steps[1], None)]
    even, odd = real_fft(steps[0::2]), real_fft(steps[1::2])
    out = [None] * (count // 2 + 1)
    out[0] = (even[0][0] + odd[0][0], None)
    out[count // 2] = (even[0][0] - odd[0][0], None)
    out[count // 4] = (even[count // 4][0], -odd[count // 4][0])
    for freq in range(1, count // 4):
        cos, sin = math.cos(2.0 * math.pi * freq / count), math.sin(2.0 * math.pi * freq / count)
        real, imag = odd[freq]
        turned_real, turned_imag = real * cos + imag * sin, imag * cos - real * sin
        real, imag = even[freq]
        out[freq] = (real + turned_real, imag + turned_imag)
        out[count // 2 - freq] = (real - turned_real, turned_imag - imag)
    return out


def real_ifft(freqs):
    count = 2 * (len(freqs) - 1)
    first, last = freqs[0][0], freqs[-1][0]
    if count == 2:
        return [first + last, first - last]
    even, odd = [None] * (count // 4 + 1), [None] * (count // 4 + 1)
    even[0], odd[0] = (first + last, None), (first - last, None)
    middle = freqs[count // 4]
    even[-1], odd[-1] = (2.0 * middle[0], None), (-2.0 * middle[1], None)
    for freq in range(1, count // 4):
        cos, sin = math.cos(2.0 * math.pi * freq / count), math.sin(2.0 * math.pi * freq / count)
        (real, imag), (other_real, other_imag) = freqs[freq], freqs[count // 2 - freq]
        even[freq] = (real + other_real, imag - other_imag)
        real, imag = real - other_real, imag + other_imag
        odd[freq] = (real * cos - imag * sin, imag * cos + real * sin)
    out = [None] * count
    out[0::2], out[1::2] = real_ifft(even), real_ifft(odd)
    return out


def tiles():
    for lane in range(0, NB, LANES):
        for block in range(SHEET // 8):
            yield lambda row: (slice(row * SHEET + block * 8, row * SHEET + block * 8 + 8), slice(lane, lane + LANES))


def to_frequencies(steps, spectrum):
    for at in tiles():
        freqs = real_fft([steps[at(n)] * DECAY**n for n in range(STEPS)])
        for freq in range(16):
            spectrum[at(freq)] = freqs[freq][0]
            spectrum[at(16 + freq)] = freqs[freq][1] if freq else freqs[16][0]


def to_steps(spectrum, steps):
    for at in tiles():
        pairs = [(spectrum[at(freq)], spectrum[at(16 + freq)]) for freq in range(16)]
        freqs = [(pairs[0][0], None)] + pairs[1:] + [(pairs[0][1], None)]
        for n, value in enumerate(real_ifft(freqs)):
            steps[at(n)] = value * (DECAY**-n / STEPS)


def trace_rows():
    pick = np.zeros((6 * LANES, NB), np.float32)
    for face in range(6):
        for lane in range(NFT):
            field, first, second = lane // 16, lane // 4 % 4, lane % 4
            place = [first, second]
            place.insert(face // 2, 0 if face % 2 == 0 else 3)
            pick[face * LANES + lane, field * 64 + place[0] * 16 + place[1] * 4 + place[2]] = 1.0
    return pick.astype(ml_dtypes.bfloat16)


def split(values):
    high = values.astype(BF16)
    low = (values - high.astype(F32)).astype(BF16)
    return high, low


def dot(a, b, dims):
    return lax.dot_general(a, b, dims, preferred_element_type=F32)


def dot_rows(a, b):
    return dot(jnp.concatenate([a[0], a[1], a[0]], 1), jnp.concatenate([b[0], b[0], b[1]], 1), NT)


def dot_columns(a, b):
    width = b[0].shape[1]
    both = dot(a[0], jnp.concatenate([b[0], b[1]], 1), NN)
    return both[:, :width] + (both[:, width:] + dot(a[1], b[0], NN))


def table_kernel(place, nbr_far, halo_far, table, nbr, halo, done):
    copies = [
        pltpu.make_async_copy(far, near, done.at[at])
        for at, (far, near) in enumerate([(nbr_far, nbr), (halo_far, halo)])
    ]
    for copy in copies:
        copy.start()
    for copy in copies:
        copy.wait()
    upper = place[1] >= SLABS // 2
    steps = jnp.where(upper, nbr[1:2, :], nbr[0:1, :])
    labels = jnp.where(upper, halo[0:1, :], halo[1:2, :])
    rows = [steps[:, :LANES], steps[:, LANES:], labels, labels, nbr[1:2, :LANES], nbr[1:2, LANES:], labels, labels]
    packed = jnp.concatenate(rows)
    for member in range(SLABS // 2):
        table[member] = packed


def order_kernel(nbr_far, halo_far, rhs_far, placed, order, spot, nbr, halo, rhs, done):
    copies = [
        pltpu.make_async_copy(far, near, done.at[at])
        for at, (far, near) in enumerate([(nbr_far, nbr), (halo_far, halo), (rhs_far, rhs)])
    ]
    for copy in copies:
        copy.start()
    copies[0].wait()
    copies[1].wait()

    def across(face, at):
        return nbr[face, at] & 255

    column = [halo[0, 0] & 255]
    for _ in range(15):
        column.append(across(5, column[-1]))
    rows = [column]
    for _ in range(7):
        rows.append([across(3, at) for at in rows[-1]])
    layers = [rows, [[across(1, at) for at in row] for row in rows]]
    for row in range(8):
        for sheet in range(16):
            spot[rows[row][sheet]] = row * 16 + sheet

    sub = lax.broadcasted_iota(jnp.int32, (8, LANES), 0)
    lane = lax.broadcasted_iota(jnp.int32, (8, LANES), 1)
    for sheet in range(16):
        for layer in range(2):
            at = jnp.zeros((8, LANES), jnp.int32)
            for row in range(8):
                at = jnp.where(sub == row, layers[layer][row][sheet], at)
            order[sheet * 2 + layer, :, :LANES] = jnp.where(lane == at, 1.0, 0.0).astype(F32)
            order[sheet * 2 + layer, :, LANES:] = jnp.where(lane + LANES == at, 1.0, 0.0).astype(F32)

    picks = order[...].reshape(SLAB, SLAB).astype(BF16)
    copies[2].wait()
    for step in range(2):
        high, low = split(rhs[step])
        values = dot(picks, high, NT) + dot(picks, low, NT)
        placed[step] = values.reshape(32, 8, NB)


def align_kernel(place, spot, placed, far, sent, shift, chain, tables, done):
    copies = [pltpu.make_async_copy(far, near, done.at[at]) for at, near in enumerate([chain, tables])]
    for copy in copies:
        copy.start()
    for copy in copies:
        copy.wait()
    group = lax.shift_right_logical(place[1], 2)
    member = place[1] & 3

    def step(slab, at):
        return chain[slab * 8 + lax.shift_right_logical(at, 7), at & 127]

    upper_rows = tables[28:30, :]
    index = lax.broadcasted_iota(jnp.int32, (2, LANES), 0) * LANES + lax.broadcasted_iota(jnp.int32, (2, LANES), 1)
    facing = jnp.sum(jnp.where(upper_rows == SLAB, index, 0)) & 255
    near = jnp.where(group == 0, facing, chain[2, 0] & 255)
    origin = near
    for hop in range(4):
        slab = jnp.where(group == 0, 3 - hop, hop)
        far_side = step(slab, near) & 255
        origin = jnp.where(slab == member, jnp.where(group == 0, far_side, near), origin)
        if hop < 3:
            label = step(slab, far_side) & 127
            ahead = jnp.where(group == 0, 2 - hop, hop + 1)
            near = chain[ahead * 8 + 2, label] & 255
    found = spot[origin] & 127
    first_row, first_sheet = lax.shift_right_logical(found, 4), found & 15
    shift[0] = (8 - first_row) & 7
    shift[1] = first_sheet
    for device in range(16):
        sheet = (SHEET_OF[device] + first_sheet) & 15
        for at in range(2):
            values = placed[at, pl.ds(sheet * 2, 2)]
            values = pltpu.roll(values, (8 - first_row) & 7, 1)
            sent[device, at * 16 : at * 16 + 16, :] = values.reshape(16, NB)


def first_weights(ref):
    return [ref.at[a:b] for a, b in [(0, 384), (384, 768), (768, 1536), (1536, 2304)]]


def second_weights(ref):
    return [ref.at[a:b] for a, b in [(0, 768), (768, 1536), (1536, 1920), (1920, 2304)]]


def face_order(place):
    core, slab = place[0] & 1, place[1] & 1
    return [1 - slab, slab, 4 + core, 5 - core, 2, 3]


def prepare_kernel(place, shift, placed_order, material, modes_in, modes_out, face_lift, rates, pick, *refs):
    order, first_set, factors_far, second_far, second_set, factors, lift, sorted_pick, done = refs
    in_h, in_l, trace_h, trace_l = first_weights(first_set)
    lift_h, lift_l, out_h, out_l = second_weights(second_set)
    same_r, same_i, cross = factors.at[0], factors.at[1], factors.at[2]
    in_parts = split(modes_in[...])
    in_h[...], in_l[...] = in_parts
    out_parts = split(modes_out[...])
    out_h[...], out_l[...] = out_parts
    for at, face in enumerate(face_order(place)):
        sorted_pick[at * LANES : (at + 1) * LANES, :] = pick[pl.ds(pl.multiple_of(face * LANES, LANES), LANES), :]
    trace_h[...] = dot(sorted_pick[...], out_parts[0], NN).astype(BF16)
    trace_l[...] = dot(sorted_pick[...], out_parts[1], NN).astype(BF16)
    for device in range(16):
        sheet = (SHEET_OF[device] + shift[1]) & 15
        picks = pltpu.roll(placed_order[pl.ds(sheet * 2, 2)], shift[0], 1)
        order[device * 16 : device * 16 + 16, :] = picks.reshape(16, SLAB).astype(BF16)
    own_picks = order[pl.ds(pl.multiple_of(place[0] * 16, 16), 16), :].astype(F32)
    own = jnp.sum(own_picks * material[...], axis=1, keepdims=True)
    for freq in range(16):
        angle = 2.0 * math.pi / STEPS * freq
        rows = slice(freq * 16, freq * 16 + 16)
        real = (1.0 - DECAY * math.cos(angle)) * own + rates[...]
        imag = jnp.broadcast_to((DECAY * math.sin(angle) if freq else 0.0) * own, (16, NB))
        size = real * real + imag * imag
        same = real / size
        same_r[rows, :] = same
        same_i[rows, :] = same if freq else 1.0 / ((1.0 + DECAY) * own + rates[...])
        cross[rows, :] = imag / size
    factors_copy = pltpu.make_async_copy(factors, factors_far, done.at[0])
    factors_copy.start()
    lift[...] = jnp.zeros_like(lift)
    for at, face in enumerate(face_order(place)):
        lift[at * LANES : at * LANES + NFT, :] = face_lift[face]
    lift_h[...], lift_l[...] = split(dot_rows(split(lift[...]), in_parts))
    copy = pltpu.make_async_copy(second_set, second_far, done.at[1])
    copy.start()
    copy.wait()
    factors_copy.wait()


def divided(modal, factors):
    real, imag = modal[:HALF], modal[HALF:]
    mixed = factors[2]
    return jnp.concatenate(
        [real * factors[0] + imag * mixed, imag * factors[1] - real * mixed]
    )


def pack(values):
    quarter = values.shape[0] // 4
    lane = lax.broadcasted_iota(jnp.int32, (quarter, LANES), 1)
    tail = values[3 * quarter :]
    parts = []
    for part in range(3):
        moved = pltpu.roll(tail, NFT - 32 * part, 1)
        parts.append(jnp.where(lane < NFT, values[part * quarter : (part + 1) * quarter], moved))
    return jnp.concatenate(parts)


def unpack(packed):
    quarter = packed.shape[0] // 3
    lane = lax.broadcasted_iota(jnp.int32, (quarter, LANES), 1)
    moved = [pltpu.roll(packed[part * quarter : (part + 1) * quarter], 32 + 32 * part, 1) for part in range(3)]
    tail = jnp.where(lane < 32, moved[0], jnp.where(lane < 64, moved[1], moved[2]))
    return jnp.concatenate([packed, tail])


def send_traces(place, solved, trace_h, trace_l, traces, solved_h, solved_l, inner, to_chip, to_next, to_even, to_odd):
    near = 1 - (place[1] & 1)
    solved_h[...], solved_l[...] = solved
    wide = 4 * LANES
    traces[...] = dot_rows(solved, (trace_h[:wide], trace_l[:wide])).reshape(STEPS, 2, 8, wide)
    to_chip[...] = pack(traces[:, :, :, 3 * LANES :].reshape(ROWS, LANES))
    to_next[...] = pack(traces[:, :, :, 2 * LANES : 3 * LANES].reshape(ROWS, LANES))
    to_even[...] = pack(traces[:, near, :, :LANES].reshape(HALF, LANES))
    to_odd[...] = pack(traces[:, 1 - near, :, LANES : 2 * LANES].reshape(HALF, LANES))
    inner[0] = traces[:, near, :, LANES : 2 * LANES].reshape(HALF, LANES)
    inner[1] = traces[:, 1 - near, :, :LANES].reshape(HALF, LANES)


def first_kernel(
    place, steps, first_set, factors_far,
    modal, solved_h, solved_l, inner, to_chip, to_next, to_even, to_odd, spectrum, traces, factors, done,
):
    factors_copy = pltpu.make_async_copy(factors_far, factors, done)
    factors_copy.start()
    in_h, in_l, trace_h, trace_l = first_weights(first_set)
    to_frequencies(steps, spectrum)
    start = dot_rows(split(spectrum[...]), (in_h[...], in_l[...]))
    modal[...] = start
    factors_copy.wait()
    solved = split(divided(start, factors))
    send_traces(
        place, solved, trace_h, trace_l, traces, solved_h, solved_l, inner, to_chip, to_next, to_even, to_odd
    )


def inside_kernel(modal, solved_h, solved_l, first_set, second_set, base):
    _, _, trace_h, trace_l = first_weights(first_set)
    lift_h, lift_l, _, _ = second_weights(second_set)
    wide = 4 * LANES
    traces = dot_rows((solved_h[...], solved_l[...]), (trace_h[wide:], trace_l[wide:]))
    traces = traces.reshape(ROWS // 8, 8, 2 * LANES)
    minus_y = pltpu.roll(traces[:, :, LANES:], 1, 1).reshape(ROWS, LANES)
    plus_y = pltpu.roll(traces[:, :, :LANES], 7, 1).reshape(ROWS, LANES)
    faces = split(jnp.concatenate([minus_y, plus_y], axis=1))
    base[...] = modal[...] - dot_columns(faces, (lift_h[wide:], lift_l[wide:]))


def meet_kernel(place, from_chip, from_next, base, inner, second_set, out, faces):
    near = 1 - (place[1] & 1)
    wide = 4 * LANES
    lift_h, lift_l, _, _ = second_weights(second_set)
    faces[:, near, :, :LANES] = jnp.zeros((STEPS, 8, LANES), F32)
    faces[:, 1 - near, :, :LANES] = inner[0].reshape(STEPS, 8, LANES)
    faces[:, near, :, LANES : 2 * LANES] = inner[1].reshape(STEPS, 8, LANES)
    faces[:, 1 - near, :, LANES : 2 * LANES] = jnp.zeros((STEPS, 8, LANES), F32)
    faces[:, :, :, 2 * LANES : 3 * LANES] = unpack(from_next[...]).reshape(STEPS, 2, 8, LANES)
    faces[:, :, :, 3 * LANES :] = unpack(from_chip[...]).reshape(STEPS, 2, 8, LANES)
    coupled = dot_columns(split(faces[...].reshape(ROWS, wide)), (lift_h[:wide], lift_l[:wide]))
    out[...] = (base[...] - coupled).reshape(STEPS, 2, 8, NB)


def corrected(place, from_even, from_odd, base, lift_h, lift_l, modes):
    near = 1 - (place[1] & 1)
    for at, (arrived, layer) in enumerate([(from_even, near), (from_odd, 1 - near)]):
        rows = slice(at * LANES, (at + 1) * LANES)
        coupled = dot_columns(split(unpack(arrived[...])), (lift_h[rows], lift_l[rows]))
        modes[:, layer] = base[:, layer] - coupled.reshape(STEPS, 8, NB)
    return modes[...].reshape(ROWS, NB)


def sweep_kernel(
    place, from_even, from_odd, base, first_set, second_set, factors,
    solved_h, solved_l, inner_out, to_chip, to_next, to_even, to_odd, modes, traces,
):
    _, _, trace_h, trace_l = first_weights(first_set)
    lift_h, lift_l, _, _ = second_weights(second_set)
    solved = split(divided(corrected(place, from_even, from_odd, base, lift_h, lift_l, modes), factors))
    send_traces(
        place, solved, trace_h, trace_l, traces, solved_h, solved_l, inner_out, to_chip, to_next, to_even, to_odd
    )


def last_kernel(place, from_even, from_odd, base, second_set, factors, steps, modes, spectrum):
    lift_h, lift_l, out_h, out_l = second_weights(second_set)
    solved = split(divided(corrected(place, from_even, from_odd, base, lift_h, lift_l, modes), factors))
    spectrum[...] = dot_rows(solved, (out_h[...], out_l[...]))
    to_steps(spectrum, steps)


def restore_kernel(arrived, order, far, out, done):
    copies = [pltpu.make_async_copy(out.at[step], far.at[step], done.at[step]) for step in range(2)]
    for step in range(2):
        values = arrived[:, step * 16 : step * 16 + 16, :].reshape(SLAB, NB)
        high, low = split(values)
        picks = order[...]
        out[step] = dot(high, picks, TN) + dot(low, picks, TN)
        copies[step].start()
    for copy in copies:
        copy.wait()


SMEM = pl.BlockSpec(memory_space=pltpu.SMEM)
VMEM = pl.BlockSpec(memory_space=pltpu.VMEM)
HBM = pl.BlockSpec(memory_space=pltpu.HBM)
KEPT = pl.BlockSpec(memory_space=pltpu.VMEM)
DMA = pltpu.SemaphoreType.DMA
HELD = ((HBM, pltpu.HBM), (KEPT, pltpu.VMEM))


def call(body, ins, outs, flops, scratch=(), megabytes=8):
    shapes = [jax.ShapeDtypeStruct(shape, kind) for shape, kind, _ in outs]
    moved = sum(a.size * a.dtype.itemsize for a in shapes + [a for a, _ in ins])
    for held, space in HELD:
        ins = [(pltpu.with_memory_space_constraint(a, space) if spec is held else a, spec) for a, spec in ins]
        shapes = [space(shape, kind) if spec is held else old for old, (shape, kind, spec) in zip(shapes, outs)]
    return pl.pallas_call(
        body,
        out_shape=shapes,
        in_specs=[spec for _, spec in ins],
        out_specs=[spec for _, _, spec in outs],
        scratch_shapes=list(scratch),
        compiler_params=pltpu.CompilerParams(vmem_limit_bytes=megabytes * 2**20),
        cost_estimate=pl.CostEstimate(flops=flops, bytes_accessed=moved, transcendentals=0),
    )(*[a for a, _ in ins])


def shards(rhs, material, modal_rates, modes_in, modes_out, face_lift, neighbours, halo_send):
    place = (jnp.stack([lax.axis_index("tm"), lax.axis_index("space")]).astype(jnp.int32), SMEM)
    (table,) = call(
        table_kernel,
        [place, (neighbours, HBM), (halo_send, HBM)],
        [((4, 8, LANES), jnp.int32, KEPT)],
        10**4,
        [pltpu.VMEM(neighbours.shape, jnp.int32), pltpu.VMEM(halo_send.shape, jnp.int32), DMA((2,))],
    )
    chain = lax.all_to_all(
        table, "space", 0, 0, tiled=True, axis_index_groups=[[0, 1, 2, 3], [4, 5, 6, 7]]
    ).reshape(32, LANES)
    placed, placed_order, spot = call(
        order_kernel,
        [(neighbours, HBM), (halo_send, HBM), (rhs, HBM)],
        [((2, 32, 8, NB), F32, KEPT), ((32, 8, SLAB), F32, KEPT), ((SLAB,), jnp.int32, SMEM)],
        2 * 4 * 256 * 256 * 384,
        [
            pltpu.SMEM(neighbours.shape, jnp.int32),
            pltpu.SMEM(halo_send.shape, jnp.int32),
            pltpu.VMEM(rhs.shape, F32),
            DMA((3,)),
        ],
    )
    sent, shift = call(
        align_kernel,
        [place, (spot, SMEM), (placed, KEPT), (chain, VMEM)],
        [((16, 32, NB), F32, KEPT), ((2,), jnp.int32, SMEM)],
        10**6,
        [pltpu.SMEM((32, LANES), jnp.int32), pltpu.VMEM((32, LANES), jnp.int32), DMA((2,))],
    )
    arrived = lax.all_to_all(sent, "tm", 0, 0, tiled=True).reshape(ROWS, NB)
    weights = [modes_in, modes_out, jnp.swapaxes(face_lift, 1, 2), modal_rates.reshape(1, NB), trace_rows()]
    prepared = [((SLAB, SLAB), BF16, KEPT), ((2304, NB), BF16, KEPT), ((3, HALF, NB), F32, HBM), ((2304, NB), BF16, HBM)]
    order, first_set, factors, second_set = call(
        prepare_kernel,
        [place, (shift, SMEM), (placed_order, KEPT), (material.reshape(1, SLAB), VMEM)]
        + [(jnp.asarray(weight), VMEM) for weight in weights],
        prepared,
        2 * 5 * 384 * 384 * 768,
        [pltpu.VMEM((2304, NB), BF16), pltpu.VMEM((3, HALF, NB), F32), pltpu.VMEM((6 * LANES, NB), F32), pltpu.VMEM((6 * LANES, NB), BF16), DMA((2,))],
    )

    faces = (
        [((ROWS, NB), BF16, KEPT)] * 2
        + [((2, HALF, LANES), F32, KEPT)]
        + [((ROWS * 3 // 4, LANES), F32, VMEM)] * 2
        + [((HALF * 3 // 4, LANES), F32, VMEM)] * 2
    )
    face_scratch = pltpu.VMEM((STEPS, 2, 8, 4 * LANES), F32)

    def exchange(to_chip, to_next, to_even, to_odd):
        from_odd = lax.ppermute(to_odd, "space", ODD_SIDES)
        from_even = lax.ppermute(to_even, "space", EVEN_SIDES)
        from_next = lax.ppermute(to_next, "tm", NEXT_CHIP)
        from_chip = lax.ppermute(to_chip, "tm", SAME_CHIP)
        return from_chip, from_next, from_even, from_odd

    def inside(solved_h, solved_l, inner, from_chip, from_next):
        (base,) = call(
            inside_kernel,
            [(a, KEPT) for a in (modal, solved_h, solved_l, first_set)] + [(second_set, VMEM)],
            [((ROWS, NB), F32, KEPT)],
            2 * 3 * 512 * 384 * 512,
        )
        (base,) = call(
            meet_kernel,
            [place]
            + [(a, VMEM) for a in (from_chip, from_next)]
            + [(base, KEPT), (inner, KEPT), (second_set, VMEM)],
            [((STEPS, 2, 8, NB), F32, KEPT)],
            2 * 3 * 512 * 384 * 512,
            [face_scratch],
        )
        return (base, KEPT)

    modal, solved_h, solved_l, inner, *outgoing = call(
        first_kernel,
        [place, (arrived, VMEM), (first_set, KEPT), (factors, HBM)],
        [((ROWS, NB), F32, KEPT)] + faces,
        2 * 3 * 512 * 384 * (384 + 512),
        [pltpu.VMEM((ROWS, NB), F32), face_scratch, pltpu.VMEM((3, HALF, NB), F32), DMA],
    )
    *incoming, from_even, from_odd = exchange(*outgoing)
    base = inside(solved_h, solved_l, inner, *incoming)
    solved_h, solved_l, inner, *outgoing = call(
        sweep_kernel,
        [place, (from_even, VMEM), (from_odd, VMEM), base, (first_set, KEPT), (second_set, VMEM), (factors, VMEM)],
        faces,
        2 * 3 * 512 * 384 * 512,
        [pltpu.VMEM((STEPS, 2, 8, NB), F32), face_scratch],
    )
    *incoming, from_even, from_odd = exchange(*outgoing)
    base = inside(solved_h, solved_l, inner, *incoming)
    (steps,) = call(
        last_kernel,
        [place, (from_even, VMEM), (from_odd, VMEM), base, (second_set, VMEM), (factors, VMEM)],
        [((ROWS, NB), F32, VMEM)],
        2 * 3 * 512 * 384 * 384,
        [pltpu.VMEM((STEPS, 2, 8, NB), F32), pltpu.VMEM((ROWS, NB), F32)],
    )
    back = lax.all_to_all(steps.reshape(16, 32, NB), "tm", 0, 0, tiled=True)
    (out,) = call(
        restore_kernel,
        [(back, VMEM), (order, KEPT)],
        [((2, NB, SLAB), F32, HBM)],
        2 * 4 * 256 * 256 * 384,
        [pltpu.VMEM((2, NB, SLAB), F32), DMA((2,))],
    )
    return out


def solution(mesh):
    return jax.shard_map(
        shards,
        mesh=mesh,
        in_specs=(
            P("tm", None, "space"),
            P("space"),
            P(),
            P(),
            P(),
            P(),
            P(None, "space"),
            P(None, "space"),
        ),
        out_specs=P("tm", None, "space"),
        check_vma=False,
    )
```

```python
import math

import jax
import jax.numpy as jnp
import ml_dtypes
import numpy as np
from jax import lax
from jax.experimental import pallas as pl
from jax.experimental.pallas import tpu as pltpu
from jax.sharding import PartitionSpec as P

NB = 384
NFT = 96
LANES = 128
STEPS = 32
SLAB = 256
SHEET = 16
ROWS = STEPS * SHEET
HALF = ROWS // 2
SLABS = 8
DECAY = 0.1 ** (1.0 / STEPS)

RING = (0, 1, 4, 5, 8, 9, 12, 13, 14, 15, 10, 11, 6, 7, 2, 3)
SHEET_OF = tuple(RING.index(device) for device in range(16))
SAME_CHIP = [(i, i ^ 1) for i in range(16)]
NEXT_CHIP = [(RING[2 * i + 1], RING[(2 * i + 2) % 16]) for i in range(8)]
NEXT_CHIP = NEXT_CHIP + [(b, a) for a, b in NEXT_CHIP]
EVEN_SIDES = [(i, i ^ 1) for i in range(8)]
ODD_SIDES = [(1, 2), (2, 1), (3, 4), (4, 3), (5, 6), (6, 5)]

F32 = jnp.float32
BF16 = jnp.bfloat16
NN = (((1,), (0,)), ((), ()))
NT = (((1,), (1,)), ((), ()))
TN = (((0,), (0,)), ((), ()))


def real_fft(steps):
    count = len(steps)
    if count == 2:
        return [(steps[0] + steps[1], None), (steps[0] - steps[1], None)]
    even, odd = real_fft(steps[0::2]), real_fft(steps[1::2])
    out = [None] * (count // 2 + 1)
    out[0] = (even[0][0] + odd[0][0], None)
    out[count // 2] = (even[0][0] - odd[0][0], None)
    out[count // 4] = (even[count // 4][0], -odd[count // 4][0])
    for freq in range(1, count // 4):
        cos, sin = math.cos(2.0 * math.pi * freq / count), math.sin(2.0 * math.pi * freq / count)
        real, imag = odd[freq]
        turned_real, turned_imag = real * cos + imag * sin, imag * cos - real * sin
        real, imag = even[freq]
        out[freq] = (real + turned_real, imag + turned_imag)
        out[count // 2 - freq] = (real - turned_real, turned_imag - imag)
    return out


def real_ifft(freqs):
    count = 2 * (len(freqs) - 1)
    first, last = freqs[0][0], freqs[-1][0]
    if count == 2:
        return [first + last, first - last]
    even, odd = [None] * (count // 4 + 1), [None] * (count // 4 + 1)
    even[0], odd[0] = (first + last, None), (first - last, None)
    middle = freqs[count // 4]
    even[-1], odd[-1] = (2.0 * middle[0], None), (-2.0 * middle[1], None)
    for freq in range(1, count // 4):
        cos, sin = math.cos(2.0 * math.pi * freq / count), math.sin(2.0 * math.pi * freq / count)
        (real, imag), (other_real, other_imag) = freqs[freq], freqs[count // 2 - freq]
        even[freq] = (real + other_real, imag - other_imag)
        real, imag = real - other_real, imag + other_imag
        odd[freq] = (real * cos - imag * sin, imag * cos + real * sin)
    out = [None] * count
    out[0::2], out[1::2] = real_ifft(even), real_ifft(odd)
    return out


def tiles():
    for lane in range(0, NB, LANES):
        for block in range(SHEET // 8):
            yield lambda row: (slice(row * SHEET + block * 8, row * SHEET + block * 8 + 8), slice(lane, lane + LANES))


def to_frequencies(steps, spectrum):
    for at in tiles():
        freqs = real_fft([steps[at(n)] * DECAY**n for n in range(STEPS)])
        for freq in range(16):
            spectrum[at(freq)] = freqs[freq][0]
            spectrum[at(16 + freq)] = freqs[freq][1] if freq else freqs[16][0]


def to_steps(spectrum, steps):
    for at in tiles():
        pairs = [(spectrum[at(freq)], spectrum[at(16 + freq)]) for freq in range(16)]
        freqs = [(pairs[0][0], None)] + pairs[1:] + [(pairs[0][1], None)]
        for n, value in enumerate(real_ifft(freqs)):
            steps[at(n)] = value * (DECAY**-n / STEPS)


def trace_rows():
    pick = np.zeros((6 * LANES, NB), np.float32)
    for face in range(6):
        for lane in range(NFT):
            field, first, second = lane // 16, lane // 4 % 4, lane % 4
            place = [first, second]
            place.insert(face // 2, 0 if face % 2 == 0 else 3)
            pick[face * LANES + lane, field * 64 + place[0] * 16 + place[1] * 4 + place[2]] = 1.0
    return pick.astype(ml_dtypes.bfloat16)


def split(values):
    high = values.astype(BF16)
    low = (values - high.astype(F32)).astype(BF16)
    return high, low


def dot(a, b, dims):
    return lax.dot_general(a, b, dims, preferred_element_type=F32)


def dot_rows(a, b):
    return dot(jnp.concatenate([a[0], a[1], a[0]], 1), jnp.concatenate([b[0], b[0], b[1]], 1), NT)


def dot_columns(a, b):
    width = b[0].shape[1]
    both = dot(a[0], jnp.concatenate([b[0], b[1]], 1), NN)
    return both[:, :width] + (both[:, width:] + dot(a[1], b[0], NN))


def table_kernel(place, nbr_far, halo_far, table, nbr, halo, done):
    copies = [
        pltpu.make_async_copy(far, near, done.at[at])
        for at, (far, near) in enumerate([(nbr_far, nbr), (halo_far, halo)])
    ]
    for copy in copies:
        copy.start()
    for copy in copies:
        copy.wait()
    upper = place[1] >= SLABS // 2
    steps = jnp.where(upper, nbr[1:2, :], nbr[0:1, :])
    labels = jnp.where(upper, halo[0:1, :], halo[1:2, :])
    index = lax.broadcasted_iota(jnp.int32, (1, SLAB), 1)
    facing = jnp.sum(jnp.where(nbr[1:2, :] == SLAB, index, 0), axis=1, keepdims=True)
    rows = [steps[:, :LANES], steps[:, LANES:], labels, jnp.broadcast_to(facing, (1, LANES))]
    packed = jnp.concatenate(rows + rows)
    for member in range(SLABS // 2):
        table[member] = packed


def order_kernel(nbr_far, halo_far, rhs_far, placed, order, spot, nbr, halo, rhs, done):
    copies = [
        pltpu.make_async_copy(far, near, done.at[at])
        for at, (far, near) in enumerate([(nbr_far, nbr), (halo_far, halo), (rhs_far, rhs)])
    ]
    for copy in copies:
        copy.start()
    copies[0].wait()
    copies[1].wait()

    def across(face, at):
        return nbr[face, at] & 255

    column = [halo[0, 0] & 255]
    for _ in range(15):
        column.append(across(5, column[-1]))
    rows = [column]
    for _ in range(7):
        rows.append([across(3, at) for at in rows[-1]])
    layers = [rows, [[across(1, at) for at in row] for row in rows]]
    for row in range(8):
        for sheet in range(16):
            spot[rows[row][sheet]] = row * 16 + sheet

    sub = lax.broadcasted_iota(jnp.int32, (8, LANES), 0)
    lane = lax.broadcasted_iota(jnp.int32, (8, LANES), 1)
    for sheet in range(16):
        for layer in range(2):
            at = jnp.zeros((8, LANES), jnp.int32)
            for row in range(8):
                at = jnp.where(sub == row, layers[layer][row][sheet], at)
            order[sheet * 2 + layer, :, :LANES] = jnp.where(lane == at, 1.0, 0.0).astype(F32)
            order[sheet * 2 + layer, :, LANES:] = jnp.where(lane + LANES == at, 1.0, 0.0).astype(F32)

    picks = order[...].reshape(SLAB, SLAB).astype(BF16)
    copies[2].wait()
    for step in range(2):
        high, low = split(rhs[step])
        values = dot(picks, high, NT) + dot(picks, low, NT)
        placed[step] = values.reshape(32, 8, NB)


def align_kernel(place, spot, chain, placed, sent, shift):
    group = lax.shift_right_logical(place[1], 2)
    member = place[1] & 3

    def step(slab, at):
        return chain[slab * 8 + lax.shift_right_logical(at, 7), at & 127]

    near = jnp.where(group == 0, chain[27, 0], chain[2, 0]) & 255
    origin = near
    for hop in range(4):
        slab = jnp.where(group == 0, 3 - hop, hop)
        far_side = step(slab, near) & 255
        origin = jnp.where(slab == member, jnp.where(group == 0, far_side, near), origin)
        if hop < 3:
            label = step(slab, far_side) & 127
            ahead = jnp.where(group == 0, 2 - hop, hop + 1)
            near = chain[ahead * 8 + 2, label] & 255
    found = spot[origin] & 127
    first_row, first_sheet = lax.shift_right_logical(found, 4), found & 15
    shift[0] = (8 - first_row) & 7
    shift[1] = first_sheet
    for device in range(16):
        sheet = (SHEET_OF[device] + first_sheet) & 15
        for at in range(2):
            values = placed[at, pl.ds(sheet * 2, 2)]
            values = pltpu.roll(values, (8 - first_row) & 7, 1)
            sent[device, at * 16 : at * 16 + 16, :] = values.reshape(16, NB)


def first_weights(ref):
    return [ref.at[a:b] for a, b in [(0, 384), (384, 768), (768, 1536), (1536, 2304)]]


def second_weights(ref):
    return [ref.at[a:b] for a, b in [(0, 768), (768, 1536), (1536, 1920), (1920, 2304)]]


def face_order(place):
    core, slab = place[0] & 1, place[1] & 1
    return [1 - slab, slab, 4 + core, 5 - core, 2, 3]


def prepare_kernel(place, shift, placed_order, material, modes_in, modes_out, face_lift, rates, pick, *refs):
    order, first_set, factors_far, second_far, second_set, factors, lift, sorted_pick, done = refs
    in_h, in_l, trace_h, trace_l = first_weights(first_set)
    lift_h, lift_l, out_h, out_l = second_weights(second_set)
    same_r, same_i, cross = factors.at[0], factors.at[1], factors.at[2]
    in_parts = split(modes_in[...])
    in_h[...], in_l[...] = in_parts
    out_parts = split(modes_out[...])
    out_h[...], out_l[...] = out_parts
    for at, face in enumerate(face_order(place)):
        sorted_pick[at * LANES : (at + 1) * LANES, :] = pick[pl.ds(pl.multiple_of(face * LANES, LANES), LANES), :]
    trace_h[...] = dot(sorted_pick[...], out_parts[0], NN).astype(BF16)
    trace_l[...] = dot(sorted_pick[...], out_parts[1], NN).astype(BF16)
    for device in range(16):
        sheet = (SHEET_OF[device] + shift[1]) & 15
        picks = pltpu.roll(placed_order[pl.ds(sheet * 2, 2)], shift[0], 1)
        order[device * 16 : device * 16 + 16, :] = picks.reshape(16, SLAB).astype(BF16)
    own_picks = order[pl.ds(pl.multiple_of(place[0] * 16, 16), 16), :].astype(F32)
    own = jnp.sum(own_picks * material[...], axis=1, keepdims=True)
    for freq in range(16):
        angle = 2.0 * math.pi / STEPS * freq
        rows = slice(freq * 16, freq * 16 + 16)
        real = (1.0 - DECAY * math.cos(angle)) * own + rates[...]
        imag = jnp.broadcast_to((DECAY * math.sin(angle) if freq else 0.0) * own, (16, NB))
        size = real * real + imag * imag
        same = real / size
        same_r[rows, :] = same
        same_i[rows, :] = same if freq else 1.0 / ((1.0 + DECAY) * own + rates[...])
        cross[rows, :] = imag / size
    factors_copy = pltpu.make_async_copy(factors, factors_far, done.at[0])
    factors_copy.start()
    lift[...] = jnp.zeros_like(lift)
    for at, face in enumerate(face_order(place)):
        lift[at * LANES : at * LANES + NFT, :] = face_lift[face]
    lift_h[...], lift_l[...] = split(dot_rows(split(lift[...]), in_parts))
    copy = pltpu.make_async_copy(second_set, second_far, done.at[1])
    copy.start()
    copy.wait()
    factors_copy.wait()


def divided(modal, factors):
    real, imag = modal[:HALF], modal[HALF:]
    mixed = factors[2]
    return jnp.concatenate(
        [real * factors[0] + imag * mixed, imag * factors[1] - real * mixed]
    )


def pack(values):
    quarter = values.shape[0] // 4
    lane = lax.broadcasted_iota(jnp.int32, (quarter, LANES), 1)
    tail = values[3 * quarter :]
    parts = []
    for part in range(3):
        moved = pltpu.roll(tail, NFT - 32 * part, 1)
        parts.append(jnp.where(lane < NFT, values[part * quarter : (part + 1) * quarter], moved))
    return jnp.concatenate(parts)


def unpack(packed):
    quarter = packed.shape[0] // 3
    lane = lax.broadcasted_iota(jnp.int32, (quarter, LANES), 1)
    moved = [pltpu.roll(packed[part * quarter : (part + 1) * quarter], 32 + 32 * part, 1) for part in range(3)]
    tail = jnp.where(lane < 32, moved[0], jnp.where(lane < 64, moved[1], moved[2]))
    return jnp.concatenate([packed, tail])


def send_traces(place, solved, trace_h, trace_l, traces, solved_h, solved_l, inner, to_chip, to_next, to_even, to_odd):
    near = 1 - (place[1] & 1)
    solved_h[...], solved_l[...] = solved
    wide = 4 * LANES
    traces[...] = dot_rows(solved, (trace_h[:wide], trace_l[:wide])).reshape(STEPS, 2, 8, wide)
    to_chip[...] = pack(traces[:, :, :, 3 * LANES :].reshape(ROWS, LANES))
    to_next[...] = pack(traces[:, :, :, 2 * LANES : 3 * LANES].reshape(ROWS, LANES))
    to_even[...] = pack(traces[:, near, :, :LANES].reshape(HALF, LANES))
    to_odd[...] = pack(traces[:, 1 - near, :, LANES : 2 * LANES].reshape(HALF, LANES))
    inner[0] = traces[:, near, :, LANES : 2 * LANES].reshape(HALF, LANES)
    inner[1] = traces[:, 1 - near, :, :LANES].reshape(HALF, LANES)


def first_kernel(
    place, steps, first_set, factors_far,
    modal, solved_h, solved_l, inner, to_chip, to_next, to_even, to_odd, spectrum, traces, factors, done,
):
    factors_copy = pltpu.make_async_copy(factors_far, factors, done)
    factors_copy.start()
    in_h, in_l, trace_h, trace_l = first_weights(first_set)
    to_frequencies(steps, spectrum)
    start = dot_rows(split(spectrum[...]), (in_h[...], in_l[...]))
    modal[...] = start
    factors_copy.wait()
    solved = split(divided(start, factors))
    send_traces(
        place, solved, trace_h, trace_l, traces, solved_h, solved_l, inner, to_chip, to_next, to_even, to_odd
    )


def inside_kernel(modal, solved_h, solved_l, first_set, second_set, base):
    _, _, trace_h, trace_l = first_weights(first_set)
    lift_h, lift_l, _, _ = second_weights(second_set)
    wide = 4 * LANES
    traces = dot_rows((solved_h[...], solved_l[...]), (trace_h[wide:], trace_l[wide:]))
    traces = traces.reshape(ROWS // 8, 8, 2 * LANES)
    minus_y = pltpu.roll(traces[:, :, LANES:], 1, 1).reshape(ROWS, LANES)
    plus_y = pltpu.roll(traces[:, :, :LANES], 7, 1).reshape(ROWS, LANES)
    faces = split(jnp.concatenate([minus_y, plus_y], axis=1))
    base[...] = modal[...] - dot_columns(faces, (lift_h[wide:], lift_l[wide:]))


def meet_kernel(place, from_chip, from_next, base, inner, second_set, out, faces):
    near = 1 - (place[1] & 1)
    wide = 4 * LANES
    lift_h, lift_l, _, _ = second_weights(second_set)
    faces[:, near, :, :LANES] = jnp.zeros((STEPS, 8, LANES), F32)
    faces[:, 1 - near, :, :LANES] = inner[0].reshape(STEPS, 8, LANES)
    faces[:, near, :, LANES : 2 * LANES] = inner[1].reshape(STEPS, 8, LANES)
    faces[:, 1 - near, :, LANES : 2 * LANES] = jnp.zeros((STEPS, 8, LANES), F32)
    faces[:, :, :, 2 * LANES : 3 * LANES] = unpack(from_next[...]).reshape(STEPS, 2, 8, LANES)
    faces[:, :, :, 3 * LANES :] = unpack(from_chip[...]).reshape(STEPS, 2, 8, LANES)
    coupled = dot_columns(split(faces[...].reshape(ROWS, wide)), (lift_h[:wide], lift_l[:wide]))
    out[...] = (base[...] - coupled).reshape(STEPS, 2, 8, NB)


def corrected(place, from_even, from_odd, base, lift_h, lift_l, modes):
    near = 1 - (place[1] & 1)
    for at, (arrived, layer) in enumerate([(from_even, near), (from_odd, 1 - near)]):
        rows = slice(at * LANES, (at + 1) * LANES)
        coupled = dot_columns(split(unpack(arrived[...])), (lift_h[rows], lift_l[rows]))
        modes[:, layer] = base[:, layer] - coupled.reshape(STEPS, 8, NB)
    return modes[...].reshape(ROWS, NB)


def sweep_kernel(
    place, from_even, from_odd, base, first_set, second_set, factors,
    solved_h, solved_l, inner_out, to_chip, to_next, to_even, to_odd, modes, traces,
):
    _, _, trace_h, trace_l = first_weights(first_set)
    lift_h, lift_l, _, _ = second_weights(second_set)
    solved = split(divided(corrected(place, from_even, from_odd, base, lift_h, lift_l, modes), factors))
    send_traces(
        place, solved, trace_h, trace_l, traces, solved_h, solved_l, inner_out, to_chip, to_next, to_even, to_odd
    )


def last_kernel(place, from_even, from_odd, base, second_set, factors, steps, modes, spectrum):
    lift_h, lift_l, out_h, out_l = second_weights(second_set)
    solved = split(divided(corrected(place, from_even, from_odd, base, lift_h, lift_l, modes), factors))
    spectrum[...] = dot_rows(solved, (out_h[...], out_l[...]))
    to_steps(spectrum, steps)


def restore_kernel(arrived, order, far, out, done):
    copies = [pltpu.make_async_copy(out.at[step], far.at[step], done.at[step]) for step in range(2)]
    for step in range(2):
        values = arrived[:, step * 16 : step * 16 + 16, :].reshape(SLAB, NB)
        high, low = split(values)
        picks = order[...]
        out[step] = dot(high, picks, TN) + dot(low, picks, TN)
        copies[step].start()
    for copy in copies:
        copy.wait()


SMEM = pl.BlockSpec(memory_space=pltpu.SMEM)
VMEM = pl.BlockSpec(memory_space=pltpu.VMEM)
HBM = pl.BlockSpec(memory_space=pltpu.HBM)
KEPT = pl.BlockSpec(memory_space=pltpu.VMEM)
DMA = pltpu.SemaphoreType.DMA
HELD = ((HBM, pltpu.HBM), (KEPT, pltpu.VMEM))


def call(body, ins, outs, flops, scratch=(), megabytes=8):
    shapes = [jax.ShapeDtypeStruct(shape, kind) for shape, kind, _ in outs]
    moved = sum(a.size * a.dtype.itemsize for a in shapes + [a for a, _ in ins])
    for held, space in HELD:
        ins = [(pltpu.with_memory_space_constraint(a, space) if spec is held else a, spec) for a, spec in ins]
        shapes = [space(shape, kind) if spec is held else old for old, (shape, kind, spec) in zip(shapes, outs)]
    return pl.pallas_call(
        body,
        out_shape=shapes,
        in_specs=[spec for _, spec in ins],
        out_specs=[spec for _, _, spec in outs],
        scratch_shapes=list(scratch),
        compiler_params=pltpu.CompilerParams(vmem_limit_bytes=megabytes * 2**20),
        cost_estimate=pl.CostEstimate(flops=flops, bytes_accessed=moved, transcendentals=0),
    )(*[a for a, _ in ins])


def shards(rhs, material, modal_rates, modes_in, modes_out, face_lift, neighbours, halo_send):
    place = (jnp.stack([lax.axis_index("tm"), lax.axis_index("space")]).astype(jnp.int32), SMEM)
    (table,) = call(
        table_kernel,
        [place, (neighbours, HBM), (halo_send, HBM)],
        [((4, 8, LANES), jnp.int32, KEPT)],
        10**4,
        [pltpu.VMEM(neighbours.shape, jnp.int32), pltpu.VMEM(halo_send.shape, jnp.int32), DMA((2,))],
    )
    chain = lax.all_to_all(
        table, "space", 0, 0, tiled=True, axis_index_groups=[[0, 1, 2, 3], [4, 5, 6, 7]]
    ).reshape(32, LANES)
    placed, placed_order, spot = call(
        order_kernel,
        [(neighbours, HBM), (halo_send, HBM), (rhs, HBM)],
        [((2, 32, 8, NB), F32, KEPT), ((32, 8, SLAB), F32, KEPT), ((SLAB,), jnp.int32, SMEM)],
        2 * 4 * 256 * 256 * 384,
        [
            pltpu.SMEM(neighbours.shape, jnp.int32),
            pltpu.SMEM(halo_send.shape, jnp.int32),
            pltpu.VMEM(rhs.shape, F32),
            DMA((3,)),
        ],
    )
    sent, shift = call(
        align_kernel,
        [place, (spot, SMEM), (chain, SMEM), (placed, KEPT)],
        [((16, 32, NB), F32, KEPT), ((2,), jnp.int32, SMEM)],
        10**6,
    )
    arrived = lax.all_to_all(sent, "tm", 0, 0, tiled=True).reshape(ROWS, NB)
    weights = [modes_in, modes_out, jnp.swapaxes(face_lift, 1, 2), modal_rates.reshape(1, NB), trace_rows()]
    prepared = [((SLAB, SLAB), BF16, KEPT), ((2304, NB), BF16, KEPT), ((3, HALF, NB), F32, HBM), ((2304, NB), BF16, HBM)]
    order, first_set, factors, second_set = call(
        prepare_kernel,
        [place, (shift, SMEM), (placed_order, KEPT), (material.reshape(1, SLAB), VMEM)]
        + [(jnp.asarray(weight), VMEM) for weight in weights],
        prepared,
        2 * 5 * 384 * 384 * 768,
        [pltpu.VMEM((2304, NB), BF16), pltpu.VMEM((3, HALF, NB), F32), pltpu.VMEM((6 * LANES, NB), F32), pltpu.VMEM((6 * LANES, NB), BF16), DMA((2,))],
    )

    faces = (
        [((ROWS, NB), BF16, KEPT)] * 2
        + [((2, HALF, LANES), F32, KEPT)]
        + [((ROWS * 3 // 4, LANES), F32, VMEM)] * 2
        + [((HALF * 3 // 4, LANES), F32, VMEM)] * 2
    )
    face_scratch = pltpu.VMEM((STEPS, 2, 8, 4 * LANES), F32)

    def exchange(to_chip, to_next, to_even, to_odd):
        from_odd = lax.ppermute(to_odd, "space", ODD_SIDES)
        from_even = lax.ppermute(to_even, "space", EVEN_SIDES)
        from_next = lax.ppermute(to_next, "tm", NEXT_CHIP)
        from_chip = lax.ppermute(to_chip, "tm", SAME_CHIP)
        return from_chip, from_next, from_even, from_odd

    def inside(solved_h, solved_l, inner, from_chip, from_next):
        (base,) = call(
            inside_kernel,
            [(a, KEPT) for a in (modal, solved_h, solved_l, first_set)] + [(second_set, VMEM)],
            [((ROWS, NB), F32, KEPT)],
            2 * 3 * 512 * 384 * 512,
        )
        (base,) = call(
            meet_kernel,
            [place]
            + [(a, VMEM) for a in (from_chip, from_next)]
            + [(base, KEPT), (inner, KEPT), (second_set, VMEM)],
            [((STEPS, 2, 8, NB), F32, KEPT)],
            2 * 3 * 512 * 384 * 512,
            [face_scratch],
        )
        return (base, KEPT)

    modal, solved_h, solved_l, inner, *outgoing = call(
        first_kernel,
        [place, (arrived, VMEM), (first_set, KEPT), (factors, HBM)],
        [((ROWS, NB), F32, KEPT)] + faces,
        2 * 3 * 512 * 384 * (384 + 512),
        [pltpu.VMEM((ROWS, NB), F32), face_scratch, pltpu.VMEM((3, HALF, NB), F32), DMA],
    )
    *incoming, from_even, from_odd = exchange(*outgoing)
    base = inside(solved_h, solved_l, inner, *incoming)
    solved_h, solved_l, inner, *outgoing = call(
        sweep_kernel,
        [place, (from_even, VMEM), (from_odd, VMEM), base, (first_set, KEPT), (second_set, VMEM), (factors, VMEM)],
        faces,
        2 * 3 * 512 * 384 * 512,
        [pltpu.VMEM((STEPS, 2, 8, NB), F32), face_scratch],
    )
    *incoming, from_even, from_odd = exchange(*outgoing)
    base = inside(solved_h, solved_l, inner, *incoming)
    (steps,) = call(
        last_kernel,
        [place, (from_even, VMEM), (from_odd, VMEM), base, (second_set, VMEM), (factors, VMEM)],
        [((ROWS, NB), F32, VMEM)],
        2 * 3 * 512 * 384 * 384,
        [pltpu.VMEM((STEPS, 2, 8, NB), F32), pltpu.VMEM((ROWS, NB), F32)],
    )
    back = lax.all_to_all(steps.reshape(16, 32, NB), "tm", 0, 0, tiled=True)
    (out,) = call(
        restore_kernel,
        [(back, VMEM), (order, KEPT)],
        [((2, NB, SLAB), F32, HBM)],
        2 * 4 * 256 * 256 * 384,
        [pltpu.VMEM((2, NB, SLAB), F32), DMA((2,))],
    )
    return out


def solution(mesh):
    return jax.shard_map(
        shards,
        mesh=mesh,
        in_specs=(
            P("tm", None, "space"),
            P("space"),
            P(),
            P(),
            P(),
            P(),
            P(None, "space"),
            P(None, "space"),
        ),
        out_specs=P("tm", None, "space"),
        check_vma=False,
    )
```

```python
import math

import jax
import jax.numpy as jnp
import ml_dtypes
import numpy as np
from jax import lax
from jax.experimental import pallas as pl
from jax.experimental.pallas import tpu as pltpu
from jax.sharding import PartitionSpec as P

NB = 384
NFT = 96
LANES = 128
STEPS = 32
SLAB = 256
SHEET = 16
ROWS = STEPS * SHEET
HALF = ROWS // 2
SLABS = 8
DECAY = 0.1 ** (1.0 / STEPS)

RING = (0, 1, 4, 5, 8, 9, 12, 13, 14, 15, 10, 11, 6, 7, 2, 3)
SHEET_OF = tuple(RING.index(device) for device in range(16))
SAME_CHIP = [(i, i ^ 1) for i in range(16)]
NEXT_CHIP = [(RING[2 * i + 1], RING[(2 * i + 2) % 16]) for i in range(8)]
NEXT_CHIP = NEXT_CHIP + [(b, a) for a, b in NEXT_CHIP]
EVEN_SIDES = [(i, i ^ 1) for i in range(8)]
ODD_SIDES = [(1, 2), (2, 1), (3, 4), (4, 3), (5, 6), (6, 5)]

F32 = jnp.float32
BF16 = jnp.bfloat16
NN = (((1,), (0,)), ((), ()))
NT = (((1,), (1,)), ((), ()))
TN = (((0,), (0,)), ((), ()))


def real_fft(steps):
    count = len(steps)
    if count == 2:
        return [(steps[0] + steps[1], None), (steps[0] - steps[1], None)]
    even, odd = real_fft(steps[0::2]), real_fft(steps[1::2])
    out = [None] * (count // 2 + 1)
    out[0] = (even[0][0] + odd[0][0], None)
    out[count // 2] = (even[0][0] - odd[0][0], None)
    out[count // 4] = (even[count // 4][0], -odd[count // 4][0])
    for freq in range(1, count // 4):
        cos, sin = math.cos(2.0 * math.pi * freq / count), math.sin(2.0 * math.pi * freq / count)
        real, imag = odd[freq]
        turned_real, turned_imag = real * cos + imag * sin, imag * cos - real * sin
        real, imag = even[freq]
        out[freq] = (real + turned_real, imag + turned_imag)
        out[count // 2 - freq] = (real - turned_real, turned_imag - imag)
    return out


def real_ifft(freqs):
    count = 2 * (len(freqs) - 1)
    first, last = freqs[0][0], freqs[-1][0]
    if count == 2:
        return [first + last, first - last]
    even, odd = [None] * (count // 4 + 1), [None] * (count // 4 + 1)
    even[0], odd[0] = (first + last, None), (first - last, None)
    middle = freqs[count // 4]
    even[-1], odd[-1] = (2.0 * middle[0], None), (-2.0 * middle[1], None)
    for freq in range(1, count // 4):
        cos, sin = math.cos(2.0 * math.pi * freq / count), math.sin(2.0 * math.pi * freq / count)
        (real, imag), (other_real, other_imag) = freqs[freq], freqs[count // 2 - freq]
        even[freq] = (real + other_real, imag - other_imag)
        real, imag = real - other_real, imag + other_imag
        odd[freq] = (real * cos - imag * sin, imag * cos + real * sin)
    out = [None] * count
    out[0::2], out[1::2] = real_ifft(even), real_ifft(odd)
    return out


def tiles():
    for lane in range(0, NB, LANES):
        for block in range(SHEET // 8):
            yield lambda row: (slice(row * SHEET + block * 8, row * SHEET + block * 8 + 8), slice(lane, lane + LANES))


def to_frequencies(steps, spectrum):
    for at in tiles():
        freqs = real_fft([steps[at(n)] * DECAY**n for n in range(STEPS)])
        for freq in range(16):
            spectrum[at(freq)] = freqs[freq][0]
            spectrum[at(16 + freq)] = freqs[freq][1] if freq else freqs[16][0]


def to_steps(spectrum, steps):
    for at in tiles():
        pairs = [(spectrum[at(freq)], spectrum[at(16 + freq)]) for freq in range(16)]
        freqs = [(pairs[0][0], None)] + pairs[1:] + [(pairs[0][1], None)]
        for n, value in enumerate(real_ifft(freqs)):
            steps[at(n)] = value * (DECAY**-n / STEPS)


def trace_rows():
    pick = np.zeros((6 * LANES, NB), np.float32)
    for face in range(6):
        for lane in range(NFT):
            field, first, second = lane // 16, lane // 4 % 4, lane % 4
            place = [first, second]
            place.insert(face // 2, 0 if face % 2 == 0 else 3)
            pick[face * LANES + lane, field * 64 + place[0] * 16 + place[1] * 4 + place[2]] = 1.0
    return pick.astype(ml_dtypes.bfloat16)


def split(values):
    high = values.astype(BF16)
    low = (values - high.astype(F32)).astype(BF16)
    return high, low


def dot(a, b, dims):
    return lax.dot_general(a, b, dims, preferred_element_type=F32)


def dot_rows(a, b):
    return dot(jnp.concatenate([a[0], a[1], a[0]], 1), jnp.concatenate([b[0], b[0], b[1]], 1), NT)


def dot_columns(a, b):
    width = b[0].shape[1]
    both = dot(a[0], jnp.concatenate([b[0], b[1]], 1), NN)
    return both[:, :width] + (both[:, width:] + dot(a[1], b[0], NN))


def table_kernel(place, nbr_far, halo_far, table, nbr, halo, done):
    copies = [
        pltpu.make_async_copy(far, near, done.at[at])
        for at, (far, near) in enumerate([(nbr_far, nbr), (halo_far, halo)])
    ]
    for copy in copies:
        copy.start()
    for copy in copies:
        copy.wait()
    upper = place[1] >= SLABS // 2
    steps = jnp.where(upper, nbr[1:2, :], nbr[0:1, :])
    labels = jnp.where(upper, halo[0:1, :], halo[1:2, :])
    index = lax.broadcasted_iota(jnp.int32, (1, SLAB), 1)
    facing = jnp.sum(jnp.where(nbr[1:2, :] == SLAB, index, 0), axis=1, keepdims=True)
    rows = [steps[:, :LANES], steps[:, LANES:], labels, jnp.broadcast_to(facing, (1, LANES))]
    packed = jnp.concatenate(rows)
    for member in range(SLABS // 2):
        table[member] = packed


def order_kernel(nbr_far, halo_far, rhs_far, placed, order, spot, nbr, halo, rhs, done):
    copies = [
        pltpu.make_async_copy(far, near, done.at[at])
        for at, (far, near) in enumerate([(nbr_far, nbr), (halo_far, halo), (rhs_far, rhs)])
    ]
    for copy in copies:
        copy.start()
    copies[0].wait()
    copies[1].wait()

    def across(face, at):
        return nbr[face, at] & 255

    column = [halo[0, 0] & 255]
    for _ in range(15):
        column.append(across(5, column[-1]))
    rows = [column]
    for _ in range(7):
        rows.append([across(3, at) for at in rows[-1]])
    layers = [rows, [[across(1, at) for at in row] for row in rows]]
    for row in range(8):
        for sheet in range(16):
            spot[rows[row][sheet]] = row * 16 + sheet

    sub = lax.broadcasted_iota(jnp.int32, (8, LANES), 0)
    lane = lax.broadcasted_iota(jnp.int32, (8, LANES), 1)
    for sheet in range(16):
        for layer in range(2):
            at = jnp.zeros((8, LANES), jnp.int32)
            for row in range(8):
                at = jnp.where(sub == row, layers[layer][row][sheet], at)
            order[sheet * 2 + layer, :, :LANES] = jnp.where(lane == at, 1.0, 0.0).astype(F32)
            order[sheet * 2 + layer, :, LANES:] = jnp.where(lane + LANES == at, 1.0, 0.0).astype(F32)

    picks = order[...].reshape(SLAB, SLAB).astype(BF16)
    copies[2].wait()
    for step in range(2):
        high, low = split(rhs[step])
        values = dot(picks, high, NT) + dot(picks, low, NT)
        placed[step] = values.reshape(32, 8, NB)


def align_kernel(place, spot, chain, placed, sent, shift):
    group = lax.shift_right_logical(place[1], 2)
    member = place[1] & 3

    def step(slab, at):
        return chain[slab, lax.shift_right_logical(at, 7), at & 127]

    near = jnp.where(group == 0, chain[3, 3, 0], chain[0, 2, 0]) & 255
    origin = near
    for hop in range(4):
        slab = jnp.where(group == 0, 3 - hop, hop)
        far_side = step(slab, near) & 255
        origin = jnp.where(slab == member, jnp.where(group == 0, far_side, near), origin)
        if hop < 3:
            label = step(slab, far_side) & 127
            ahead = jnp.where(group == 0, 2 - hop, hop + 1)
            near = chain[ahead, 2, label] & 255
    found = spot[origin] & 127
    first_row, first_sheet = lax.shift_right_logical(found, 4), found & 15
    shift[0] = (8 - first_row) & 7
    shift[1] = first_sheet
    for device in range(16):
        sheet = (SHEET_OF[device] + first_sheet) & 15
        for at in range(2):
            values = placed[at, pl.ds(sheet * 2, 2)]
            values = pltpu.roll(values, (8 - first_row) & 7, 1)
            sent[device, at * 16 : at * 16 + 16, :] = values.reshape(16, NB)


def first_weights(ref):
    return [ref.at[a:b] for a, b in [(0, 384), (384, 768), (768, 1536), (1536, 2304)]]


def second_weights(ref):
    return [ref.at[a:b] for a, b in [(0, 768), (768, 1536), (1536, 1920), (1920, 2304)]]


def face_order(place):
    core, slab = place[0] & 1, place[1] & 1
    return [1 - slab, slab, 4 + core, 5 - core, 2, 3]


def prepare_kernel(place, shift, placed_order, material, modes_in, modes_out, face_lift, rates, pick, *refs):
    order, first_set, factors_far, second_far, second_set, factors, lift, sorted_pick, done = refs
    in_h, in_l, trace_h, trace_l = first_weights(first_set)
    lift_h, lift_l, out_h, out_l = second_weights(second_set)
    same_r, same_i, cross = factors.at[0], factors.at[1], factors.at[2]
    in_parts = split(modes_in[...])
    in_h[...], in_l[...] = in_parts
    out_parts = split(modes_out[...])
    out_h[...], out_l[...] = out_parts
    for at, face in enumerate(face_order(place)):
        sorted_pick[at * LANES : (at + 1) * LANES, :] = pick[pl.ds(pl.multiple_of(face * LANES, LANES), LANES), :]
    trace_h[...] = dot(sorted_pick[...], out_parts[0], NN).astype(BF16)
    trace_l[...] = dot(sorted_pick[...], out_parts[1], NN).astype(BF16)
    for device in range(16):
        sheet = (SHEET_OF[device] + shift[1]) & 15
        picks = pltpu.roll(placed_order[pl.ds(sheet * 2, 2)], shift[0], 1)
        order[device * 16 : device * 16 + 16, :] = picks.reshape(16, SLAB).astype(BF16)
    own_picks = order[pl.ds(pl.multiple_of(place[0] * 16, 16), 16), :].astype(F32)
    own = jnp.sum(own_picks * material[...], axis=1, keepdims=True)
    for freq in range(16):
        angle = 2.0 * math.pi / STEPS * freq
        rows = slice(freq * 16, freq * 16 + 16)
        real = (1.0 - DECAY * math.cos(angle)) * own + rates[...]
        imag = jnp.broadcast_to((DECAY * math.sin(angle) if freq else 0.0) * own, (16, NB))
        size = real * real + imag * imag
        same = real / size
        same_r[rows, :] = same
        same_i[rows, :] = same if freq else 1.0 / ((1.0 + DECAY) * own + rates[...])
        cross[rows, :] = imag / size
    factors_copy = pltpu.make_async_copy(factors, factors_far, done.at[0])
    factors_copy.start()
    lift[...] = jnp.zeros_like(lift)
    for at, face in enumerate(face_order(place)):
        lift[at * LANES : at * LANES + NFT, :] = face_lift[face]
    lift_h[...], lift_l[...] = split(dot_rows(split(lift[...]), in_parts))
    copy = pltpu.make_async_copy(second_set, second_far, done.at[1])
    copy.start()
    copy.wait()
    factors_copy.wait()


def divided(modal, factors):
    real, imag = modal[:HALF], modal[HALF:]
    mixed = factors[2]
    return jnp.concatenate(
        [real * factors[0] + imag * mixed, imag * factors[1] - real * mixed]
    )


def pack(values):
    quarter = values.shape[0] // 4
    lane = lax.broadcasted_iota(jnp.int32, (quarter, LANES), 1)
    tail = values[3 * quarter :]
    parts = []
    for part in range(3):
        moved = pltpu.roll(tail, NFT - 32 * part, 1)
        parts.append(jnp.where(lane < NFT, values[part * quarter : (part + 1) * quarter], moved))
    return jnp.concatenate(parts)


def unpack(packed):
    quarter = packed.shape[0] // 3
    lane = lax.broadcasted_iota(jnp.int32, (quarter, LANES), 1)
    moved = [pltpu.roll(packed[part * quarter : (part + 1) * quarter], 32 + 32 * part, 1) for part in range(3)]
    tail = jnp.where(lane < 32, moved[0], jnp.where(lane < 64, moved[1], moved[2]))
    return jnp.concatenate([packed, tail])


def send_traces(place, solved, trace_h, trace_l, traces, solved_h, solved_l, inner, to_chip, to_next, to_even, to_odd):
    near = 1 - (place[1] & 1)
    solved_h[...], solved_l[...] = solved
    wide = 4 * LANES
    traces[...] = dot_rows(solved, (trace_h[:wide], trace_l[:wide])).reshape(STEPS, 2, 8, wide)
    to_chip[...] = pack(traces[:, :, :, 3 * LANES :].reshape(ROWS, LANES))
    to_next[...] = pack(traces[:, :, :, 2 * LANES : 3 * LANES].reshape(ROWS, LANES))
    to_even[...] = pack(traces[:, near, :, :LANES].reshape(HALF, LANES))
    to_odd[...] = pack(traces[:, 1 - near, :, LANES : 2 * LANES].reshape(HALF, LANES))
    inner[0] = traces[:, near, :, LANES : 2 * LANES].reshape(HALF, LANES)
    inner[1] = traces[:, 1 - near, :, :LANES].reshape(HALF, LANES)


def first_kernel(
    place, steps, first_set, factors_far,
    modal, solved_h, solved_l, inner, to_chip, to_next, to_even, to_odd, spectrum, traces, factors, done,
):
    factors_copy = pltpu.make_async_copy(factors_far, factors, done)
    factors_copy.start()
    in_h, in_l, trace_h, trace_l = first_weights(first_set)
    to_frequencies(steps, spectrum)
    start = dot_rows(split(spectrum[...]), (in_h[...], in_l[...]))
    modal[...] = start
    factors_copy.wait()
    solved = split(divided(start, factors))
    send_traces(
        place, solved, trace_h, trace_l, traces, solved_h, solved_l, inner, to_chip, to_next, to_even, to_odd
    )


def inside_kernel(modal, solved_h, solved_l, first_set, second_set, base):
    _, _, trace_h, trace_l = first_weights(first_set)
    lift_h, lift_l, _, _ = second_weights(second_set)
    wide = 4 * LANES
    traces = dot_rows((solved_h[...], solved_l[...]), (trace_h[wide:], trace_l[wide:]))
    traces = traces.reshape(ROWS // 8, 8, 2 * LANES)
    minus_y = pltpu.roll(traces[:, :, LANES:], 1, 1).reshape(ROWS, LANES)
    plus_y = pltpu.roll(traces[:, :, :LANES], 7, 1).reshape(ROWS, LANES)
    faces = split(jnp.concatenate([minus_y, plus_y], axis=1))
    base[...] = modal[...] - dot_columns(faces, (lift_h[wide:], lift_l[wide:]))


def meet_kernel(place, from_chip, from_next, base, inner, second_set, out, faces):
    near = 1 - (place[1] & 1)
    wide = 4 * LANES
    lift_h, lift_l, _, _ = second_weights(second_set)
    faces[:, near, :, :LANES] = jnp.zeros((STEPS, 8, LANES), F32)
    faces[:, 1 - near, :, :LANES] = inner[0].reshape(STEPS, 8, LANES)
    faces[:, near, :, LANES : 2 * LANES] = inner[1].reshape(STEPS, 8, LANES)
    faces[:, 1 - near, :, LANES : 2 * LANES] = jnp.zeros((STEPS, 8, LANES), F32)
    faces[:, :, :, 2 * LANES : 3 * LANES] = unpack(from_next[...]).reshape(STEPS, 2, 8, LANES)
    faces[:, :, :, 3 * LANES :] = unpack(from_chip[...]).reshape(STEPS, 2, 8, LANES)
    coupled = dot_columns(split(faces[...].reshape(ROWS, wide)), (lift_h[:wide], lift_l[:wide]))
    out[...] = (base[...] - coupled).reshape(STEPS, 2, 8, NB)


def corrected(place, from_even, from_odd, base, lift_h, lift_l, modes):
    near = 1 - (place[1] & 1)
    for at, (arrived, layer) in enumerate([(from_even, near), (from_odd, 1 - near)]):
        rows = slice(at * LANES, (at + 1) * LANES)
        coupled = dot_columns(split(unpack(arrived[...])), (lift_h[rows], lift_l[rows]))
        modes[:, layer] = base[:, layer] - coupled.reshape(STEPS, 8, NB)
    return modes[...].reshape(ROWS, NB)


def sweep_kernel(
    place, from_even, from_odd, base, first_set, second_set, factors,
    solved_h, solved_l, inner_out, to_chip, to_next, to_even, to_odd, modes, traces,
):
    _, _, trace_h, trace_l = first_weights(first_set)
    lift_h, lift_l, _, _ = second_weights(second_set)
    solved = split(divided(corrected(place, from_even, from_odd, base, lift_h, lift_l, modes), factors))
    send_traces(
        place, solved, trace_h, trace_l, traces, solved_h, solved_l, inner_out, to_chip, to_next, to_even, to_odd
    )


def last_kernel(place, from_even, from_odd, base, second_set, factors, steps, modes, spectrum):
    lift_h, lift_l, out_h, out_l = second_weights(second_set)
    solved = split(divided(corrected(place, from_even, from_odd, base, lift_h, lift_l, modes), factors))
    spectrum[...] = dot_rows(solved, (out_h[...], out_l[...]))
    to_steps(spectrum, steps)


def restore_kernel(arrived, order, far, out, done):
    copies = [pltpu.make_async_copy(out.at[step], far.at[step], done.at[step]) for step in range(2)]
    for step in range(2):
        values = arrived[:, step * 16 : step * 16 + 16, :].reshape(SLAB, NB)
        high, low = split(values)
        picks = order[...]
        out[step] = dot(high, picks, TN) + dot(low, picks, TN)
        copies[step].start()
    for copy in copies:
        copy.wait()


SMEM = pl.BlockSpec(memory_space=pltpu.SMEM)
VMEM = pl.BlockSpec(memory_space=pltpu.VMEM)
HBM = pl.BlockSpec(memory_space=pltpu.HBM)
KEPT = pl.BlockSpec(memory_space=pltpu.VMEM)
DMA = pltpu.SemaphoreType.DMA
HELD = ((HBM, pltpu.HBM), (KEPT, pltpu.VMEM))


def call(body, ins, outs, flops, scratch=(), megabytes=8):
    shapes = [jax.ShapeDtypeStruct(shape, kind) for shape, kind, _ in outs]
    moved = sum(a.size * a.dtype.itemsize for a in shapes + [a for a, _ in ins])
    for held, space in HELD:
        ins = [(pltpu.with_memory_space_constraint(a, space) if spec is held else a, spec) for a, spec in ins]
        shapes = [space(shape, kind) if spec is held else old for old, (shape, kind, spec) in zip(shapes, outs)]
    return pl.pallas_call(
        body,
        out_shape=shapes,
        in_specs=[spec for _, spec in ins],
        out_specs=[spec for _, _, spec in outs],
        scratch_shapes=list(scratch),
        compiler_params=pltpu.CompilerParams(vmem_limit_bytes=megabytes * 2**20),
        cost_estimate=pl.CostEstimate(flops=flops, bytes_accessed=moved, transcendentals=0),
    )(*[a for a, _ in ins])


def shards(rhs, material, modal_rates, modes_in, modes_out, face_lift, neighbours, halo_send):
    place = (jnp.stack([lax.axis_index("tm"), lax.axis_index("space")]).astype(jnp.int32), SMEM)
    (table,) = call(
        table_kernel,
        [place, (neighbours, HBM), (halo_send, HBM)],
        [((4, 4, LANES), jnp.int32, KEPT)],
        10**4,
        [pltpu.VMEM(neighbours.shape, jnp.int32), pltpu.VMEM(halo_send.shape, jnp.int32), DMA((2,))],
    )
    chain = lax.all_to_all(
        table, "space", 0, 0, tiled=True, axis_index_groups=[[0, 1, 2, 3], [4, 5, 6, 7]]
    )
    placed, placed_order, spot = call(
        order_kernel,
        [(neighbours, HBM), (halo_send, HBM), (rhs, HBM)],
        [((2, 32, 8, NB), F32, KEPT), ((32, 8, SLAB), F32, KEPT), ((SLAB,), jnp.int32, SMEM)],
        2 * 4 * 256 * 256 * 384,
        [
            pltpu.SMEM(neighbours.shape, jnp.int32),
            pltpu.SMEM(halo_send.shape, jnp.int32),
            pltpu.VMEM(rhs.shape, F32),
            DMA((3,)),
        ],
    )
    sent, shift = call(
        align_kernel,
        [place, (spot, SMEM), (chain, SMEM), (placed, KEPT)],
        [((16, 32, NB), F32, KEPT), ((2,), jnp.int32, SMEM)],
        10**6,
    )
    arrived = lax.all_to_all(sent, "tm", 0, 0, tiled=True).reshape(ROWS, NB)
    weights = [modes_in, modes_out, jnp.swapaxes(face_lift, 1, 2), modal_rates.reshape(1, NB), trace_rows()]
    prepared = [((SLAB, SLAB), BF16, KEPT), ((2304, NB), BF16, KEPT), ((3, HALF, NB), F32, HBM), ((2304, NB), BF16, HBM)]
    order, first_set, factors, second_set = call(
        prepare_kernel,
        [place, (shift, SMEM), (placed_order, KEPT), (material.reshape(1, SLAB), VMEM)]
        + [(jnp.asarray(weight), VMEM) for weight in weights],
        prepared,
        2 * 5 * 384 * 384 * 768,
        [pltpu.VMEM((2304, NB), BF16), pltpu.VMEM((3, HALF, NB), F32), pltpu.VMEM((6 * LANES, NB), F32), pltpu.VMEM((6 * LANES, NB), BF16), DMA((2,))],
    )

    faces = (
        [((ROWS, NB), BF16, KEPT)] * 2
        + [((2, HALF, LANES), F32, KEPT)]
        + [((ROWS * 3 // 4, LANES), F32, VMEM)] * 2
        + [((HALF * 3 // 4, LANES), F32, VMEM)] * 2
    )
    face_scratch = pltpu.VMEM((STEPS, 2, 8, 4 * LANES), F32)

    def exchange(to_chip, to_next, to_even, to_odd):
        from_odd = lax.ppermute(to_odd, "space", ODD_SIDES)
        from_even = lax.ppermute(to_even, "space", EVEN_SIDES)
        from_next = lax.ppermute(to_next, "tm", NEXT_CHIP)
        from_chip = lax.ppermute(to_chip, "tm", SAME_CHIP)
        return from_chip, from_next, from_even, from_odd

    def inside(solved_h, solved_l, inner, from_chip, from_next):
        (base,) = call(
            inside_kernel,
            [(a, KEPT) for a in (modal, solved_h, solved_l, first_set)] + [(second_set, VMEM)],
            [((ROWS, NB), F32, KEPT)],
            2 * 3 * 512 * 384 * 512,
        )
        (base,) = call(
            meet_kernel,
            [place]
            + [(a, VMEM) for a in (from_chip, from_next)]
            + [(base, KEPT), (inner, KEPT), (second_set, VMEM)],
            [((STEPS, 2, 8, NB), F32, KEPT)],
            2 * 3 * 512 * 384 * 512,
            [face_scratch],
        )
        return (base, KEPT)

    modal, solved_h, solved_l, inner, *outgoing = call(
        first_kernel,
        [place, (arrived, VMEM), (first_set, KEPT), (factors, HBM)],
        [((ROWS, NB), F32, KEPT)] + faces,
        2 * 3 * 512 * 384 * (384 + 512),
        [pltpu.VMEM((ROWS, NB), F32), face_scratch, pltpu.VMEM((3, HALF, NB), F32), DMA],
    )
    *incoming, from_even, from_odd = exchange(*outgoing)
    base = inside(solved_h, solved_l, inner, *incoming)
    solved_h, solved_l, inner, *outgoing = call(
        sweep_kernel,
        [place, (from_even, VMEM), (from_odd, VMEM), base, (first_set, KEPT), (second_set, VMEM), (factors, VMEM)],
        faces,
        2 * 3 * 512 * 384 * 512,
        [pltpu.VMEM((STEPS, 2, 8, NB), F32), face_scratch],
    )
    *incoming, from_even, from_odd = exchange(*outgoing)
    base = inside(solved_h, solved_l, inner, *incoming)
    (steps,) = call(
        last_kernel,
        [place, (from_even, VMEM), (from_odd, VMEM), base, (second_set, VMEM), (factors, VMEM)],
        [((ROWS, NB), F32, VMEM)],
        2 * 3 * 512 * 384 * 384,
        [pltpu.VMEM((STEPS, 2, 8, NB), F32), pltpu.VMEM((ROWS, NB), F32)],
    )
    back = lax.all_to_all(steps.reshape(16, 32, NB), "tm", 0, 0, tiled=True)
    (out,) = call(
        restore_kernel,
        [(back, VMEM), (order, KEPT)],
        [((2, NB, SLAB), F32, HBM)],
        2 * 4 * 256 * 256 * 384,
        [pltpu.VMEM((2, NB, SLAB), F32), DMA((2,))],
    )
    return out


def solution(mesh):
    return jax.shard_map(
        shards,
        mesh=mesh,
        in_specs=(
            P("tm", None, "space"),
            P("space"),
            P(),
            P(),
            P(),
            P(),
            P(None, "space"),
            P(None, "space"),
        ),
        out_specs=P("tm", None, "space"),
        check_vma=False,
    )
```
